32 devices in a mesh: dp: 16 (over z, x, core), blk: 2 (over y).
Axes of the slice: x: 2, y: 2, z: 4, core: 2. Of those that a mesh axis runs over, the one named last changes fastest.
Arguments:
- tokens: bfloat16 [4, 16, 1024, 768], P(None, 'dp', 'blk'), may hold values from -6 to 6
- lengths: int32 [4, 16], P(None, 'dp'), may hold values from 50 to 1024, as said below
- norm1_gain: bfloat16 [768], P(('dp', 'blk')), may hold values from 0.25 to 1.75
- w_query: bfloat16 [768, 768], P(('dp', 'blk')), may hold values from -0.21875 to 0.21875
- w_key: bfloat16 [768, 768], P(('dp', 'blk')), may hold values from -0.21875 to 0.21875
- w_value: bfloat16 [768, 768], P(('dp', 'blk')), may hold values from -0.21875 to 0.21875
- w_out: bfloat16 [768, 768], P(('dp', 'blk')), may hold values from -2.5 to 2.5
- rel_table: float32 [32, 12], replicated, may hold values from -3 to 3
- norm2_gain: bfloat16 [768], P(('dp', 'blk')), may hold values from 0.25 to 1.75
- w_in: bfloat16 [768, 3072], P(('dp', 'blk')), may hold values from -0.21875 to 0.21875
- w_down: bfloat16 [768, 3072], P(('dp', 'blk')), may hold values from -0.109375 to 0.109375
- cotangent: bfloat16 [4, 16, 1024, 768], P(None, 'dp', 'blk'), may hold values from -6 to 6
Outputs:
- mixed: bfloat16 [4, 16, 1024, 768], P(None, 'dp', 'blk')
- grad_tokens: bfloat16 [4, 16, 1024, 768], P(None, 'dp', 'blk')
- grad_norm1: float32 [768], P(('dp', 'blk'))
- grad_query: float32 [768, 768], P(('dp', 'blk'))
- grad_key: float32 [768, 768], P(('dp', 'blk'))
- grad_value: float32 [768, 768], P(('dp', 'blk'))
- grad_out: float32 [768, 768], P(('dp', 'blk'))
- grad_table: float32 [32, 12], replicated
- grad_norm2: float32 [768], P(('dp', 'blk'))
- grad_in: float32 [768, 3072], P(('dp', 'blk'))
- grad_down: float32 [768, 3072], P(('dp', 'blk'))
The draws below stay inside these ranges and needn't reach their ends.
Inputs may be any that keep to these rules, and one draw needn't show every extreme that they name: `lengths`: in each index of dp, at least one of its 4 documents has length 1024; which one is drawn.
All inputs are finite; a program needn't handle non-finite values.
Results may differ from the reference program's by a relative error of at most 0.035.
Values may be sent and summed in bfloat16 or wider, within the bound.
A program may use at most 448 MiB of HBM per device.

```python
import jax
import jax.numpy as jnp
from jax import lax

D = 768
H = 12
HD = 64
FF = 3072
BUCKETS = 32
SEQ = 1024
LEN_MIN = 50
MB = 4
DOCS = 1
DOCS_ALL = 16


def draw_lengths(key, part):
    key = jax.random.fold_in(key, 11)
    base_key, pick_key = jax.random.split(key)
    group_count = DOCS_ALL // DOCS
    drawn = jax.random.randint(base_key, (MB, group_count, DOCS), LEN_MIN, SEQ + 1)
    chosen = jax.random.randint(pick_key, (group_count,), 0, MB * DOCS)
    slot_ids = jnp.arange(MB)[:, None, None] * DOCS + jnp.arange(DOCS)[None, None, :]
    longest = slot_ids == chosen[None, :, None]
    return jnp.where(longest, SEQ, drawn).reshape(MB, DOCS_ALL).astype(jnp.int32)


def raised(array, stream_key, source, target, blocks, factor):
    def block_of(dim):
        return (jnp.arange(array.shape[dim]) // (array.shape[dim] // blocks)).reshape((-1,) + (1,) * (array.ndim - 1 - dim))

    one_side = jax.random.permutation(stream_key, blocks)[block_of(target)]
    other_side = (block_of(target) + blocks // 2) % blocks
    return jnp.where((block_of(source) == one_side) | (block_of(source) == other_side), factor * array, array)


def block_scale(stream_key, dims, pieces, least, top_value):
    def one(axis_at, parts):
        steps = jax.random.uniform(jax.random.fold_in(jax.random.fold_in(stream_key, 6), axis_at), (parts,), jnp.float32, least / len(pieces), top_value / len(pieces))
        return jnp.repeat(jnp.exp(steps), dims[axis_at] // parts).reshape((-1,) + (1,) * (len(dims) - axis_at - 1))

    level = one(*pieces[0])
    for cut in pieces[1:]:
        level = level * one(*cut)
    return level


def centred(rng, shape, width, bound, shards=(), held_as=jnp.bfloat16):
    entries = width * jax.random.normal(rng, shape, jnp.float32)
    if shards:
        entries = entries * block_scale(rng, shape, shards, -0.22, 0.18)
    return jnp.clip(entries, -bound, bound).astype(held_as)


def noise_with(rng, shape, scale, bound, cuts, heavy, kind=jnp.bfloat16):
    array = scale * jax.random.normal(rng, shape, jnp.float32)
    if cuts:
        array = array * block_scale(rng, shape, cuts, -0.22, 0.18)
    return jnp.clip(raised(array, jax.random.fold_in(rng, 3), *heavy), -bound, bound).astype(kind)


def setup_inputs(seed: int = 0) -> dict:
    keys = jax.random.split(jax.random.key(seed), 13)
    tokens = centred(keys[0], (MB, DOCS_ALL, SEQ, D), 1.0, 6.0, ((1, 16), (2, 2)))
    lengths = draw_lengths(jax.random.fold_in(keys[12], 71), 0)
    norm1_gain = jnp.clip(1.0 + 0.15 * jax.random.normal(keys[2], (D,), jnp.float32), 0.25, 1.75).astype(jnp.bfloat16)
    w_query = centred(keys[3], (D, D), D ** -0.5, 0.21875, ((0, 32),))
    w_key = centred(keys[4], (D, D), D ** -0.5, 0.21875, ((0, 32),))
    w_value = centred(keys[5], (D, D), D ** -0.5, 0.21875, ((0, 32),))
    w_out = centred(keys[6], (D, D), (D // 128) ** -0.5, 2.5, ((0, 32),))
    rel_table = centred(keys[7], (BUCKETS, H), 0.5, 3.0, (), jnp.float32)
    norm2_gain = jnp.clip(1.0 + 0.15 * jax.random.normal(keys[8], (D,), jnp.float32), 0.25, 1.75).astype(jnp.bfloat16)
    w_in = centred(keys[9], (D, FF), D ** -0.5, 0.21875, ((0, 32),))
    w_down = centred(keys[10], (D, FF), FF ** -0.5, 0.109375, ((0, 32),))
    cotangent = noise_with(keys[11], (MB, DOCS_ALL, SEQ, D), 1.0, 6.0, ((1, 16), (2, 2)), (1, 3, 16, 2.0))
    return {"tokens": tokens, "lengths": lengths, "norm1_gain": norm1_gain, "w_query": w_query, "w_key": w_key, "w_value": w_value, "w_out": w_out, "rel_table": rel_table, "norm2_gain": norm2_gain, "w_in": w_in, "w_down": w_down, "cotangent": cotangent}


@jax.custom_vjp
def low(v):
    return lax.optimization_barrier(v.astype(jnp.bfloat16)).astype(jnp.float32)

@jax.custom_vjp
def low_back(v):
    return v

def low_keep(v):
    return (low(v), None)

def low_pass(kept, grad):
    return (grad,)

def back_keep(v):
    return (v, None)

def back_low(kept, grad):
    return (low(grad),)
low.defvjp(low_keep, low_pass)
low_back.defvjp(back_keep, back_low)
EPS = 1e-06
NEG = -1e+30
HIGH = lax.Precision.HIGHEST
LIMITS = (12, 16, 23, 32, 46, 64, 91)

def bucket_of(relative):
    distance = jnp.abs(relative)
    far_bucket = 8 + sum(((distance >= border).astype(jnp.int32) for border in LIMITS))
    bucket = jnp.where(distance < 8, distance, far_bucket)
    return (bucket + 16 * (relative > 0).astype(jnp.int32)).astype(jnp.int32)

def rms_norm(vector, gain_row):
    return vector * lax.rsqrt(lax.optimization_barrier(jnp.mean(vector * vector, -1, keepdims=True)) + EPS) * gain_row

def matmul(left_side, weight):
    return jnp.einsum('gsd,de->gse', left_side, weight, precision=HIGH)

def encoder_layer(inputs, key_valid, buckets, params):
    gain_first, query_w, key_w, value_w, out_w, bias_table, gain_second, in_w, down_w = params
    doc_count = inputs.shape[0]
    normed_low = low(rms_norm(inputs, gain_first))
    query_heads = low(low_back(matmul(normed_low, query_w))).reshape(doc_count, SEQ, H, HD)
    key_heads = low(low_back(matmul(normed_low, key_w))).reshape(doc_count, SEQ, H, HD)
    value_heads = low(low_back(matmul(normed_low, value_w))).reshape(doc_count, SEQ, H, HD)
    raw_score = low_back(jnp.einsum('gqhd,gkhd->ghqk', query_heads, key_heads, precision=HIGH))
    pos_bias = jnp.transpose(bias_table[buckets], (2, 0, 1))
    scores = jnp.where(key_valid[:, None, None, :], raw_score * HD ** (-0.5) + pos_bias[None], NEG)
    row_max = lax.optimization_barrier(jnp.max(scores, -1, keepdims=True))
    exp_score = jnp.exp(scores - row_max)
    probability = exp_score / lax.optimization_barrier(jnp.sum(exp_score, -1, keepdims=True))
    attended = jnp.einsum('ghqk,gkhd->gqhd', low(probability), value_heads, precision=HIGH).reshape(doc_count, SEQ, D)
    residual_mid = inputs + low_back(matmul(low(low_back(attended)), out_w))
    mid_low = low(rms_norm(residual_mid, gain_second))
    up_proj = low_back(matmul(mid_low, in_w))
    activated = low(jax.nn.gelu(up_proj))
    return residual_mid + jnp.einsum('gsf,df->gsd', activated, down_w, precision=HIGH)

def reference(tokens, lengths, norm1_gain, w_query, w_key, w_value, w_out, rel_table, norm2_gain, w_in, w_down, cotangent):
    weights = tuple((w.astype(jnp.float32) for w in (norm1_gain, w_query, w_key, w_value, w_out, rel_table, norm2_gain, w_in, w_down)))
    doc_total = MB * DOCS_ALL
    group_size = 2
    steps_count = doc_total // group_size
    inputs = tokens.reshape(steps_count, group_size, SEQ, D).astype(jnp.float32)
    cot_all = cotangent.reshape(steps_count, group_size, SEQ, D).astype(jnp.float32)
    length_all = lengths.reshape(steps_count, group_size).astype(jnp.int32)
    positions = jnp.arange(SEQ, dtype=jnp.int32)
    buckets = bucket_of(positions[None, :] - positions[:, None])

    def scan_step(running, item):
        doc_rows, cot_rows, doc_length = item
        key_valid = positions[None, :] < doc_length[:, None]

        def forward(layer_in, params):
            return encoder_layer(layer_in, key_valid, buckets, params)
        mixed_rows, pullback = jax.vjp(forward, doc_rows, weights)
        grad_rows, grad_weights = pullback(cot_rows * key_valid[:, :, None].astype(jnp.float32))
        running = jax.tree.map(jnp.add, running, grad_weights)
        return (running, (mixed_rows.astype(jnp.bfloat16), grad_rows.astype(jnp.bfloat16)))
    zero_grads = jax.tree.map(jnp.zeros_like, weights)
    totals, (mixed_all, grad_all) = lax.scan(scan_step, zero_grads, (inputs, cot_all, length_all))
    mixed = mixed_all.reshape(MB, DOCS_ALL, SEQ, D)
    grad_tokens = grad_all.reshape(MB, DOCS_ALL, SEQ, D)
    return (mixed, grad_tokens, totals[0], totals[1], totals[2], totals[3], totals[4], totals[5], totals[6], totals[7], totals[8])
```

```python
import functools

import jax
import jax.numpy as jnp
from jax import lax
from jax.experimental import pallas as pl
from jax.experimental.pallas import tpu as pltpu
from jax.sharding import PartitionSpec as P

EPS = 1e-06
NEG = -1e30
LIMITS = (12, 16, 23, 32, 46, 64, 91)
SUB = 128
LOG2E = 1.4426950408889634
GELU_A = 0.7978845608028654
GELU_B = 0.044715
VMEM = 62 * 2**20
NN = (((1,), (0,)), ((), ()))
NT = (((1,), (1,)), ((), ()))
TN = (((0,), (0,)), ((), ()))
low_type = jnp.bfloat16
f32 = jnp.float32


def dot(left, right, dims=NN):
    return lax.dot_general(left, right, dims, preferred_element_type=f32)


def bucket_of(relative):
    distance = jnp.abs(relative)
    far_bucket = 8 + sum(((distance >= border).astype(jnp.int32) for border in LIMITS))
    bucket = jnp.where(distance < 8, distance, far_bucket)
    return bucket + 16 * (relative > 0).astype(jnp.int32)


def norm_rows(rows):
    inverse = lax.rsqrt(jnp.mean(rows * rows, -1, keepdims=True) + EPS)
    return rows * inverse, inverse


def whole(shape):
    return pl.BlockSpec(shape, lambda *_: (0,) * len(shape), pipeline_mode=pl.Buffered(1))


def params():
    return pltpu.CompilerParams(vmem_limit_bytes=VMEM)


def struct(shape, dtype=low_type):
    return jax.ShapeDtypeStruct(shape, dtype)


SMEM = pl.BlockSpec(memory_space=pltpu.SMEM)


def qkv_kernel(x_ref, gain_ref, w_ref, q_ref, k_ref, v_ref):
    width = q_ref.shape[1]
    normed, _ = norm_rows(x_ref[...].astype(f32))
    low = (normed * gain_ref[...]).astype(low_type)
    q_ref[...] = (dot(low, w_ref[:, :width]) * (0.125 * LOG2E)).astype(low_type)
    k_ref[...] = dot(low, w_ref[:, width : 2 * width]).astype(low_type)
    v_ref[...] = dot(low, w_ref[:, 2 * width : 3 * width]).astype(low_type)


def qkv_call(x, gain, w_first, heads_width, rows=512):
    total, width = x.shape
    row = pl.BlockSpec((rows, width), lambda i: (i, 0))
    return pl.pallas_call(
        qkv_kernel,
        grid=(total // rows,),
        in_specs=[row, whole((1, width)), whole(w_first.shape)],
        out_specs=[pl.BlockSpec((rows, heads_width), lambda i: (i, 0))] * 3,
        out_shape=[struct((total, heads_width))] * 3,
        compiler_params=params(),
        name="qkv",
    )(x, gain, w_first)


def attend_kernel(
    len_ref, far_ref, q_ref, k_ref, v_ref, near_ref, o_ref, lse_ref, *, rows
):
    pair, doc = pl.program_id(0), pl.program_id(1)
    seq = q_ref.shape[0]
    subs = seq // SUB
    first = lax.broadcasted_iota(jnp.int32, (1, 128), 1) < 64
    live = lax.broadcasted_iota(jnp.int32, (1, seq), 1) < len_ref[doc]
    one = jnp.ones((), low_type)
    k, v = k_ref[...], v_ref[...]
    v_ones = (jnp.where(first, v, one), jnp.where(first, one, v))
    for block in range(seq // rows):
        span = slice(block * rows, (block + 1) * rows)
        q = q_ref[span, :]
        outs, tops = [], []
        for h in range(2):
            q_one = jnp.where(first == (h == 0), q, jnp.zeros((), low_type))
            raw = dot(q_one, k, NT)
            strips = []
            for a in range(rows // SUB):
                at = block * (rows // SUB) + a
                strip = raw[a * SUB : (a + 1) * SUB]
                low, high = max(at - 1, 0), min(at + 2, subs)
                parts = []
                if low > 0:
                    parts.append(strip[:, : low * SUB] + far_ref[2 * pair + h, 0])
                for b in range(low, high):
                    parts.append(strip[:, b * SUB : (b + 1) * SUB] + near_ref[h, b - at + 1])
                if high < subs:
                    parts.append(strip[:, high * SUB :] + far_ref[2 * pair + h, 1])
                strips.append(jnp.concatenate(parts, 1))
            scores = jnp.where(live, jnp.concatenate(strips, 0), NEG)
            top = jnp.max(scores, 1, keepdims=True)
            outs.append(dot(jnp.exp2(scores - top).astype(low_type), v_ones[h]))
            tops.append(top)
        total = jnp.where(first, pltpu.roll(outs[0], 64, 1), pltpu.roll(outs[1], 64, 1))
        o_ref[span, :] = (jnp.where(first, outs[0], outs[1]) / total).astype(low_type)
        log_total = (jnp.where(first, tops[0], tops[1]) + jnp.log2(total)).T
        lse_ref[0, 0, 0:1, span] = log_total[0:1]
        lse_ref[0, 0, 1:2, span] = log_total[64:65]


def attend_call(lengths, far, q, k, v, near, rows=512):
    docs, (total, width) = lengths.shape[0], q.shape
    seq, pairs = total // docs, width // 128
    slab = pl.BlockSpec((seq, 128), lambda p, d: (d, p))
    return pl.pallas_call(
        functools.partial(attend_kernel, rows=rows),
        grid=(pairs, docs),
        in_specs=[
            SMEM,
            SMEM,
            slab,
            slab,
            slab,
            pl.BlockSpec((2, 3, SUB, SUB), lambda p, d: (p, 0, 0, 0)),
        ],
        out_specs=[slab, pl.BlockSpec((1, 1, 2, seq), lambda p, d: (d, p, 0, 0))],
        out_shape=[struct((total, width)), struct((docs, pairs, 2, seq), f32)],
        compiler_params=params(),
        name="attend",
    )(lengths, far, q, k, v, near)


def middle_kernel(
    len_ref,
    x_ref,
    heads_ref,
    cot_ref,
    gain_ref,
    w_ref,
    mixed_ref,
    hgrad_ref,
    mid_ref,
    gw_ref,
    gn_ref,
    acc,
    acc_gain,
    *,
    seq,
    chunk,
):
    step = pl.program_id(0)
    rows, width = x_ref.shape
    hidden = (w_ref.shape[1] - width) // 2

    @pl.when(step == 0)
    def _():
        acc[...] = jnp.zeros_like(acc)
        acc_gain[...] = jnp.zeros_like(acc_gain)

    per = seq // rows
    place = (step % per) * rows + lax.broadcasted_iota(jnp.int32, (rows, 1), 0)
    heads, gain = heads_ref[...], gain_ref[...]
    residual = x_ref[...].astype(f32) + dot(heads, w_ref[:, :width])
    normed, inverse = norm_rows(residual)
    low = (normed * gain).astype(low_type)
    out_grad = jnp.where(place < len_ref[step // per], cot_ref[...], jnp.zeros((), low_type))
    mixed, normed_grad = residual, jnp.zeros((rows, width), f32)
    for at in range(0, hidden, chunk):
        up = slice(width + at, width + at + chunk)
        down = slice(width + hidden + at, width + hidden + at + chunk)
        u = dot(low, w_ref[:, up])
        square = u * u
        bend = jnp.tanh(u * (GELU_A + GELU_A * GELU_B * square))
        half = 0.5 + 0.5 * bend
        act = (u * half).astype(low_type)
        slope = half + (0.5 * u) * (1 - bend * bend) * (GELU_A + 3 * GELU_A * GELU_B * square)
        up_grad = (dot(out_grad, w_ref[:, down]) * slope).astype(low_type)
        mixed = mixed + dot(act, w_ref[:, down], NT)
        normed_grad = normed_grad + dot(up_grad, w_ref[:, up], NT)
        acc[:, down] += dot(out_grad, act, TN)
        acc[:, up] += dot(low, up_grad, TN)
    mixed_ref[...] = mixed.astype(low_type)
    scaled = normed_grad * gain
    inner = jnp.mean(scaled * normed, -1, keepdims=True)
    mid = (out_grad.astype(f32) + inverse * (scaled - normed * inner)).astype(low_type)
    acc_gain[...] += jnp.sum((normed_grad * normed).reshape(rows // 8, 8, width), 0)
    mid_ref[...] = mid
    acc[:, :width] += dot(heads, mid, TN)
    hgrad_ref[...] = dot(mid, w_ref[:, :width], NT).astype(low_type)

    @pl.when(step == pl.num_programs(0) - 1)
    def _():
        gw_ref[...] = acc[...].astype(low_type)
        gn_ref[...] = jnp.sum(acc_gain[...], 0, keepdims=True)


def middle_call(lengths, x, heads, cot, gain, w_second, rows=256, chunk=1024):
    total, width = x.shape
    row = pl.BlockSpec((rows, width), lambda i: (i, 0))
    return pl.pallas_call(
        functools.partial(middle_kernel, seq=total // lengths.shape[0], chunk=chunk),
        grid=(total // rows,),
        in_specs=[SMEM, row, row, row, whole((1, width)), whole(w_second.shape)],
        out_specs=[row, row, row, whole(w_second.shape), whole((1, width))],
        out_shape=[struct((total, width))] * 3 + [struct(w_second.shape), struct((1, width), f32)],
        scratch_shapes=[pltpu.VMEM(w_second.shape, f32), pltpu.VMEM((8, width), f32)],
        compiler_params=params(),
        name="middle",
    )(lengths, x, heads, cot, gain, w_second)


def attend_back_kernel(
    len_ref,
    far_ref,
    q_ref,
    k_ref,
    v_ref,
    grad_ref,
    o_ref,
    lse_ref,
    near_ref,
    dq_ref,
    dk_ref,
    dv_ref,
    near_sum,
    far_sum,
    acc,
    *,
    keys,
    queries,
):
    pair, doc = pl.program_id(0), pl.program_id(1)
    seq = q_ref.shape[0]
    first = lax.broadcasted_iota(jnp.int32, (1, 128), 1) < 64
    zero = jnp.zeros((), low_type)

    def halves(x):
        return jnp.where(first, x, zero), jnp.where(first, zero, x)

    grad = grad_ref[...]
    q_one, g_one = halves(q_ref[...]), halves(grad)
    product = grad.astype(f32) * o_ref[...].astype(f32)
    upper = product.astype(low_type)
    lower = (product - upper.astype(f32)).astype(low_type)
    row = lax.broadcasted_iota(jnp.int32, (16, 128), 0)
    column = lax.broadcasted_iota(jnp.int32, (16, 128), 1)
    member = (row == column // 64).astype(f32).astype(low_type)
    delta = dot(member, upper, NT) + dot(member, lower, NT)

    @pl.when(doc == 0)
    def _():
        near_sum[...] = jnp.zeros_like(near_sum)
        far_sum[...] = jnp.zeros_like(far_sum)

    acc[...] = jnp.zeros_like(acc)
    for kb in range(seq // keys):
        held = slice(kb * keys, (kb + 1) * keys)
        k, v = k_ref[held, :], v_ref[held, :]
        k_one = halves(k)
        live = (kb * keys + lax.broadcasted_iota(jnp.int32, (keys, 1), 0)) < len_ref[doc]
        dk = jnp.zeros((keys, 128), f32)
        dv = jnp.zeros((keys, 128), f32)
        for qb in range(seq // queries):
            span = slice(qb * queries, (qb + 1) * queries)
            dq = None
            for h in range(2):
                scores = dot(k, q_one[h][span], NT)
                prob_grad = dot(v, g_one[h][span], NT)
                lse = lse_ref[0, 0, h : h + 1, span]
                lse_side = (lse - far_ref[2 * pair + h, 0], lse - far_ref[2 * pair + h, 1])
                row_delta = delta[h : h + 1, span]
                prob_rows, grad_rows = [], []
                for a in range(keys // SUB):
                    down = slice(a * SUB, (a + 1) * SUB)
                    probs, grads = [], []
                    for b in range(queries // SUB):
                        across = slice(b * SUB, (b + 1) * SUB)
                        apart = kb * (keys // SUB) + a - qb * (queries // SUB) - b
                        tile = scores[down, across]
                        if abs(apart) <= 1:
                            tile = tile + near_ref[h, apart + 1] - lse[:, across]
                        else:
                            tile = tile - lse_side[int(apart > 0)][:, across]
                        prob = jnp.where(live[down], jnp.exp2(tile), 0.0)
                        score_grad = prob * (prob_grad[down, across] - row_delta[:, across])
                        if abs(apart) <= 1:
                            near_sum[h, apart + 1] += score_grad
                        else:
                            far_sum[h, int(apart > 0)] += jnp.sum(
                                score_grad.reshape(SUB // 8, 8, SUB), 0
                            )
                        probs.append(prob.astype(low_type))
                        grads.append(score_grad.astype(low_type))
                    prob_rows.append(jnp.concatenate(probs, 1))
                    grad_rows.append(jnp.concatenate(grads, 1))
                prob_low = jnp.concatenate(prob_rows, 0)
                grad_low = jnp.concatenate(grad_rows, 0)
                dv = dv + dot(prob_low, g_one[h][span])
                dk = dk + dot(grad_low, q_one[h][span])
                part = dot(grad_low, k_one[h], TN)
                dq = part if dq is None else dq + part
            acc[span, :] += dq
        dv_ref[held, :] = dv.astype(low_type)
        dk_ref[held, :] = (dk * (1 / LOG2E)).astype(low_type)
    dq_ref[...] = (acc[...] * 0.125).astype(low_type)


def attend_back_call(lengths, far, q, k, v, grad, o, lse, near, keys=256, queries=1024):
    docs, (total, width) = lengths.shape[0], q.shape
    seq, pairs = total // docs, width // 128
    queries = min(queries, seq)
    slab = pl.BlockSpec((seq, 128), lambda p, d: (d, p))
    tiles = pl.BlockSpec((2, 3, SUB, SUB), lambda p, d: (p, 0, 0, 0))
    return pl.pallas_call(
        functools.partial(attend_back_kernel, keys=keys, queries=queries),
        grid=(pairs, docs),
        in_specs=[
            SMEM,
            SMEM,
            slab,
            slab,
            slab,
            slab,
            slab,
            pl.BlockSpec((1, 1, 2, seq), lambda p, d: (d, p, 0, 0)),
            tiles,
        ],
        out_specs=[
            slab,
            slab,
            slab,
            tiles,
            pl.BlockSpec((2, 2, 8, SUB), lambda p, d: (p, 0, 0, 0)),
        ],
        out_shape=[struct((total, width))] * 3
        + [struct((2 * pairs, 3, SUB, SUB), f32), struct((2 * pairs, 2, 8, SUB), f32)],
        scratch_shapes=[pltpu.VMEM((seq, 128), f32)],
        compiler_params=params(),
        name="attend_back",
    )(lengths, far, q, k, v, grad, o, lse, near)


def last_kernel(
    x_ref,
    dq_ref,
    dk_ref,
    dv_ref,
    mid_ref,
    gain_ref,
    w_ref,
    gn_second_ref,
    gt_ref,
    gw_ref,
    acc,
    acc_gain,
):
    step = pl.program_id(0)
    rows, width = x_ref.shape

    @pl.when(step == 0)
    def _():
        acc[...] = jnp.zeros_like(acc)
        acc_gain[...] = jnp.zeros_like(acc_gain)

    gain = gain_ref[...]
    normed, inverse = norm_rows(x_ref[...].astype(f32))
    low = (normed * gain).astype(low_type)
    normed_grad = None
    for index, ref in enumerate((dq_ref, dk_ref, dv_ref)):
        part = slice(index * width, (index + 1) * width)
        grad = ref[...]
        acc[:, part] += dot(low, grad, TN)
        back = dot(grad, w_ref[:, part], NT)
        normed_grad = back if normed_grad is None else normed_grad + back
    acc_gain[...] += jnp.sum((normed_grad * normed).reshape(rows // 8, 8, width), 0)
    scaled = normed_grad * gain
    inner = jnp.mean(scaled * normed, -1, keepdims=True)
    gt_ref[...] = (mid_ref[...].astype(f32) + inverse * (scaled - normed * inner)).astype(low_type)

    @pl.when(step == pl.num_programs(0) - 1)
    def _():
        gw_ref[:, : 3 * width] = acc[...].astype(low_type)
        pick = lax.broadcasted_iota(jnp.int32, (128, 1), 0)
        gains = jnp.where(
            pick == 0,
            jnp.sum(acc_gain[...], 0, keepdims=True),
            jnp.where(pick == 1, gn_second_ref[...], 0.0),
        )
        gw_ref[:, 3 * width :] = gains.T.astype(low_type)


def last_call(x, dq, dk, dv, mid, gain, w_first, gn_second, rows=512):
    total, width = x.shape
    row = pl.BlockSpec((rows, width), lambda i: (i, 0))
    return pl.pallas_call(
        last_kernel,
        grid=(total // rows,),
        in_specs=[row] * 5 + [whole((1, width)), whole(w_first.shape), whole((1, width))],
        out_specs=[row, whole(w_first.shape)],
        out_shape=[struct((total, width)), struct(w_first.shape)],
        scratch_shapes=[pltpu.VMEM((width, 3 * width), f32), pltpu.VMEM((8, width), f32)],
        compiler_params=params(),
        name="last",
    )(x, dq, dk, dv, mid, gain, w_first, gn_second)


def sharing(count):
    ways = lax.axis_size("blk")
    return max(1, count // ways), max(1, ways // count)


def to_documents(x):
    count, rows, width = x.shape
    ways, me = lax.axis_size("blk"), lax.axis_index("blk")
    per, share = sharing(count)
    if share > 1:
        everything = lax.all_gather(x, "blk", axis=1, tiled=True)
        return lax.dynamic_index_in_dim(everything, me // share, 0, keepdims=False)
    out = jnp.zeros((per, ways * rows, width), x.dtype)
    for hop in range(ways):
        piece = lax.dynamic_slice_in_dim(x, lax.rem(me + hop, ways) * per, per, 0)
        if hop:
            piece = lax.ppermute(piece, "blk", [(i, (i + hop) % ways) for i in range(ways)])
        source = lax.rem(me - hop + ways, ways)
        out = lax.dynamic_update_slice_in_dim(out, piece, source * rows, 1)
    return out.reshape(per * ways * rows, width)


def from_documents(y, count):
    ways, me = lax.axis_size("blk"), lax.axis_index("blk")
    per, share = sharing(count)
    width = y.shape[1]
    if share > 1:
        everything = lax.all_gather(y, "blk", axis=0, tiled=True).reshape(count, -1, width)
        rows = everything.shape[1] // ways
        return lax.dynamic_slice_in_dim(everything, me * rows, rows, 1)
    y = y.reshape(per, -1, width)
    rows = y.shape[1] // ways
    out = jnp.zeros((count, rows, width), y.dtype)
    for hop in range(ways):
        piece = lax.dynamic_slice_in_dim(y, lax.rem(me + hop, ways) * rows, rows, 1)
        if hop:
            piece = lax.ppermute(piece, "blk", [(i, (i + hop) % ways) for i in range(ways)])
        source = lax.rem(me - hop + ways, ways)
        out = lax.dynamic_update_slice_in_dim(out, piece, source * per, 0)
    return out


def among(y, share, split, concat):
    if share == 1:
        return y
    ways = lax.axis_size("blk")
    groups = [list(range(at, at + share)) for at in range(0, ways, share)]
    return lax.all_to_all(
        y, "blk", split, concat, axis_index_groups=groups, tiled=True
    )


def my_share(y, share, axis):
    if share == 1:
        return y
    size = y.shape[axis] // share
    at = lax.rem(lax.axis_index("blk"), share) * size
    return lax.dynamic_slice_in_dim(y, at, size, axis)


def bias_tiles(table):
    offset = jnp.arange(SUB)[None, :] - jnp.arange(SUB)[:, None]
    buckets = bucket_of(offset[None] + SUB * jnp.arange(-1, 2)[:, None, None])
    tiles = jnp.zeros((table.shape[1],) + buckets.shape, f32)
    for b in range(table.shape[0]):
        tiles = jnp.where(buckets == b, table[b][:, None, None, None], tiles)
    return tiles, buckets


def body(
    tokens,
    lengths,
    norm1_gain,
    w_query,
    w_key,
    w_value,
    w_out,
    rel_table,
    norm2_gain,
    w_in,
    w_down,
    cotangent,
):
    micro, docs, rows, width = tokens.shape
    count = micro * docs
    per, share = sharing(count)
    both = ("dp", "blk")
    gains = jnp.pad(jnp.stack([norm1_gain, norm2_gain], 1), ((0, 0), (0, 126)))
    w_first = lax.all_gather(
        jnp.concatenate([w_query, w_key, w_value, gains], 1), both, axis=0, tiled=True
    )
    w_second = lax.all_gather(
        jnp.concatenate([w_out, w_in, w_down], 1), both, axis=0, tiled=True
    )
    gain_rows = w_first[:, 3 * width : 3 * width + 2].astype(f32).T
    gain_first, gain_second = gain_rows[:1], gain_rows[1:]
    own = lax.dynamic_slice_in_dim(
        lengths.reshape(count), lax.axis_index("blk") // share * per, per, 0
    )
    x = to_documents(tokens.reshape(count, rows, width))
    cot = to_documents(cotangent.reshape(count, rows, width))
    x_rows, cot_rows = my_share(x, share, 0), my_share(cot, share, 0)
    own_rows, w_heads = own, w_first
    if share > 1:
        own_rows = own - lax.rem(lax.axis_index("blk"), share) * x_rows.shape[0]
        w_heads = jnp.concatenate(
            [my_share(w_first[:, i * width : (i + 1) * width], share, 1) for i in range(3)], 1
        )

    table = rel_table * LOG2E
    near, buckets = bias_tiles(my_share(table, share, 1))
    far = my_share(jnp.stack([table[15], table[31]], 1), share, 0)

    q, k, v = qkv_call(x, gain_first, w_heads, width // share)
    heads, lse = attend_call(own, far, q, k, v, near)
    mixed, heads_grad, mid, g_second, gn_second = middle_call(
        own_rows, x_rows, among(heads, share, 0, 1), cot_rows, gain_second, w_second
    )
    dq, dk, dv, near_sum, far_sum = attend_back_call(
        own, far, q, k, v, among(heads_grad, share, 1, 0), heads, lse, jnp.swapaxes(near, 2, 3)
    )
    dq, dk, dv = (among(grad, share, 0, 1) for grad in (dq, dk, dv))
    grad_tokens, g_first = last_call(x_rows, dq, dk, dv, mid, gain_first, w_first, gn_second)

    flipped = jnp.swapaxes(buckets, 1, 2)
    rows_of = []
    for b in range(rel_table.shape[0]):
        rows_of.append(jnp.sum(jnp.where(flipped == b, near_sum, 0.0), (1, 2, 3)))
    table_sum = jnp.stack(rows_of)
    far_total = jnp.sum(far_sum, (2, 3))
    table_sum = table_sum.at[15].add(far_total[:, 0]).at[31].add(far_total[:, 1])
    if share > 1:
        at = lax.rem(lax.axis_index("blk"), share) * table_sum.shape[1]
        table_sum = lax.dynamic_update_slice_in_dim(
            jnp.zeros(rel_table.shape, f32), table_sum, at, 1
        )
    grad_table = lax.psum(table_sum, both)

    g_first = lax.psum_scatter(g_first, both, scatter_dimension=0, tiled=True).astype(f32)
    g_second = lax.psum_scatter(g_second, both, scatter_dimension=0, tiled=True).astype(f32)
    hidden = w_in.shape[1]
    return (
        from_documents(mixed, count).reshape(tokens.shape),
        from_documents(grad_tokens, count).reshape(tokens.shape),
        g_first[:, 3 * width],
        g_first[:, :width],
        g_first[:, width : 2 * width],
        g_first[:, 2 * width : 3 * width],
        g_second[:, :width],
        grad_table,
        g_first[:, 3 * width + 1],
        g_second[:, width : width + hidden],
        g_second[:, width + hidden :],
    )


def solution(mesh):
    rows = P(None, "dp", "blk", None)
    weight = P(("dp", "blk"), None)
    gain = P(("dp", "blk"))
    return jax.shard_map(
        body,
        mesh=mesh,
        in_specs=(
            rows,
            P(None, "dp"),
            gain,
            weight,
            weight,
            weight,
            weight,
            P(),
            gain,
            weight,
            weight,
            rows,
        ),
        out_specs=(rows, rows, gain, weight, weight, weight, weight, P(), gain, weight, weight),
        check_vma=False,
    )
```

```python
import functools

import jax
import jax.numpy as jnp
from jax import lax
from jax.experimental import pallas as pl
from jax.experimental.pallas import tpu as pltpu
from jax.sharding import PartitionSpec as P

EPS = 1e-06
NEG = -1e30
LIMITS = (12, 16, 23, 32, 46, 64, 91)
SUB = 128
LOG2E = 1.4426950408889634
GELU_A = 0.7978845608028654
GELU_B = 0.044715
VMEM = 62 * 2**20
NN = (((1,), (0,)), ((), ()))
NT = (((1,), (1,)), ((), ()))
TN = (((0,), (0,)), ((), ()))
low_type = jnp.bfloat16
f32 = jnp.float32


def dot(left, right, dims=NN):
    return lax.dot_general(left, right, dims, preferred_element_type=f32)


def bucket_of(relative):
    distance = jnp.abs(relative)
    far_bucket = 8 + sum(((distance >= border).astype(jnp.int32) for border in LIMITS))
    bucket = jnp.where(distance < 8, distance, far_bucket)
    return bucket + 16 * (relative > 0).astype(jnp.int32)


def norm_rows(rows):
    inverse = lax.rsqrt(jnp.mean(rows * rows, -1, keepdims=True) + EPS)
    return rows * inverse, inverse


def whole(shape):
    return pl.BlockSpec(shape, lambda *_: (0,) * len(shape), pipeline_mode=pl.Buffered(1))


def params():
    return pltpu.CompilerParams(vmem_limit_bytes=VMEM)


def struct(shape, dtype=low_type):
    return jax.ShapeDtypeStruct(shape, dtype)


SMEM = pl.BlockSpec(memory_space=pltpu.SMEM)


def tile_buckets(apart, keys_dim):
    keys = lax.broadcasted_iota(jnp.int32, (SUB, SUB), keys_dim)
    queries = lax.broadcasted_iota(jnp.int32, (SUB, SUB), 1 - keys_dim)
    return bucket_of(keys - queries + SUB * apart)


def tile_range(apart):
    return range(0 if apart <= 0 else 16, 16 if apart < 0 else 32)


def fill_tiles(near, table_ref, pair, keys_dim):
    for apart in (-1, 0, 1):
        buckets = tile_buckets(apart, keys_dim)
        masks = [(b, buckets == b) for b in tile_range(apart)]
        for h in range(2):
            tile = jnp.zeros((SUB, SUB), f32)
            for b, mask in masks:
                tile = jnp.where(mask, table_ref[2 * pair + h, b], tile)
            near[h, apart + 1] = tile


def qkv_kernel(x_ref, gain_ref, w_ref, q_ref, k_ref, v_ref):
    width = q_ref.shape[1]
    normed, _ = norm_rows(x_ref[...].astype(f32))
    low = (normed * gain_ref[...]).astype(low_type)
    q_ref[...] = (dot(low, w_ref[:, :width]) * (0.125 * LOG2E)).astype(low_type)
    k_ref[...] = dot(low, w_ref[:, width : 2 * width]).astype(low_type)
    v_ref[...] = dot(low, w_ref[:, 2 * width : 3 * width]).astype(low_type)


def qkv_call(x, gain, w_first, heads_width, rows=512):
    total, width = x.shape
    row = pl.BlockSpec((rows, width), lambda i: (i, 0))
    return pl.pallas_call(
        qkv_kernel,
        grid=(total // rows,),
        in_specs=[row, whole((1, width)), whole(w_first.shape)],
        out_specs=[pl.BlockSpec((rows, heads_width), lambda i: (i, 0))] * 3,
        out_shape=[struct((total, heads_width))] * 3,
        compiler_params=params(),
        name="qkv",
    )(x, gain, w_first)


def attend_kernel(
    len_ref, table_ref, q_ref, k_ref, v_ref, o_ref, lse_ref, near_ref, *, rows
):
    pair, doc = pl.program_id(0), pl.program_id(1)

    @pl.when(doc == 0)
    def _():
        fill_tiles(near_ref, table_ref, pair, 1)

    seq = q_ref.shape[0]
    subs = seq // SUB
    first = lax.broadcasted_iota(jnp.int32, (1, 128), 1) < 64
    live = lax.broadcasted_iota(jnp.int32, (1, seq), 1) < len_ref[doc]
    one = jnp.ones((), low_type)
    k, v = k_ref[...], v_ref[...]
    v_ones = (jnp.where(first, v, one), jnp.where(first, one, v))
    for block in range(seq // rows):
        span = slice(block * rows, (block + 1) * rows)
        q = q_ref[span, :]
        outs, tops = [], []
        for h in range(2):
            q_one = jnp.where(first == (h == 0), q, jnp.zeros((), low_type))
            raw = dot(q_one, k, NT)
            strips = []
            for a in range(rows // SUB):
                at = block * (rows // SUB) + a
                strip = raw[a * SUB : (a + 1) * SUB]
                low, high = max(at - 1, 0), min(at + 2, subs)
                parts = []
                if low > 0:
                    parts.append(strip[:, : low * SUB] + table_ref[2 * pair + h, 15])
                for b in range(low, high):
                    parts.append(strip[:, b * SUB : (b + 1) * SUB] + near_ref[h, b - at + 1])
                if high < subs:
                    parts.append(strip[:, high * SUB :] + table_ref[2 * pair + h, 31])
                strips.append(jnp.concatenate(parts, 1))
            scores = jnp.where(live, jnp.concatenate(strips, 0), NEG)
            top = jnp.max(scores, 1, keepdims=True)
            outs.append(dot(jnp.exp2(scores - top).astype(low_type), v_ones[h]))
            tops.append(top)
        total = jnp.where(first, pltpu.roll(outs[0], 64, 1), pltpu.roll(outs[1], 64, 1))
        o_ref[span, :] = (jnp.where(first, outs[0], outs[1]) / total).astype(low_type)
        log_total = (jnp.where(first, tops[0], tops[1]) + jnp.log2(total)).T
        lse_ref[0, 0, 0:1, span] = log_total[0:1]
        lse_ref[0, 0, 1:2, span] = log_total[64:65]


def attend_call(lengths, table, q, k, v, rows=512):
    docs, (total, width) = lengths.shape[0], q.shape
    seq, pairs = total // docs, width // 128
    slab = pl.BlockSpec((seq, 128), lambda p, d: (d, p))
    return pl.pallas_call(
        functools.partial(attend_kernel, rows=rows),
        grid=(pairs, docs),
        in_specs=[
            SMEM,
            SMEM,
            slab,
            slab,
            slab,
        ],
        out_specs=[slab, pl.BlockSpec((1, 1, 2, seq), lambda p, d: (d, p, 0, 0))],
        out_shape=[struct((total, width)), struct((docs, pairs, 2, seq), f32)],
        scratch_shapes=[pltpu.VMEM((2, 3, SUB, SUB), f32)],
        compiler_params=params(),
        name="attend",
    )(lengths, table, q, k, v)


def middle_kernel(
    len_ref,
    x_ref,
    heads_ref,
    cot_ref,
    gain_ref,
    w_ref,
    mixed_ref,
    hgrad_ref,
    mid_ref,
    gw_ref,
    gn_ref,
    acc,
    acc_gain,
    *,
    seq,
    chunk,
):
    step = pl.program_id(0)
    rows, width = x_ref.shape
    hidden = (w_ref.shape[1] - width) // 2

    @pl.when(step == 0)
    def _():
        acc[...] = jnp.zeros_like(acc)
        acc_gain[...] = jnp.zeros_like(acc_gain)

    per = seq // rows
    place = (step % per) * rows + lax.broadcasted_iota(jnp.int32, (rows, 1), 0)
    heads, gain = heads_ref[...], gain_ref[...]
    residual = x_ref[...].astype(f32) + dot(heads, w_ref[:, :width])
    normed, inverse = norm_rows(residual)
    low = (normed * gain).astype(low_type)
    out_grad = jnp.where(place < len_ref[step // per], cot_ref[...], jnp.zeros((), low_type))
    mixed, normed_grad = residual, jnp.zeros((rows, width), f32)
    for at in range(0, hidden, chunk):
        up = slice(width + at, width + at + chunk)
        down = slice(width + hidden + at, width + hidden + at + chunk)
        u = dot(low, w_ref[:, up])
        square = u * u
        bend = jnp.tanh(u * (GELU_A + GELU_A * GELU_B * square))
        half = 0.5 + 0.5 * bend
        act = (u * half).astype(low_type)
        slope = half + (0.5 * u) * (1 - bend * bend) * (GELU_A + 3 * GELU_A * GELU_B * square)
        up_grad = (dot(out_grad, w_ref[:, down]) * slope).astype(low_type)
        mixed = mixed + dot(act, w_ref[:, down], NT)
        normed_grad = normed_grad + dot(up_grad, w_ref[:, up], NT)
        acc[:, down] += dot(out_grad, act, TN)
        acc[:, up] += dot(low, up_grad, TN)
    mixed_ref[...] = mixed.astype(low_type)
    scaled = normed_grad * gain
    inner = jnp.mean(scaled * normed, -1, keepdims=True)
    mid = (out_grad.astype(f32) + inverse * (scaled - normed * inner)).astype(low_type)
    acc_gain[...] += jnp.sum((normed_grad * normed).reshape(rows // 8, 8, width), 0)
    mid_ref[...] = mid
    acc[:, :width] += dot(heads, mid, TN)
    hgrad_ref[...] = dot(mid, w_ref[:, :width], NT).astype(low_type)

    @pl.when(step == pl.num_programs(0) - 1)
    def _():
        gw_ref[...] = acc[...].astype(low_type)
        gn_ref[...] = jnp.sum(acc_gain[...], 0, keepdims=True)


def middle_call(lengths, x, heads, cot, gain, w_second, rows=256, chunk=1024):
    total, width = x.shape
    row = pl.BlockSpec((rows, width), lambda i: (i, 0))
    return pl.pallas_call(
        functools.partial(middle_kernel, seq=total // lengths.shape[0], chunk=chunk),
        grid=(total // rows,),
        in_specs=[SMEM, row, row, row, whole((1, width)), whole(w_second.shape)],
        out_specs=[row, row, row, whole(w_second.shape), whole((1, width))],
        out_shape=[struct((total, width))] * 3 + [struct(w_second.shape), struct((1, width), f32)],
        scratch_shapes=[pltpu.VMEM(w_second.shape, f32), pltpu.VMEM((8, width), f32)],
        compiler_params=params(),
        name="middle",
    )(lengths, x, heads, cot, gain, w_second)


def attend_back_kernel(
    len_ref,
    table_ref,
    q_ref,
    k_ref,
    v_ref,
    grad_ref,
    o_ref,
    lse_ref,
    dq_ref,
    dk_ref,
    dv_ref,
    table_sum,
    near_ref,
    near_sum,
    far_sum,
    acc,
    *,
    keys,
    queries,
):
    pair, doc = pl.program_id(0), pl.program_id(1)
    seq = q_ref.shape[0]
    first = lax.broadcasted_iota(jnp.int32, (1, 128), 1) < 64
    zero = jnp.zeros((), low_type)

    def halves(x):
        return jnp.where(first, x, zero), jnp.where(first, zero, x)

    grad = grad_ref[...]
    q_one, g_one = halves(q_ref[...]), halves(grad)
    product = grad.astype(f32) * o_ref[...].astype(f32)
    upper = product.astype(low_type)
    lower = (product - upper.astype(f32)).astype(low_type)
    row = lax.broadcasted_iota(jnp.int32, (16, 128), 0)
    column = lax.broadcasted_iota(jnp.int32, (16, 128), 1)
    member = (row == column // 64).astype(f32).astype(low_type)
    delta = dot(member, upper, NT) + dot(member, lower, NT)

    @pl.when(doc == 0)
    def _():
        fill_tiles(near_ref, table_ref, pair, 0)
        near_sum[...] = jnp.zeros_like(near_sum)
        far_sum[...] = jnp.zeros_like(far_sum)

    acc[...] = jnp.zeros_like(acc)
    for kb in range(seq // keys):
        held = slice(kb * keys, (kb + 1) * keys)
        k, v = k_ref[held, :], v_ref[held, :]
        k_one = halves(k)
        live = (kb * keys + lax.broadcasted_iota(jnp.int32, (keys, 1), 0)) < len_ref[doc]
        dk = jnp.zeros((keys, 128), f32)
        dv = jnp.zeros((keys, 128), f32)
        for qb in range(seq // queries):
            span = slice(qb * queries, (qb + 1) * queries)
            dq = None
            for h in range(2):
                scores = dot(k, q_one[h][span], NT)
                prob_grad = dot(v, g_one[h][span], NT)
                lse = lse_ref[0, 0, h : h + 1, span]
                lse_side = (lse - table_ref[2 * pair + h, 15], lse - table_ref[2 * pair + h, 31])
                row_delta = delta[h : h + 1, span]
                prob_rows, grad_rows = [], []
                for a in range(keys // SUB):
                    down = slice(a * SUB, (a + 1) * SUB)
                    probs, grads = [], []
                    for b in range(queries // SUB):
                        across = slice(b * SUB, (b + 1) * SUB)
                        apart = kb * (keys // SUB) + a - qb * (queries // SUB) - b
                        tile = scores[down, across]
                        if abs(apart) <= 1:
                            tile = tile + near_ref[h, apart + 1] - lse[:, across]
                        else:
                            tile = tile - lse_side[int(apart > 0)][:, across]
                        prob = jnp.where(live[down], jnp.exp2(tile), 0.0)
                        score_grad = prob * (prob_grad[down, across] - row_delta[:, across])
                        if abs(apart) <= 1:
                            near_sum[h, apart + 1] += score_grad
                        else:
                            far_sum[h, int(apart > 0)] += jnp.sum(
                                score_grad.reshape(SUB // 8, 8, SUB), 0
                            )
                        probs.append(prob.astype(low_type))
                        grads.append(score_grad.astype(low_type))
                    prob_rows.append(jnp.concatenate(probs, 1))
                    grad_rows.append(jnp.concatenate(grads, 1))
                prob_low = jnp.concatenate(prob_rows, 0)
                grad_low = jnp.concatenate(grad_rows, 0)
                dv = dv + dot(prob_low, g_one[h][span])
                dk = dk + dot(grad_low, q_one[h][span])
                part = dot(grad_low, k_one[h], TN)
                dq = part if dq is None else dq + part
            acc[span, :] += dq
        dv_ref[held, :] = dv.astype(low_type)
        dk_ref[held, :] = (dk * (1 / LOG2E)).astype(low_type)
    dq_ref[...] = (acc[...] * 0.125).astype(low_type)

    @pl.when(doc == pl.num_programs(1) - 1)
    def _():
        sums = {}
        for apart in (-1, 0, 1):
            buckets = tile_buckets(apart, 0)
            masks = [(b, buckets == b) for b in tile_range(apart)]
            for h in range(2):
                tile = near_sum[h, apart + 1]
                for b, mask in masks:
                    part = jnp.sum(jnp.where(mask, tile, 0.0), 0, keepdims=True)
                    sums[h, b] = sums[h, b] + part if (h, b) in sums else part
        for h in range(2):
            for side, b in enumerate((15, 31)):
                sums[h, b] = sums[h, b] + jnp.sum(far_sum[h, side], 0, keepdims=True)
            for b in range(32):
                table_sum[h, b : b + 1] = sums[h, b]


def attend_back_call(lengths, table, q, k, v, grad, o, lse, keys=256, queries=1024):
    docs, (total, width) = lengths.shape[0], q.shape
    seq, pairs = total // docs, width // 128
    queries = min(queries, seq)
    slab = pl.BlockSpec((seq, 128), lambda p, d: (d, p))
    return pl.pallas_call(
        functools.partial(attend_back_kernel, keys=keys, queries=queries),
        grid=(pairs, docs),
        in_specs=[
            SMEM,
            SMEM,
            slab,
            slab,
            slab,
            slab,
            slab,
            pl.BlockSpec((1, 1, 2, seq), lambda p, d: (d, p, 0, 0)),
        ],
        out_specs=[slab, slab, slab, pl.BlockSpec((2, 32, SUB), lambda p, d: (p, 0, 0))],
        out_shape=[struct((total, width))] * 3 + [struct((2 * pairs, 32, SUB), f32)],
        scratch_shapes=[
            pltpu.VMEM((2, 3, SUB, SUB), f32),
            pltpu.VMEM((2, 3, SUB, SUB), f32),
            pltpu.VMEM((2, 2, 8, SUB), f32),
            pltpu.VMEM((seq, 128), f32),
        ],
        compiler_params=params(),
        name="attend_back",
    )(lengths, table, q, k, v, grad, o, lse)


def last_kernel(
    x_ref,
    dq_ref,
    dk_ref,
    dv_ref,
    mid_ref,
    gain_ref,
    w_ref,
    gn_second_ref,
    gt_ref,
    gw_ref,
    acc,
    acc_gain,
):
    step = pl.program_id(0)
    rows, width = x_ref.shape

    @pl.when(step == 0)
    def _():
        acc[...] = jnp.zeros_like(acc)
        acc_gain[...] = jnp.zeros_like(acc_gain)

    gain = gain_ref[...]
    normed, inverse = norm_rows(x_ref[...].astype(f32))
    low = (normed * gain).astype(low_type)
    normed_grad = None
    for index, ref in enumerate((dq_ref, dk_ref, dv_ref)):
        part = slice(index * width, (index + 1) * width)
        grad = ref[...]
        acc[:, part] += dot(low, grad, TN)
        back = dot(grad, w_ref[:, part], NT)
        normed_grad = back if normed_grad is None else normed_grad + back
    acc_gain[...] += jnp.sum((normed_grad * normed).reshape(rows // 8, 8, width), 0)
    scaled = normed_grad * gain
    inner = jnp.mean(scaled * normed, -1, keepdims=True)
    gt_ref[...] = (mid_ref[...].astype(f32) + inverse * (scaled - normed * inner)).astype(low_type)

    @pl.when(step == pl.num_programs(0) - 1)
    def _():
        gw_ref[:, : 3 * width] = acc[...].astype(low_type)
        pick = lax.broadcasted_iota(jnp.int32, (128, 1), 0)
        gains = jnp.where(
            pick == 0,
            jnp.sum(acc_gain[...], 0, keepdims=True),
            jnp.where(pick == 1, gn_second_ref[...], 0.0),
        )
        gw_ref[:, 3 * width :] = gains.T.astype(low_type)


def last_call(x, dq, dk, dv, mid, gain, w_first, gn_second, rows=512):
    total, width = x.shape
    row = pl.BlockSpec((rows, width), lambda i: (i, 0))
    return pl.pallas_call(
        last_kernel,
        grid=(total // rows,),
        in_specs=[row] * 5 + [whole((1, width)), whole(w_first.shape), whole((1, width))],
        out_specs=[row, whole(w_first.shape)],
        out_shape=[struct((total, width)), struct(w_first.shape)],
        scratch_shapes=[pltpu.VMEM((width, 3 * width), f32), pltpu.VMEM((8, width), f32)],
        compiler_params=params(),
        name="last",
    )(x, dq, dk, dv, mid, gain, w_first, gn_second)


MESH_ID = pl.DeviceIdType.MESH
ANY = pl.BlockSpec(memory_space=pl.ANY)
VMEM_WHOLE = pl.BlockSpec(memory_space=pltpu.VMEM)
SPARE = 128


class Place:
    def __init__(self):
        self.dp, self.y = lax.axis_index("dp"), lax.axis_index("blk")
        self.depth = lax.axis_size("dp") // 4
        self.z = self.dp // 4
        self.x = lax.rem(self.dp // 2, 2)
        self.core = lax.rem(self.dp, 2)
        self.has_left = self.z > 0
        self.has_right = self.z < self.depth - 1

    def unit(self, z, x, core):
        return (z * 2 + x) * 2 + core

    def left(self):
        return (self.dp - 4, self.y)

    def right(self):
        return (self.dp + 4, self.y)

    def over_x(self):
        return (self.unit(self.z, 1 - self.x, self.core), self.y)

    def over_core(self):
        return (self.unit(self.z, self.x, 1 - self.core), self.y)

    def over_y(self):
        return (self.dp, 1 - self.y)

    def greet(self):
        barrier = pltpu.get_barrier_semaphore()
        for target in (self.over_x(), self.over_core(), self.over_y()):
            pl.semaphore_signal(barrier, device_id=target, device_id_type=MESH_ID)

        @pl.when(self.has_left)
        def _():
            pl.semaphore_signal(barrier, device_id=self.left(), device_id_type=MESH_ID)

        @pl.when(self.has_right)
        def _():
            pl.semaphore_signal(barrier, device_id=self.right(), device_id_type=MESH_ID)

        ends = self.has_left.astype(jnp.int32) + self.has_right.astype(jnp.int32)
        pl.semaphore_wait(barrier, 3 + ends)


def remote(source, target, send, recv, device):
    return pltpu.make_async_remote_copy(
        src_ref=source,
        dst_ref=target,
        send_sem=send,
        recv_sem=recv,
        device_id=device,
        device_id_type=MESH_ID,
    )


def head_kernel(
    shard_ref, tokens_ref, w_ref, x_ref, other, pair, send_sem, recv_sem, swap_sem, local_sem
):
    place = Place()
    depth, unit_rows = place.depth, pair.shape[0]
    own_rows = unit_rows // 2
    per, rows = x_ref.shape[0], tokens_ref.shape[1]
    place.greet()

    def unit_at(u):
        return w_ref.at[pl.ds(pl.multiple_of(u * unit_rows, 16), unit_rows)]

    meet = remote(shard_ref, other, swap_sem.at[0], swap_sem.at[1], place.over_y())
    meet.start()
    target = x_ref.at[:, pl.ds(pl.multiple_of(place.y * rows, 16), rows)]
    swap = remote(
        tokens_ref.at[pl.ds((1 - place.y) * per, per)],
        target,
        swap_sem.at[2],
        swap_sem.at[3],
        place.over_y(),
    )
    swap.start()
    keep = pltpu.make_async_copy(tokens_ref.at[pl.ds(place.y * per, per)], target, local_sem.at[0])
    keep.start()
    meet.wait()
    mine, theirs = shard_ref[:own_rows].astype(f32), other[:own_rows].astype(f32)
    is_first = place.y == 0
    pair[...] = jnp.concatenate(
        [jnp.where(is_first, mine, theirs), jnp.where(is_first, theirs, mine)], 0
    ).astype(low_type)
    mine_at = place.unit(place.z, place.x, place.core)
    put = pltpu.make_async_copy(pair, unit_at(mine_at), local_sem.at[1])
    put.start()

    def sends(u, source, kinds):
        out = []
        for kind in kinds:
            device = (place.left, place.right, place.over_x, place.over_core)[kind]()
            out.append(remote(source, unit_at(u), send_sem.at[kind, u], recv_sem.at[u], device))
        return out

    def arrival(u):
        remote(
            unit_at(u), unit_at(u), send_sem.at[3, u], recv_sem.at[u], place.over_core()
        ).wait_recv()

    for copy in sends(mine_at, pair, (2, 3)):
        copy.start()
    for kind, there in ((0, place.has_left), (1, place.has_right)):

        @pl.when(there)
        def _(kind=kind):
            sends(mine_at, pair, (kind,))[0].start()

    for step in range(1, depth):
        for kind, z in ((1, place.z - step), (0, place.z + step)):
            u = place.unit(z, place.x, place.core)
            onward = place.has_right if kind == 1 else place.has_left

            @pl.when((z >= 0) & (z < depth))
            def _(u=u, kind=kind, onward=onward):
                arrival(u)

                @pl.when(onward)
                def _():
                    sends(u, unit_at(u), (kind,))[0].start()

                for copy in sends(u, unit_at(u), (2, 3)):
                    copy.start()

    for z in range(depth):
        u = place.unit(z, 1 - place.x, place.core)
        arrival(u)
        sends(u, unit_at(u), (3,))[0].start()
    for z in range(depth):
        for x in range(2):
            arrival(place.unit(z, x, 1 - place.core))
    put.wait()
    keep.wait()
    for z in range(depth):
        u = place.unit(z, place.x, place.core)
        for copy in sends(u, unit_at(u), (2, 3)):
            copy.wait_send()

        @pl.when((place.z >= z) & place.has_right)
        def _(u=u):
            sends(u, unit_at(u), (1,))[0].wait_send()

        @pl.when((place.z <= z) & place.has_left)
        def _(u=u):
            sends(u, unit_at(u), (0,))[0].wait_send()

        u = place.unit(z, 1 - place.x, place.core)
        sends(u, unit_at(u), (3,))[0].wait_send()
    swap.wait()


def head_call(shard, tokens, ways):
    units = lax.axis_size("dp")
    count, rows, width = tokens.shape
    own_rows, columns = shard.shape
    padded = jnp.pad(shard, ((0, -own_rows % 16), (0, 0)))
    return pl.pallas_call(
        head_kernel,
        in_specs=[VMEM_WHOLE, ANY],
        out_specs=[ANY, ANY],
        out_shape=[
            struct((units * ways * own_rows, columns)),
            struct((count // ways, rows * ways, width)),
        ],
        scratch_shapes=[
            pltpu.VMEM(padded.shape, low_type),
            pltpu.VMEM((ways * own_rows, columns), low_type),
            pltpu.SemaphoreType.DMA((4, units)),
            pltpu.SemaphoreType.DMA((units,)),
            pltpu.SemaphoreType.DMA((4,)),
            pltpu.SemaphoreType.DMA((2,)),
        ],
        compiler_params=pltpu.CompilerParams(
            collective_id=1, has_side_effects=True, vmem_limit_bytes=VMEM
        ),
        name="head",
    )(padded, tokens)


def tail_kernel(
    g_ref,
    gt_ref,
    table_ref,
    gq_ref,
    gk_ref,
    gv_ref,
    gain_ref,
    out_ref,
    table_out,
    core_buf,
    x_send,
    x_buf,
    z_send,
    z_buf,
    y_send,
    y_buf,
    table_send,
    table_buf,
    core_sem,
    x_sem,
    z_sem,
    y_sem,
    table_sem,
    local_sem,
):
    place = Place()
    depth, unit_rows = place.depth, core_buf.shape[2]
    own_rows, width = unit_rows // 2, gq_ref.shape[1]
    per, rows = gt_ref.shape[0], out_ref.shape[1]
    place.greet()
    target = out_ref.at[pl.ds(place.y * per, per)]
    swap = remote(
        gt_ref.at[:, pl.ds(pl.multiple_of((1 - place.y) * rows, 16), rows)],
        target,
        y_sem.at[2],
        y_sem.at[3],
        place.over_y(),
    )
    keep = pltpu.make_async_copy(
        gt_ref.at[:, pl.ds(pl.multiple_of(place.y * rows, 16), rows)], target, local_sem
    )
    order = []
    for at in range((depth + 1) // 2):
        order += [depth - 1 - at] + ([at] if at != depth - 1 - at else [])

    def unit_at(u):
        return g_ref.at[pl.ds(pl.multiple_of(u * unit_rows, 16), unit_rows)]

    def over_core(side, z):
        x = place.x if side == 0 else 1 - place.x
        return remote(
            unit_at(place.unit(z, x, 1 - place.core)),
            core_buf.at[side, z],
            core_sem.at[0, side, z],
            core_sem.at[1, side, z],
            place.over_core(),
        )

    def over_x(z):
        return remote(x_send.at[z], x_buf.at[z], x_sem.at[0, z], x_sem.at[1, z], place.over_x())

    def along(kind, z):
        device = place.right() if kind else place.left()
        return remote(
            z_send.at[z], z_buf.at[kind, z], z_sem.at[0, z], z_sem.at[1 + kind, z], device
        )

    for side in (1, 0):
        for z in order:
            over_core(side, z).start()
    swap.start()
    keep.start()

    tables = (
        place.over_core(),
        place.over_x(),
        place.over_y(),
    )
    span = 1
    while span < depth:
        flip = place.z + span - 2 * span * lax.rem(place.z // span, 2)
        tables += ((place.unit(flip, place.x, place.core), place.y),)
        span *= 2
    reduced = table_ref[...]

    def table_copy(at):
        return remote(
            table_send.at[at], table_buf.at[at], table_sem.at[0, at], table_sem.at[1, at], tables[at]
        )

    def table_start(at, value):
        table_send[at] = value
        table_copy(at).start()

    def table_finish(at, value):
        table_copy(at).wait()
        return value + table_buf[at]

    table_start(0, reduced)
    for z in order:
        over_core(1, z).wait_recv()
        mine = unit_at(place.unit(z, 1 - place.x, place.core))
        x_send[z] = (mine[...].astype(f32) + core_buf[1, z].astype(f32)).astype(low_type)
        over_x(z).start()
    reduced = table_finish(0, reduced)
    table_start(1, reduced)
    at = 1
    for z in order:
        over_core(0, z).wait_recv()
        over_x(z).wait_recv()
        mine = unit_at(place.unit(z, place.x, place.core))
        part = mine[...].astype(f32) + core_buf[0, z].astype(f32) + x_buf[z].astype(f32)
        z_send[z] = part.astype(low_type)

        @pl.when(place.z < z)
        def _(z=z):
            @pl.when(place.has_left)
            def _():
                along(1, z).wait_recv()
                z_send[z] = (z_send[z].astype(f32) + z_buf[1, z].astype(f32)).astype(low_type)

            along(1, z).start()

        @pl.when(place.z > z)
        def _(z=z):
            @pl.when(place.has_right)
            def _():
                along(0, z).wait_recv()
                z_send[z] = (z_send[z].astype(f32) + z_buf[0, z].astype(f32)).astype(low_type)

            along(0, z).start()

        if at < len(tables):
            reduced = table_finish(at, reduced)
            at += 1
            if at < len(tables):
                table_start(at, reduced)

    for z in range(depth):

        @pl.when(place.z == z)
        def _(z=z):
            @pl.when(place.has_left)
            def _():
                along(1, z).wait_recv()
                z_send[z] = (z_send[z].astype(f32) + z_buf[1, z].astype(f32)).astype(low_type)

            @pl.when(place.has_right)
            def _():
                along(0, z).wait_recv()
                z_send[z] = (z_send[z].astype(f32) + z_buf[0, z].astype(f32)).astype(low_type)

    total = z_send[place.z].astype(f32)
    upper, lower = total[:own_rows], total[own_rows:]
    is_first = place.y == 0
    y_send[:own_rows] = jnp.where(is_first, lower, upper)
    meet = remote(y_send, y_buf, y_sem.at[0], y_sem.at[1], place.over_y())
    meet.start()
    while at < len(tables):
        reduced = table_finish(at, reduced)
        at += 1
        if at < len(tables):
            table_start(at, reduced)
    table_out[...] = reduced
    meet.wait()
    final = jnp.where(is_first, upper, lower) + y_buf[:own_rows]
    gq_ref[...] = final[:, :width]
    gk_ref[...] = final[:, width : 2 * width]
    gv_ref[...] = final[:, 2 * width : 3 * width]
    gain_ref[...] = final[:, 3 * width :]
    for z in range(depth):
        for side in (1, 0):
            over_core(side, z).wait_send()
        over_x(z).wait_send()

        @pl.when(place.z < z)
        def _(z=z):
            along(1, z).wait_send()

        @pl.when(place.z > z)
        def _(z=z):
            along(0, z).wait_send()

    keep.wait()
    swap.wait()


def tail_call(grads, gt, table, ways):
    units = lax.axis_size("dp")
    depth = units // 4
    steps = 3 + (depth - 1).bit_length()
    per, seq, width = gt.shape
    columns = grads.shape[1]
    unit = grads.shape[0] // units
    own = unit // ways
    return pl.pallas_call(
        tail_kernel,
        in_specs=[VMEM_WHOLE, ANY, VMEM_WHOLE],
        out_specs=[VMEM_WHOLE] * 4 + [ANY, VMEM_WHOLE],
        out_shape=[struct((own, width), f32)] * 3
        + [
            struct((own, columns - 3 * width), f32),
            struct((per * ways, seq // ways, width)),
            struct(table.shape, f32),
        ],
        scratch_shapes=[
            pltpu.VMEM((2, depth, unit, columns), low_type),
            pltpu.VMEM((depth, unit, columns), low_type),
            pltpu.VMEM((depth, unit, columns), low_type),
            pltpu.VMEM((depth, unit, columns), low_type),
            pltpu.VMEM((2, depth, unit, columns), low_type),
            pltpu.VMEM((own, columns), f32),
            pltpu.VMEM((own, columns), f32),
            pltpu.VMEM((steps,) + table.shape, f32),
            pltpu.VMEM((steps,) + table.shape, f32),
            pltpu.SemaphoreType.DMA((2, 2, depth)),
            pltpu.SemaphoreType.DMA((2, depth)),
            pltpu.SemaphoreType.DMA((3, depth)),
            pltpu.SemaphoreType.DMA((4,)),
            pltpu.SemaphoreType.DMA((2, steps)),
            pltpu.SemaphoreType.DMA,
        ],
        compiler_params=pltpu.CompilerParams(
            collective_id=2, has_side_effects=True, vmem_limit_bytes=VMEM
        ),
        name="tail",
    )(grads, gt, table)


def sharing(count):
    ways = lax.axis_size("blk")
    return max(1, count // ways), max(1, ways // count)


def to_documents(x):
    count, rows, width = x.shape
    ways, me = lax.axis_size("blk"), lax.axis_index("blk")
    per, share = sharing(count)
    if share > 1:
        everything = lax.all_gather(x, "blk", axis=1, tiled=True)
        return lax.dynamic_index_in_dim(everything, me // share, 0, keepdims=False)
    out = jnp.zeros((per, ways * rows, width), x.dtype)
    for hop in range(ways):
        piece = lax.dynamic_slice_in_dim(x, lax.rem(me + hop, ways) * per, per, 0)
        if hop:
            piece = lax.ppermute(piece, "blk", [(i, (i + hop) % ways) for i in range(ways)])
        source = lax.rem(me - hop + ways, ways)
        out = lax.dynamic_update_slice_in_dim(out, piece, source * rows, 1)
    return out.reshape(per * ways * rows, width)


def from_documents(y, count):
    ways, me = lax.axis_size("blk"), lax.axis_index("blk")
    per, share = sharing(count)
    width = y.shape[1]
    if share > 1:
        everything = lax.all_gather(y, "blk", axis=0, tiled=True).reshape(count, -1, width)
        rows = everything.shape[1] // ways
        return lax.dynamic_slice_in_dim(everything, me * rows, rows, 1)
    y = y.reshape(per, -1, width)
    rows = y.shape[1] // ways
    out = jnp.zeros((count, rows, width), y.dtype)
    for hop in range(ways):
        piece = lax.dynamic_slice_in_dim(y, lax.rem(me + hop, ways) * rows, rows, 1)
        if hop:
            piece = lax.ppermute(piece, "blk", [(i, (i + hop) % ways) for i in range(ways)])
        source = lax.rem(me - hop + ways, ways)
        out = lax.dynamic_update_slice_in_dim(out, piece, source * per, 0)
    return out


def among(y, share, split, concat):
    if share == 1:
        return y
    ways = lax.axis_size("blk")
    groups = [list(range(at, at + share)) for at in range(0, ways, share)]
    return lax.all_to_all(
        y, "blk", split, concat, axis_index_groups=groups, tiled=True
    )


def my_share(y, share, axis):
    if share == 1:
        return y
    size = y.shape[axis] // share
    at = lax.rem(lax.axis_index("blk"), share) * size
    return lax.dynamic_slice_in_dim(y, at, size, axis)


def body(
    tokens,
    lengths,
    norm1_gain,
    w_query,
    w_key,
    w_value,
    w_out,
    rel_table,
    norm2_gain,
    w_in,
    w_down,
    cotangent,
):
    micro, docs, rows, width = tokens.shape
    count = micro * docs
    per, share = sharing(count)
    both = ("dp", "blk")
    direct = lax.axis_size("blk") == 2 and per * 2 == count and lax.axis_size("dp") % 4 == 0
    gains = jnp.pad(jnp.stack([norm1_gain, norm2_gain], 1), ((0, 0), (0, SPARE - 2)))
    shard_first = jnp.concatenate([w_query, w_key, w_value, gains], 1)
    shard_second = jnp.concatenate([w_out, w_in, w_down], 1)
    w_second = lax.all_gather(shard_second, both, axis=0, tiled=True)
    tokens_here = tokens.reshape(count, rows, width)
    cot_here = cotangent.reshape(count, rows, width)
    if direct:
        w_first, x = head_call(shard_first, tokens_here, 2)
        x = x.reshape(-1, width)
        cot_here, x = lax.optimization_barrier((cot_here, x))
    else:
        w_first = lax.all_gather(shard_first, both, axis=0, tiled=True)
        x = to_documents(tokens_here)
    cot = to_documents(cot_here)
    gain_rows = w_first[:, 3 * width : 3 * width + 2].astype(f32).T
    gain_first, gain_second = gain_rows[:1], gain_rows[1:]
    own = lax.dynamic_slice_in_dim(
        lengths.reshape(count), lax.axis_index("blk") // share * per, per, 0
    )
    x_rows, cot_rows = my_share(x, share, 0), my_share(cot, share, 0)
    own_rows, w_heads = own, w_first
    if share > 1:
        own_rows = own - lax.rem(lax.axis_index("blk"), share) * x_rows.shape[0]
        w_heads = jnp.concatenate(
            [my_share(w_first[:, i * width : (i + 1) * width], share, 1) for i in range(3)], 1
        )
    table = my_share((rel_table * LOG2E).T, share, 0)

    q, k, v = qkv_call(x, gain_first, w_heads, width // share)
    heads, lse = attend_call(own, table, q, k, v)
    mixed, heads_grad, mid, g_second, gn_second = middle_call(
        own_rows, x_rows, among(heads, share, 0, 1), cot_rows, gain_second, w_second
    )
    mixed = from_documents(mixed, count)
    g_second = lax.psum_scatter(g_second, both, scatter_dimension=0, tiled=True).astype(f32)
    dq, dk, dv, table_sum = attend_back_call(
        own, table, q, k, v, among(heads_grad, share, 1, 0), heads, lse
    )
    dq, dk, dv = (among(grad, share, 0, 1) for grad in (dq, dk, dv))
    grad_tokens, g_first = last_call(x_rows, dq, dk, dv, mid, gain_first, w_first, gn_second)
    table_sum = jnp.sum(table_sum, 2)
    if direct:
        head_count, bucket_count = table_sum.shape
        table_sum = jnp.pad(
            table_sum, ((0, -head_count % 8), (0, SUB - bucket_count))
        )
        grad_query, grad_key, grad_value, gains, grad_tokens, table_sum = tail_call(
            g_first, grad_tokens.reshape(per, -1, width), table_sum, 2
        )
        grad_table = table_sum[:head_count, :bucket_count].T
    else:
        grad_tokens = from_documents(grad_tokens, count)
        g_first = lax.psum_scatter(g_first, both, scatter_dimension=0, tiled=True).astype(f32)
        grad_query, grad_key, grad_value, gains = jnp.split(
            g_first, (width, 2 * width, 3 * width), 1
        )
        if share > 1:
            at = lax.rem(lax.axis_index("blk"), share) * table_sum.shape[0]
            table_sum = lax.dynamic_update_slice_in_dim(
                jnp.zeros(rel_table.T.shape, f32), table_sum, at, 0
            )
        grad_table = lax.psum(table_sum, both).T
    hidden = w_in.shape[1]
    return (
        mixed.reshape(tokens.shape),
        grad_tokens.reshape(tokens.shape),
        gains[:, 0],
        grad_query,
        grad_key,
        grad_value,
        g_second[:, :width],
        grad_table,
        gains[:, 1],
        g_second[:, width : width + hidden],
        g_second[:, width + hidden :],
    )


def solution(mesh):
    rows = P(None, "dp", "blk", None)
    weight = P(("dp", "blk"), None)
    gain = P(("dp", "blk"))
    return jax.shard_map(
        body,
        mesh=mesh,
        in_specs=(
            rows,
            P(None, "dp"),
            gain,
            weight,
            weight,
            weight,
            weight,
            P(),
            gain,
            weight,
            weight,
            rows,
        ),
        out_specs=(rows, rows, gain, weight, weight, weight, weight, P(), gain, weight, weight),
        check_vma=False,
    )
```

```python
import functools

import jax
import jax.numpy as jnp
from jax import lax
from jax.experimental import pallas as pl
from jax.experimental.pallas import tpu as pltpu
from jax.sharding import PartitionSpec as P

EPS = 1e-06
NEG = -1e30
LIMITS = (12, 16, 23, 32, 46, 64, 91)
SUB = 128
LOG2E = 1.4426950408889634
GELU_A = 0.7978845608028654
GELU_B = 0.044715
VMEM = 62 * 2**20
NN = (((1,), (0,)), ((), ()))
NT = (((1,), (1,)), ((), ()))
TN = (((0,), (0,)), ((), ()))
low_type = jnp.bfloat16
f32 = jnp.float32


def dot(left, right, dims=NN):
    return lax.dot_general(left, right, dims, preferred_element_type=f32)


def bucket_of(relative):
    distance = jnp.abs(relative)
    far_bucket = 8 + sum(((distance >= border).astype(jnp.int32) for border in LIMITS))
    bucket = jnp.where(distance < 8, distance, far_bucket)
    return bucket + 16 * (relative > 0).astype(jnp.int32)


def norm_rows(rows):
    inverse = lax.rsqrt(jnp.mean(rows * rows, -1, keepdims=True) + EPS)
    return rows * inverse, inverse


def whole(shape):
    return pl.BlockSpec(shape, lambda *_: (0,) * len(shape), pipeline_mode=pl.Buffered(1))


def params():
    return pltpu.CompilerParams(vmem_limit_bytes=VMEM)


def struct(shape, dtype=low_type):
    return jax.ShapeDtypeStruct(shape, dtype)


SMEM = pl.BlockSpec(memory_space=pltpu.SMEM)


def tile_buckets(apart, keys_dim):
    keys = lax.broadcasted_iota(jnp.int32, (SUB, SUB), keys_dim)
    queries = lax.broadcasted_iota(jnp.int32, (SUB, SUB), 1 - keys_dim)
    return bucket_of(keys - queries + SUB * apart)


def tile_range(apart):
    return range(0 if apart <= 0 else 16, 16 if apart < 0 else 32)


def fill_tiles(near, table_ref, pair, keys_dim):
    for apart in (-1, 0, 1):
        buckets = tile_buckets(apart, keys_dim)
        masks = [(b, buckets == b) for b in tile_range(apart)]
        for h in range(2):
            tile = jnp.zeros((SUB, SUB), f32)
            for b, mask in masks:
                tile = jnp.where(mask, table_ref[2 * pair + h, b], tile)
            near[h, apart + 1] = tile


def qkv_kernel(x_ref, gain_ref, w_ref, q_ref, k_ref, v_ref):
    width = q_ref.shape[1]
    normed, _ = norm_rows(x_ref[...].astype(f32))
    low = (normed * gain_ref[...]).astype(low_type)
    q_ref[...] = (dot(low, w_ref[:, :width]) * (0.125 * LOG2E)).astype(low_type)
    k_ref[...] = dot(low, w_ref[:, width : 2 * width]).astype(low_type)
    v_ref[...] = dot(low, w_ref[:, 2 * width : 3 * width]).astype(low_type)


def qkv_call(x, gain, w_first, heads_width, rows=512):
    total, width = x.shape
    row = pl.BlockSpec((rows, width), lambda i: (i, 0))
    return pl.pallas_call(
        qkv_kernel,
        grid=(total // rows,),
        in_specs=[row, whole((1, width)), whole(w_first.shape)],
        out_specs=[pl.BlockSpec((rows, heads_width), lambda i: (i, 0))] * 3,
        out_shape=[struct((total, heads_width))] * 3,
        compiler_params=params(),
        name="qkv",
    )(x, gain, w_first)


def attend_kernel(
    len_ref, table_ref, q_ref, k_ref, v_ref, o_ref, lse_ref, near_ref, *, rows
):
    pair, doc = pl.program_id(0), pl.program_id(1)

    @pl.when(doc == 0)
    def _():
        fill_tiles(near_ref, table_ref, pair, 1)

    seq = q_ref.shape[0]
    subs = seq // SUB
    first = lax.broadcasted_iota(jnp.int32, (1, 128), 1) < 64
    live = lax.broadcasted_iota(jnp.int32, (1, seq), 1) < len_ref[doc]
    one = jnp.ones((), low_type)
    k, v = k_ref[...], v_ref[...]
    v_ones = (jnp.where(first, v, one), jnp.where(first, one, v))
    for block in range(seq // rows):
        span = slice(block * rows, (block + 1) * rows)
        q = q_ref[span, :]
        outs, tops = [], []
        for h in range(2):
            q_one = jnp.where(first == (h == 0), q, jnp.zeros((), low_type))
            raw = dot(q_one, k, NT)
            strips = []
            for a in range(rows // SUB):
                at = block * (rows // SUB) + a
                strip = raw[a * SUB : (a + 1) * SUB]
                low, high = max(at - 1, 0), min(at + 2, subs)
                parts = []
                if low > 0:
                    parts.append(strip[:, : low * SUB] + table_ref[2 * pair + h, 15])
                for b in range(low, high):
                    parts.append(strip[:, b * SUB : (b + 1) * SUB] + near_ref[h, b - at + 1])
                if high < subs:
                    parts.append(strip[:, high * SUB :] + table_ref[2 * pair + h, 31])
                strips.append(jnp.concatenate(parts, 1))
            scores = jnp.where(live, jnp.concatenate(strips, 0), NEG)
            top = jnp.max(scores, 1, keepdims=True)
            outs.append(dot(jnp.exp2(scores - top).astype(low_type), v_ones[h]))
            tops.append(top)
        total = jnp.where(first, pltpu.roll(outs[0], 64, 1), pltpu.roll(outs[1], 64, 1))
        o_ref[span, :] = (jnp.where(first, outs[0], outs[1]) / total).astype(low_type)
        log_total = (jnp.where(first, tops[0], tops[1]) + jnp.log2(total)).T
        lse_ref[0, 0, 0:1, span] = log_total[0:1]
        lse_ref[0, 0, 1:2, span] = log_total[64:65]


def attend_call(lengths, table, q, k, v, rows=512):
    docs, (total, width) = lengths.shape[0], q.shape
    seq, pairs = total // docs, width // 128
    slab = pl.BlockSpec((seq, 128), lambda p, d: (d, p))
    return pl.pallas_call(
        functools.partial(attend_kernel, rows=rows),
        grid=(pairs, docs),
        in_specs=[
            SMEM,
            SMEM,
            slab,
            slab,
            slab,
        ],
        out_specs=[slab, pl.BlockSpec((1, 1, 2, seq), lambda p, d: (d, p, 0, 0))],
        out_shape=[struct((total, width)), struct((docs, pairs, 2, seq), f32)],
        scratch_shapes=[pltpu.VMEM((2, 3, SUB, SUB), f32)],
        compiler_params=params(),
        name="attend",
    )(lengths, table, q, k, v)


def middle_kernel(
    len_ref,
    x_ref,
    heads_ref,
    cot_ref,
    gain_ref,
    w_ref,
    mixed_ref,
    hgrad_ref,
    mid_ref,
    gw_ref,
    gn_ref,
    acc,
    acc_gain,
    *,
    seq,
    chunk,
):
    step = pl.program_id(0)
    rows, width = x_ref.shape
    hidden = (w_ref.shape[1] - width) // 2

    @pl.when(step == 0)
    def _():
        acc[...] = jnp.zeros_like(acc)
        acc_gain[...] = jnp.zeros_like(acc_gain)

    per = seq // rows
    place = (step % per) * rows + lax.broadcasted_iota(jnp.int32, (rows, 1), 0)
    heads, gain = heads_ref[...], gain_ref[...]
    residual = x_ref[...].astype(f32) + dot(heads, w_ref[:, :width])
    normed, inverse = norm_rows(residual)
    low = (normed * gain).astype(low_type)
    out_grad = jnp.where(place < len_ref[step // per], cot_ref[...], jnp.zeros((), low_type))
    mixed, normed_grad = residual, jnp.zeros((rows, width), f32)
    for at in range(0, hidden, chunk):
        up = slice(width + at, width + at + chunk)
        down = slice(width + hidden + at, width + hidden + at + chunk)
        u = dot(low, w_ref[:, up])
        square = u * u
        bend = jnp.tanh(u * (GELU_A + GELU_A * GELU_B * square))
        half = 0.5 + 0.5 * bend
        act = (u * half).astype(low_type)
        slope = half + (0.5 * u) * (1 - bend * bend) * (GELU_A + 3 * GELU_A * GELU_B * square)
        up_grad = (dot(out_grad, w_ref[:, down]) * slope).astype(low_type)
        mixed = mixed + dot(act, w_ref[:, down], NT)
        normed_grad = normed_grad + dot(up_grad, w_ref[:, up], NT)
        acc[:, down] += dot(out_grad, act, TN)
        acc[:, up] += dot(low, up_grad, TN)
    mixed_ref[...] = mixed.astype(low_type)
    scaled = normed_grad * gain
    inner = jnp.mean(scaled * normed, -1, keepdims=True)
    mid = (out_grad.astype(f32) + inverse * (scaled - normed * inner)).astype(low_type)
    acc_gain[...] += jnp.sum((normed_grad * normed).reshape(rows // 8, 8, width), 0)
    mid_ref[...] = mid
    acc[:, :width] += dot(heads, mid, TN)
    hgrad_ref[...] = dot(mid, w_ref[:, :width], NT).astype(low_type)

    @pl.when(step == pl.num_programs(0) - 1)
    def _():
        gw_ref[...] = acc[...].astype(low_type)
        gn_ref[...] = jnp.sum(acc_gain[...], 0, keepdims=True)


def middle_call(lengths, x, heads, cot, gain, w_second, rows=256, chunk=1024):
    total, width = x.shape
    row = pl.BlockSpec((rows, width), lambda i: (i, 0))
    return pl.pallas_call(
        functools.partial(middle_kernel, seq=total // lengths.shape[0], chunk=chunk),
        grid=(total // rows,),
        in_specs=[SMEM, row, row, row, whole((1, width)), whole(w_second.shape)],
        out_specs=[row, row, row, whole(w_second.shape), whole((1, width))],
        out_shape=[struct((total, width))] * 3 + [struct(w_second.shape), struct((1, width), f32)],
        scratch_shapes=[pltpu.VMEM(w_second.shape, f32), pltpu.VMEM((8, width), f32)],
        compiler_params=params(),
        name="middle",
    )(lengths, x, heads, cot, gain, w_second)


def attend_back_kernel(
    len_ref,
    table_ref,
    q_ref,
    k_ref,
    v_ref,
    grad_ref,
    o_ref,
    lse_ref,
    dq_ref,
    dk_ref,
    dv_ref,
    table_sum,
    near_ref,
    near_sum,
    far_sum,
    acc,
    *,
    keys,
    queries,
):
    pair, doc = pl.program_id(0), pl.program_id(1)
    seq = q_ref.shape[0]
    first = lax.broadcasted_iota(jnp.int32, (1, 128), 1) < 64
    zero = jnp.zeros((), low_type)

    def halves(x):
        return jnp.where(first, x, zero), jnp.where(first, zero, x)

    grad = grad_ref[...]
    q_one, g_one = halves(q_ref[...]), halves(grad)
    product = grad.astype(f32) * o_ref[...].astype(f32)
    upper = product.astype(low_type)
    lower = (product - upper.astype(f32)).astype(low_type)
    row = lax.broadcasted_iota(jnp.int32, (16, 128), 0)
    column = lax.broadcasted_iota(jnp.int32, (16, 128), 1)
    member = (row == column // 64).astype(f32).astype(low_type)
    delta = dot(member, upper, NT) + dot(member, lower, NT)

    @pl.when(doc == 0)
    def _():
        fill_tiles(near_ref, table_ref, pair, 0)
        near_sum[...] = jnp.zeros_like(near_sum)
        far_sum[...] = jnp.zeros_like(far_sum)

    acc[...] = jnp.zeros_like(acc)
    for kb in range(seq // keys):
        held = slice(kb * keys, (kb + 1) * keys)
        k, v = k_ref[held, :], v_ref[held, :]
        k_one = halves(k)
        live = (kb * keys + lax.broadcasted_iota(jnp.int32, (keys, 1), 0)) < len_ref[doc]
        dk = jnp.zeros((keys, 128), f32)
        dv = jnp.zeros((keys, 128), f32)
        for qb in range(seq // queries):
            span = slice(qb * queries, (qb + 1) * queries)
            dq = None
            for h in range(2):
                scores = dot(k, q_one[h][span], NT)
                prob_grad = dot(v, g_one[h][span], NT)
                lse = lse_ref[0, 0, h : h + 1, span]
                lse_side = (lse - table_ref[2 * pair + h, 15], lse - table_ref[2 * pair + h, 31])
                row_delta = delta[h : h + 1, span]
                prob_rows, grad_rows = [], []
                for a in range(keys // SUB):
                    down = slice(a * SUB, (a + 1) * SUB)
                    probs, grads = [], []
                    for b in range(queries // SUB):
                        across = slice(b * SUB, (b + 1) * SUB)
                        apart = kb * (keys // SUB) + a - qb * (queries // SUB) - b
                        tile = scores[down, across]
                        if abs(apart) <= 1:
                            tile = tile + near_ref[h, apart + 1] - lse[:, across]
                        else:
                            tile = tile - lse_side[int(apart > 0)][:, across]
                        prob = jnp.where(live[down], jnp.exp2(tile), 0.0)
                        score_grad = prob * (prob_grad[down, across] - row_delta[:, across])
                        if abs(apart) <= 1:
                            near_sum[h, apart + 1] += score_grad
                        else:
                            far_sum[h, int(apart > 0)] += jnp.sum(
                                score_grad.reshape(SUB // 8, 8, SUB), 0
                            )
                        probs.append(prob.astype(low_type))
                        grads.append(score_grad.astype(low_type))
                    prob_rows.append(jnp.concatenate(probs, 1))
                    grad_rows.append(jnp.concatenate(grads, 1))
                prob_low = jnp.concatenate(prob_rows, 0)
                grad_low = jnp.concatenate(grad_rows, 0)
                dv = dv + dot(prob_low, g_one[h][span])
                dk = dk + dot(grad_low, q_one[h][span])
                part = dot(grad_low, k_one[h], TN)
                dq = part if dq is None else dq + part
            acc[span, :] += dq
        dv_ref[held, :] = dv.astype(low_type)
        dk_ref[held, :] = (dk * (1 / LOG2E)).astype(low_type)
    dq_ref[...] = (acc[...] * 0.125).astype(low_type)

    @pl.when(doc == pl.num_programs(1) - 1)
    def _():
        sums = {}
        for apart in (-1, 0, 1):
            buckets = tile_buckets(apart, 0)
            masks = [(b, buckets == b) for b in tile_range(apart)]
            for h in range(2):
                tile = near_sum[h, apart + 1]
                for b, mask in masks:
                    part = jnp.sum(jnp.where(mask, tile, 0.0), 0, keepdims=True)
                    sums[h, b] = sums[h, b] + part if (h, b) in sums else part
        for h in range(2):
            for side, b in enumerate((15, 31)):
                sums[h, b] = sums[h, b] + jnp.sum(far_sum[h, side], 0, keepdims=True)
            for b in range(32):
                table_sum[h, b : b + 1] = sums[h, b]


def attend_back_call(lengths, table, q, k, v, grad, o, lse, keys=256, queries=1024):
    docs, (total, width) = lengths.shape[0], q.shape
    seq, pairs = total // docs, width // 128
    queries = min(queries, seq)
    slab = pl.BlockSpec((seq, 128), lambda p, d: (d, p))
    return pl.pallas_call(
        functools.partial(attend_back_kernel, keys=keys, queries=queries),
        grid=(pairs, docs),
        in_specs=[
            SMEM,
            SMEM,
            slab,
            slab,
            slab,
            slab,
            slab,
            pl.BlockSpec((1, 1, 2, seq), lambda p, d: (d, p, 0, 0)),
        ],
        out_specs=[slab, slab, slab, pl.BlockSpec((2, 32, SUB), lambda p, d: (p, 0, 0))],
        out_shape=[struct((total, width))] * 3 + [struct((2 * pairs, 32, SUB), f32)],
        scratch_shapes=[
            pltpu.VMEM((2, 3, SUB, SUB), f32),
            pltpu.VMEM((2, 3, SUB, SUB), f32),
            pltpu.VMEM((2, 2, 8, SUB), f32),
            pltpu.VMEM((seq, 128), f32),
        ],
        compiler_params=params(),
        name="attend_back",
    )(lengths, table, q, k, v, grad, o, lse)


def last_kernel(
    x_ref,
    dq_ref,
    dk_ref,
    dv_ref,
    mid_ref,
    gain_ref,
    w_ref,
    gt_ref,
    gw_ref,
    gn_ref,
    acc,
    acc_gain,
):
    step = pl.program_id(0)
    rows, width = x_ref.shape

    @pl.when(step == 0)
    def _():
        acc[...] = jnp.zeros_like(acc)
        acc_gain[...] = jnp.zeros_like(acc_gain)

    gain = gain_ref[...]
    normed, inverse = norm_rows(x_ref[...].astype(f32))
    low = (normed * gain).astype(low_type)
    normed_grad = None
    for index, ref in enumerate((dq_ref, dk_ref, dv_ref)):
        part = slice(index * width, (index + 1) * width)
        grad = ref[...]
        acc[:, part] += dot(low, grad, TN)
        back = dot(grad, w_ref[:, part], NT)
        normed_grad = back if normed_grad is None else normed_grad + back
    acc_gain[...] += jnp.sum((normed_grad * normed).reshape(rows // 8, 8, width), 0)
    scaled = normed_grad * gain
    inner = jnp.mean(scaled * normed, -1, keepdims=True)
    gt_ref[...] = (mid_ref[...].astype(f32) + inverse * (scaled - normed * inner)).astype(low_type)

    @pl.when(step == pl.num_programs(0) - 1)
    def _():
        gw_ref[...] = acc[...].astype(low_type)
        gn_ref[...] = jnp.sum(acc_gain[...], 0, keepdims=True)


def last_call(x, dq, dk, dv, mid, gain, w_first, rows=512):
    total, width = x.shape
    row = pl.BlockSpec((rows, width), lambda i: (i, 0))
    grads = (width, 3 * width)
    return pl.pallas_call(
        last_kernel,
        grid=(total // rows,),
        in_specs=[row] * 5 + [whole((1, width)), whole(w_first.shape)],
        out_specs=[row, whole(grads), whole((1, width))],
        out_shape=[struct((total, width)), struct(grads), struct((1, width), f32)],
        scratch_shapes=[pltpu.VMEM(grads, f32), pltpu.VMEM((8, width), f32)],
        compiler_params=params(),
        name="last",
    )(x, dq, dk, dv, mid, gain, w_first)


MESH_ID = pl.DeviceIdType.MESH
ANY = pl.BlockSpec(memory_space=pl.ANY)
VMEM_WHOLE = pl.BlockSpec(memory_space=pltpu.VMEM)
DMA = pltpu.SemaphoreType.DMA
SPARE = 128


class Place:
    def __init__(self):
        self.dp, self.y = lax.axis_index("dp"), lax.axis_index("blk")
        self.depth = lax.axis_size("dp") // 4
        self.z = self.dp // 4
        self.x = lax.rem(self.dp // 2, 2)
        self.core = lax.rem(self.dp, 2)
        self.hops = sorted(range(1, self.depth), key=lambda hop: min(hop, self.depth - hop))

    def unit(self, z, x, core):
        return (z * 2 + x) * 2 + core

    def z_after(self, hop):
        return lax.rem(self.z + hop, self.depth)

    def z_before(self, hop):
        return lax.rem(self.z + self.depth - hop, self.depth)

    def along_z(self, hop):
        return (self.unit(self.z_after(hop), self.x, self.core), self.y)

    def over_x(self):
        return (self.unit(self.z, 1 - self.x, self.core), self.y)

    def over_core(self):
        return (self.unit(self.z, self.x, 1 - self.core), self.y)

    def over_y(self):
        return (self.dp, 1 - self.y)

    def greet(self):
        barrier = pltpu.get_barrier_semaphore()
        peers = [self.over_x(), self.over_core(), self.over_y()]
        peers += [self.along_z(hop) for hop in self.hops]
        for peer in peers:
            pl.semaphore_signal(barrier, device_id=peer, device_id_type=MESH_ID)
        pl.semaphore_wait(barrier, len(peers))


def remote(source, target, send, recv, device):
    return pltpu.make_async_remote_copy(
        src_ref=source,
        dst_ref=target,
        send_sem=send,
        recv_sem=recv,
        device_id=device,
        device_id_type=MESH_ID,
    )


class Gather:
    def __init__(self, place, shard, other, pair, full, sems):
        self.place, self.shard, self.other, self.pair, self.full = place, shard, other, pair, full
        self.meet_sem, self.send_sem, self.recv_sem, self.put_sem = sems
        self.rows = pair.shape[0]
        self.mine = place.unit(place.z, place.x, place.core)

    @staticmethod
    def scratch(own_rows, columns, units):
        return [
            pltpu.VMEM((own_rows + -own_rows % 16, columns), low_type),
            pltpu.VMEM((2 * own_rows, columns), low_type),
            DMA((2,)),
            DMA((units, 5)),
            DMA((units,)),
            DMA,
        ]

    def at(self, u):
        return self.full.at[pl.ds(pl.multiple_of(u * self.rows, 16), self.rows)]

    def meet(self):
        return remote(
            self.shard, self.other, self.meet_sem.at[0], self.meet_sem.at[1], self.place.over_y()
        )

    def send(self, u, kind, source=None):
        device = {"x": self.place.over_x, "core": self.place.over_core}.get(kind)
        device = device() if device else self.place.along_z(kind)
        slot = {"x": 3, "core": 4}.get(kind, None)
        slot = self.place.hops.index(kind) if slot is None else slot
        source = self.at(u) if source is None else source
        return remote(source, self.at(u), self.send_sem.at[u, slot], self.recv_sem.at[u], device)

    def put(self):
        return pltpu.make_async_copy(self.pair, self.at(self.mine), self.put_sem)

    def start(self):
        self.meet().start()

    def spread(self):
        place = self.place
        self.meet().wait()
        half = self.rows // 2
        mine = self.shard[:half].astype(f32)
        theirs = self.other[:half].astype(f32)
        first = place.y == 0
        self.pair[...] = jnp.concatenate(
            [jnp.where(first, mine, theirs), jnp.where(first, theirs, mine)], 0
        ).astype(low_type)
        self.put().start()
        for kind in place.hops + ["x", "core"]:
            self.send(self.mine, kind, self.pair).start()

    def from_z(self, hop):
        u = self.place.unit(self.place.z_before(hop), self.place.x, self.place.core)
        self.send(u, "core").wait_recv()
        self.send(u, "x").start()
        self.send(u, "core").start()

    def from_x(self, hop):
        u = self.place.unit(self.place.z_before(hop), 1 - self.place.x, self.place.core)
        self.send(u, "core").wait_recv()
        self.send(u, "core").start()

    def from_core(self):
        place = self.place
        for z in range(place.depth):
            for x in range(2):
                self.send(place.unit(z, x, 1 - place.core), "core").wait_recv()
        self.put().wait()

    def stages(self):
        out = [self.start, self.spread]
        hops = self.place.hops
        for at, hop in enumerate(hops):
            out.append(lambda hop=hop: self.from_z(hop))
            out.append(lambda hop=([0] + hops)[at]: self.from_x(hop))
        out.append(lambda: self.from_x(hops[-1]))
        out.append(self.from_core)
        return out

    def drain(self):
        place = self.place
        for kind in place.hops + ["x", "core"]:
            self.send(self.mine, kind, self.pair).wait_send()
        for hop in place.hops:
            u = place.unit(place.z_before(hop), place.x, place.core)
            self.send(u, "x").wait_send()
            self.send(u, "core").wait_send()
        for hop in [0] + place.hops:
            u = place.unit(place.z_before(hop), 1 - place.x, place.core)
            self.send(u, "core").wait_send()


class Scatter:
    def __init__(self, place, full, bufs, sems):
        self.place, self.full = place, full
        self.core_buf, self.x_send, self.x_buf, self.z_send, self.z_buf, self.y_send, self.y_buf = bufs
        self.core_sem, self.x_sem, self.z_sem, self.y_sem = sems
        self.rows = self.x_send.shape[1]
        self.order = place.hops + [0]

    @staticmethod
    def scratch(own_rows, columns, units):
        depth, unit = units // 4, (2 * own_rows, columns)
        return [
            pltpu.VMEM((2, depth) + unit, low_type),
            pltpu.VMEM((depth,) + unit, low_type),
            pltpu.VMEM((depth,) + unit, low_type),
            pltpu.VMEM((depth,) + unit, low_type),
            pltpu.VMEM((depth,) + unit, low_type),
            pltpu.VMEM((own_rows, columns), f32),
            pltpu.VMEM((own_rows, columns), f32),
            DMA((2, 2, depth)),
            DMA((2, depth)),
            DMA((2, depth)),
            DMA((2,)),
        ]

    def at(self, z, x, core):
        u = self.place.unit(z, x, core)
        return self.full.at[pl.ds(pl.multiple_of(u * self.rows, 16), self.rows)]

    def x_of(self, side):
        return self.place.x if side == 0 else 1 - self.place.x

    def to_core(self, side, hop):
        place = self.place
        return remote(
            self.at(place.z_after(hop), self.x_of(side), 1 - place.core),
            self.core_buf.at[side, hop],
            self.core_sem.at[0, side, hop],
            self.core_sem.at[1, side, hop],
            place.over_core(),
        )

    def to_x(self, hop):
        return remote(
            self.x_send.at[hop],
            self.x_buf.at[hop],
            self.x_sem.at[0, hop],
            self.x_sem.at[1, hop],
            self.place.over_x(),
        )

    def to_z(self, hop):
        return remote(
            self.z_send.at[hop],
            self.z_buf.at[hop],
            self.z_sem.at[0, hop],
            self.z_sem.at[1, hop],
            self.place.along_z(hop),
        )

    def to_y(self):
        return remote(
            self.y_send, self.y_buf, self.y_sem.at[0], self.y_sem.at[1], self.place.over_y()
        )

    def start(self):
        for side in (1, 0):
            for hop in self.order:
                self.to_core(side, hop).start()

    def mine(self, side, hop):
        place = self.place
        self.to_core(side, hop).wait_recv()
        own = self.at(place.z_after(hop), self.x_of(side), place.core)
        return own[...].astype(f32) + self.core_buf[side, hop].astype(f32)

    def stage_x(self, hop):
        self.x_send[hop] = self.mine(1, hop).astype(low_type)
        self.to_x(hop).start()

    def stage_z(self, hop):
        part = self.mine(0, hop)
        self.to_x(hop).wait_recv()
        part = part + self.x_buf[hop].astype(f32)
        self.z_send[hop] = part.astype(low_type)
        if hop:
            self.to_z(hop).start()

    def stage_y(self):
        total = self.z_send[0].astype(f32)
        for hop in self.place.hops:
            self.to_z(hop).wait_recv()
            total = total + self.z_buf[hop].astype(f32)
        half = self.rows // 2
        first = self.place.y == 0
        self.y_send[...] = jnp.where(first, total[half:], total[:half])
        self.to_y().start()
        return jnp.where(first, total[:half], total[half:])

    def finish(self, kept):
        self.to_y().wait()
        return kept + self.y_buf[...]

    def drain(self):
        for hop in self.order:
            for side in (1, 0):
                self.to_core(side, hop).wait_send()
            self.to_x(hop).wait_send()
            if hop:
                self.to_z(hop).wait_send()


class Exchange:
    def __init__(self, place, send, recv, sem):
        self.send, self.recv, self.sem = send, recv, sem
        self.targets = [place.over_core(), place.over_x(), place.over_y()]
        span = 1
        while span < place.depth:
            flip = place.z + span - 2 * span * lax.rem(place.z // span, 2)
            self.targets.append((place.unit(flip, place.x, place.core), place.y))
            span *= 2

    @staticmethod
    def rounds(units):
        return 3 + (units // 4 - 1).bit_length()

    @staticmethod
    def scratch(shape, units):
        rounds = Exchange.rounds(units)
        return [
            pltpu.VMEM((rounds,) + shape, f32),
            pltpu.VMEM((rounds,) + shape, f32),
            DMA((2, rounds)),
        ]

    def copy(self, at):
        return remote(
            self.send.at[at], self.recv.at[at], self.sem.at[0, at], self.sem.at[1, at], self.targets[at]
        )

    def start(self, at, value):
        self.send[at] = value
        self.copy(at).start()

    def finish(self, at):
        self.copy(at).wait()
        return self.send[at] + self.recv[at]


def comm_params(collective):
    return pltpu.CompilerParams(
        collective_id=collective, has_side_effects=True, vmem_limit_bytes=VMEM
    )


def first_kernel(
    shard_ref,
    tokens_ref,
    q_ref,
    k_ref,
    v_ref,
    x_ref,
    w_ref,
    gain_ref,
    w_all,
    x_in,
    stage,
    other,
    pair,
    meet_sem,
    send_sem,
    recv_sem,
    put_sem,
    swap_sem,
    load_sem,
    save_sem,
    stage_sem,
    w_sem,
):
    place = Place()
    per, seq, width = x_ref.shape
    rows = tokens_ref.shape[1]
    gather = Gather(
        place, shard_ref, other, pair, w_all, (meet_sem, send_sem, recv_sem, put_sem)
    )
    place.greet()

    def swap(doc):
        return remote(
            tokens_ref.at[(1 - place.y) * per + doc],
            x_in.at[per + doc],
            swap_sem.at[0, doc],
            swap_sem.at[1, doc],
            place.over_y(),
        )

    def load(doc):
        return pltpu.make_async_copy(
            tokens_ref.at[place.y * per + doc], x_in.at[doc], load_sem.at[doc]
        )

    def start_of(block):
        y = place.y if block < per else 1 - place.y
        return pl.multiple_of(y * rows, 16)

    def save(block):
        return pltpu.make_async_copy(
            x_in.at[block], x_ref.at[block % per, pl.ds(start_of(block), rows)], save_sem.at[block]
        )

    def store(block, index):
        target = (q_ref, k_ref, v_ref)[index]
        begin = pl.multiple_of(block % per * seq + start_of(block), 16)
        return pltpu.make_async_copy(
            stage.at[block % 2, index], target.at[pl.ds(begin, rows)], stage_sem.at[block % 2, index]
        )

    stages = gather.stages()
    stages[0]()
    for doc in range(per):
        load(doc).start()
        swap(doc).start()
    for step in stages[1:]:
        step()
    keep = pltpu.make_async_copy(w_all, w_ref, w_sem)
    keep.start()
    gains = w_all[:, 3 * width :].astype(f32).T
    gain_ref[...] = gains[: gain_ref.shape[0]]
    gain = gains[0:1]
    for block in range(2 * per):
        if block < per:
            load(block).wait()
        else:
            swap(block - per).wait_recv()
        save(block).start()
        normed, _ = norm_rows(x_in[block].astype(f32))
        low = (normed * gain).astype(low_type)
        for index in range(3):
            part = dot(low, w_all[:, index * width : (index + 1) * width])
            if index == 0:
                part = part * (0.125 * LOG2E)
            if block >= 2:
                store(block - 2, index).wait()
            stage[block % 2, index] = part.astype(low_type)
            store(block, index).start()
    for block in range(2 * per):
        save(block).wait()
        if block >= 2 * per - 2:
            for index in range(3):
                store(block, index).wait()
    keep.wait()
    gather.drain()
    for doc in range(per):
        swap(doc).wait_send()


def first_call(shard, tokens, ways):
    units = lax.axis_size("dp")
    count, rows, width = tokens.shape
    own_rows, columns = shard.shape
    per = count // ways
    padded = jnp.pad(shard, ((0, -own_rows % 16), (0, 0)))
    total = per * rows * ways
    return pl.pallas_call(
        first_kernel,
        in_specs=[VMEM_WHOLE, ANY],
        out_specs=[ANY] * 5 + [VMEM_WHOLE],
        out_shape=[struct((total, width))] * 3
        + [
            struct((per, rows * ways, width)),
            struct((units * ways * own_rows, columns)),
            struct((8, width), f32),
        ],
        scratch_shapes=[
            pltpu.VMEM((units * ways * own_rows, columns), low_type),
            pltpu.VMEM((2 * per, rows, width), low_type),
            pltpu.VMEM((2, 3, rows, width), low_type),
        ]
        + Gather.scratch(own_rows, columns, units)
        + [DMA((2, per)), DMA((per,)), DMA((2 * per,)), DMA((2, 3)), DMA],
        compiler_params=comm_params(1),
        name="first",
    )(padded, tokens)


def end_kernel(
    x_ref,
    dq_ref,
    dk_ref,
    dv_ref,
    mid_ref,
    w_ref,
    gain_ref,
    gn_second_ref,
    table_ref,
    gw_ref,
    gt_ref,
    small_ref,
    rows_in,
    acc,
    grads,
    gt,
    core_buf,
    x_send,
    x_buf,
    z_send,
    z_buf,
    y_send,
    y_buf,
    core_sem,
    x_sem,
    z_sem,
    y_sem,
    small_send,
    small_recv,
    small_sem,
    load_sem,
    gt_sem,
):
    place = Place()
    count, rows, width = gt_ref.shape
    per = count // 2
    seq = 2 * rows
    scatter = Scatter(
        place,
        grads,
        (core_buf, x_send, x_buf, z_send, z_buf, y_send, y_buf),
        (core_sem, x_sem, z_sem, y_sem),
    )
    exchange = Exchange(place, small_send, small_recv, small_sem)
    sources = (x_ref, dq_ref, dk_ref, dv_ref, mid_ref)

    def load(block, index):
        y = 1 - place.y if block < per else place.y
        begin = pl.multiple_of(block % per * seq + y * rows, 16)
        return pltpu.make_async_copy(
            sources[index].at[pl.ds(begin, rows)], rows_in.at[block, index], load_sem.at[block, index]
        )

    def give(block):
        target = gt_ref.at[place.y * per + block % per]
        if block < per:
            return remote(
                gt.at[block], target, gt_sem.at[0, block], gt_sem.at[1, block], place.over_y()
            )
        return pltpu.make_async_copy(gt.at[block], target, gt_sem.at[0, block])

    for block in range(2 * per):
        for index in range(5):
            load(block, index).start()
    place.greet()
    gain = gain_ref[0:1]
    gain_sum = []

    def normed_of(block):
        return norm_rows(rows_in[block, 0].astype(f32))

    def rows_back(block):
        normed, inverse = normed_of(block)
        normed_grad = None
        for index in range(3):
            part = dot(
                rows_in[block, 1 + index], w_ref[:, index * width : (index + 1) * width], NT
            )
            normed_grad = part if normed_grad is None else normed_grad + part
        gain_sum.append(jnp.sum((normed_grad * normed).reshape(rows // 8, 8, width), 0))
        scaled = normed_grad * gain
        inner = jnp.mean(scaled * normed, -1, keepdims=True)
        mid = rows_in[block, 4].astype(f32)
        gt[block] = (mid + inverse * (scaled - normed * inner)).astype(low_type)
        give(block).start()

    def weights_back(block, last):
        normed, _ = normed_of(block)
        low = (normed * gain).astype(low_type)
        for index in range(3):
            span = slice(index * width, (index + 1) * width)
            part = dot(low, rows_in[block, 1 + index], TN)
            if block:
                part = part + acc[:, span]
            if last:
                grads[:, span] = part.astype(low_type)
            else:
                acc[:, span] = part

    for block in range(2 * per):
        for index in range(5):
            load(block, index).wait()
        if block < per:
            rows_back(block)
        weights_back(block, block == 2 * per - 1)
    scatter.start()
    rows_back(per)
    order = scatter.order
    for hop in order[:2]:
        scatter.stage_x(hop)
    for block in range(per + 1, 2 * per):
        rows_back(block)
    for hop in order[2:]:
        scatter.stage_x(hop)
    gain_row = jnp.sum(sum(gain_sum[1:], gain_sum[0]), 0, keepdims=True)
    lines = [table_ref[...]]
    for row in (gain_row, gn_second_ref[...]):
        lines += [row[:, at : at + 128] for at in range(0, width, 128)]
    gap = small_ref.shape[0] - sum(line.shape[0] for line in lines)
    if gap:
        lines.append(jnp.zeros((gap, 128), f32))
    exchange.start(0, jnp.concatenate(lines, 0))
    rounds = len(exchange.targets)
    at = 0
    for hop in order:
        scatter.stage_z(hop)
        if at < rounds - 1:
            exchange.start(at + 1, exchange.finish(at))
            at += 1
    kept = scatter.stage_y()
    while at < rounds - 1:
        exchange.start(at + 1, exchange.finish(at))
        at += 1
    small_ref[...] = exchange.finish(at)
    gw_ref[...] = scatter.finish(kept)
    scatter.drain()
    for block in range(2 * per):
        give(block).wait()


def end_call(x, dq, dk, dv, mid, w_first, gains, gn_second, table, docs, ways):
    units = lax.axis_size("dp")
    total, width = x.shape
    own = width // (units * ways)
    rows = total // (docs * ways)
    small = (table.shape[0] + -(-2 * (width // 128) // 8) * 8, 128)
    return pl.pallas_call(
        end_kernel,
        in_specs=[ANY] * 5 + [VMEM_WHOLE] * 4,
        out_specs=[VMEM_WHOLE, ANY, VMEM_WHOLE],
        out_shape=[
            struct((own, 3 * width), f32),
            struct((docs * ways, rows, width)),
            struct(small, f32),
        ],
        scratch_shapes=[
            pltpu.VMEM((docs * ways, 5, rows, width), low_type),
            pltpu.VMEM((width, 3 * width), f32),
            pltpu.VMEM((width, 3 * width), low_type),
            pltpu.VMEM((docs * ways, rows, width), low_type),
        ]
        + Scatter.scratch(own, 3 * width, units)
        + Exchange.scratch(small, units)
        + [DMA((docs * ways, 5)), DMA((2, docs * ways))],
        compiler_params=comm_params(2),
        name="end",
    )(x, dq, dk, dv, mid, w_first, gains, gn_second, table)


def sharing(count):
    ways = lax.axis_size("blk")
    return max(1, count // ways), max(1, ways // count)


def to_documents(x):
    count, rows, width = x.shape
    ways, me = lax.axis_size("blk"), lax.axis_index("blk")
    per, share = sharing(count)
    if share > 1:
        everything = lax.all_gather(x, "blk", axis=1, tiled=True)
        return lax.dynamic_index_in_dim(everything, me // share, 0, keepdims=False)
    out = jnp.zeros((per, ways * rows, width), x.dtype)
    for hop in range(ways):
        piece = lax.dynamic_slice_in_dim(x, lax.rem(me + hop, ways) * per, per, 0)
        if hop:
            piece = lax.ppermute(piece, "blk", [(i, (i + hop) % ways) for i in range(ways)])
        source = lax.rem(me - hop + ways, ways)
        out = lax.dynamic_update_slice_in_dim(out, piece, source * rows, 1)
    return out.reshape(per * ways * rows, width)


def from_documents(y, count):
    ways, me = lax.axis_size("blk"), lax.axis_index("blk")
    per, share = sharing(count)
    width = y.shape[1]
    if share > 1:
        everything = lax.all_gather(y, "blk", axis=0, tiled=True).reshape(count, -1, width)
        rows = everything.shape[1] // ways
        return lax.dynamic_slice_in_dim(everything, me * rows, rows, 1)
    y = y.reshape(per, -1, width)
    rows = y.shape[1] // ways
    out = jnp.zeros((count, rows, width), y.dtype)
    for hop in range(ways):
        piece = lax.dynamic_slice_in_dim(y, lax.rem(me + hop, ways) * rows, rows, 1)
        if hop:
            piece = lax.ppermute(piece, "blk", [(i, (i + hop) % ways) for i in range(ways)])
        source = lax.rem(me - hop + ways, ways)
        out = lax.dynamic_update_slice_in_dim(out, piece, source * per, 0)
    return out


def among(y, share, split, concat):
    if share == 1:
        return y
    ways = lax.axis_size("blk")
    groups = [list(range(at, at + share)) for at in range(0, ways, share)]
    return lax.all_to_all(
        y, "blk", split, concat, axis_index_groups=groups, tiled=True
    )


def my_share(y, share, axis):
    if share == 1:
        return y
    size = y.shape[axis] // share
    at = lax.rem(lax.axis_index("blk"), share) * size
    return lax.dynamic_slice_in_dim(y, at, size, axis)


def body(
    tokens,
    lengths,
    norm1_gain,
    w_query,
    w_key,
    w_value,
    w_out,
    rel_table,
    norm2_gain,
    w_in,
    w_down,
    cotangent,
):
    micro, docs, rows, width = tokens.shape
    count = micro * docs
    per, share = sharing(count)
    both = ("dp", "blk")
    direct = lax.axis_size("blk") == 2 and per * 2 == count and lax.axis_size("dp") % 4 == 0
    gains = jnp.pad(jnp.stack([norm1_gain, norm2_gain], 1), ((0, 0), (0, SPARE - 2)))
    shard_first = jnp.concatenate([w_query, w_key, w_value, gains], 1)
    shard_second = jnp.concatenate([w_out, w_in, w_down], 1)
    w_second = lax.all_gather(shard_second, both, axis=0, tiled=True)
    tokens_here = tokens.reshape(count, rows, width)
    cot_here = cotangent.reshape(count, rows, width)
    if direct:
        q, k, v, x, w_first, gain_rows = first_call(shard_first, tokens_here, 2)
        x = x.reshape(-1, width)
        cot_here, x = lax.optimization_barrier((cot_here, x))
    else:
        w_first = lax.all_gather(shard_first, both, axis=0, tiled=True)
        x = to_documents(tokens_here)
        gain_rows = w_first[:, 3 * width : 3 * width + 2].astype(f32).T
    cot = to_documents(cot_here)
    gain_first, gain_second = gain_rows[:1], gain_rows[1:2]
    own = lax.dynamic_slice_in_dim(
        lengths.reshape(count), lax.axis_index("blk") // share * per, per, 0
    )
    x_rows, cot_rows = my_share(x, share, 0), my_share(cot, share, 0)
    own_rows, w_heads = own, w_first
    if share > 1:
        own_rows = own - lax.rem(lax.axis_index("blk"), share) * x_rows.shape[0]
        w_heads = jnp.concatenate(
            [my_share(w_first[:, i * width : (i + 1) * width], share, 1) for i in range(3)], 1
        )
    table = my_share((rel_table * LOG2E).T, share, 0)

    if not direct:
        q, k, v = qkv_call(x, gain_first, w_heads, width // share)
    heads, lse = attend_call(own, table, q, k, v)
    mixed, heads_grad, mid, g_second, gn_second = middle_call(
        own_rows, x_rows, among(heads, share, 0, 1), cot_rows, gain_second, w_second
    )
    mixed = from_documents(mixed, count)
    g_second = lax.psum_scatter(g_second, both, scatter_dimension=0, tiled=True).astype(f32)
    dq, dk, dv, table_sum = attend_back_call(
        own, table, q, k, v, among(heads_grad, share, 1, 0), heads, lse
    )
    dq, dk, dv = (among(grad, share, 0, 1) for grad in (dq, dk, dv))
    table_sum = jnp.sum(table_sum, 2)
    head_count, bucket_count = rel_table.shape[1], rel_table.shape[0]
    index = lax.axis_index("dp") * lax.axis_size("blk") + lax.axis_index("blk")
    own_gain = norm1_gain.shape[0]
    if direct:
        table_sum = jnp.pad(table_sum, ((0, -head_count % 8), (0, SUB - bucket_count)))
        g_first, grad_tokens, small = end_call(
            x, dq, dk, dv, mid, w_first, gain_rows, gn_second, table_sum, per, 2
        )
        grad_table = small[:head_count, :bucket_count].T
        gains = small[table_sum.shape[0] :][: 2 * (width // 128)].reshape(2, width)
        gains = lax.dynamic_slice_in_dim(gains, index * own_gain, own_gain, 1)
    else:
        grad_tokens, g_first, gn_first = last_call(
            x_rows, dq, dk, dv, mid, gain_first, w_first
        )
        grad_tokens = from_documents(grad_tokens, count)
        g_first = lax.psum_scatter(g_first, both, scatter_dimension=0, tiled=True).astype(f32)
        gains = lax.psum_scatter(
            jnp.concatenate([gn_first, gn_second], 0), both, scatter_dimension=1, tiled=True
        )
        if share > 1:
            at = lax.rem(lax.axis_index("blk"), share) * table_sum.shape[0]
            table_sum = lax.dynamic_update_slice_in_dim(
                jnp.zeros(rel_table.T.shape, f32), table_sum, at, 0
            )
        grad_table = lax.psum(table_sum, both).T
    grad_query, grad_key, grad_value = (
        g_first[:, i * width : (i + 1) * width] for i in range(3)
    )
    hidden = w_in.shape[1]
    return (
        mixed.reshape(tokens.shape),
        grad_tokens.reshape(tokens.shape),
        gains[0],
        grad_query,
        grad_key,
        grad_value,
        g_second[:, :width],
        grad_table,
        gains[1],
        g_second[:, width : width + hidden],
        g_second[:, width + hidden :],
    )


def solution(mesh):
    rows = P(None, "dp", "blk", None)
    weight = P(("dp", "blk"), None)
    gain = P(("dp", "blk"))
    return jax.shard_map(
        body,
        mesh=mesh,
        in_specs=(
            rows,
            P(None, "dp"),
            gain,
            weight,
            weight,
            weight,
            weight,
            P(),
            gain,
            weight,
            weight,
            rows,
        ),
        out_specs=(rows, rows, gain, weight, weight, weight, weight, P(), gain, weight, weight),
        check_vma=False,
    )
```

```python
import functools

import jax
import jax.numpy as jnp
from jax import lax
from jax.experimental import pallas as pl
from jax.experimental.pallas import tpu as pltpu
from jax.sharding import PartitionSpec as P

EPS = 1e-06
NEG = -1e30
LIMITS = (12, 16, 23, 32, 46, 64, 91)
SUB = 128
LOG2E = 1.4426950408889634
GELU_A = 0.7978845608028654
GELU_B = 0.044715
VMEM = 62 * 2**20
NN = (((1,), (0,)), ((), ()))
NT = (((1,), (1,)), ((), ()))
TN = (((0,), (0,)), ((), ()))
low_type = jnp.bfloat16
f32 = jnp.float32


def dot(left, right, dims=NN):
    return lax.dot_general(left, right, dims, preferred_element_type=f32)


def bucket_of(relative):
    distance = jnp.abs(relative)
    far_bucket = 8 + sum(((distance >= border).astype(jnp.int32) for border in LIMITS))
    bucket = jnp.where(distance < 8, distance, far_bucket)
    return bucket + 16 * (relative > 0).astype(jnp.int32)


def norm_rows(rows):
    inverse = lax.rsqrt(jnp.mean(rows * rows, -1, keepdims=True) + EPS)
    return rows * inverse, inverse


def whole(shape):
    return pl.BlockSpec(shape, lambda *_: (0,) * len(shape), pipeline_mode=pl.Buffered(1))


def params():
    return pltpu.CompilerParams(vmem_limit_bytes=VMEM)


def struct(shape, dtype=low_type):
    return jax.ShapeDtypeStruct(shape, dtype)


SMEM = pl.BlockSpec(memory_space=pltpu.SMEM)


def tile_buckets(apart, keys_dim):
    keys = lax.broadcasted_iota(jnp.int32, (SUB, SUB), keys_dim)
    queries = lax.broadcasted_iota(jnp.int32, (SUB, SUB), 1 - keys_dim)
    return bucket_of(keys - queries + SUB * apart)


def tile_range(apart):
    return range(0 if apart <= 0 else 16, 16 if apart < 0 else 32)


def fill_tiles(near, table_ref, pair, keys_dim):
    for apart in (-1, 0, 1):
        buckets = tile_buckets(apart, keys_dim)
        masks = [(b, buckets == b) for b in tile_range(apart)]
        for h in range(2):
            tile = jnp.zeros((SUB, SUB), f32)
            for b, mask in masks:
                tile = jnp.where(mask, table_ref[2 * pair + h, b], tile)
            near[h, apart + 1] = tile


def qkv_kernel(x_ref, gain_ref, w_ref, q_ref, k_ref, v_ref):
    width = q_ref.shape[1]
    normed, _ = norm_rows(x_ref[...].astype(f32))
    low = (normed * gain_ref[...]).astype(low_type)
    q_ref[...] = (dot(low, w_ref[:, :width]) * (0.125 * LOG2E)).astype(low_type)
    k_ref[...] = dot(low, w_ref[:, width : 2 * width]).astype(low_type)
    v_ref[...] = dot(low, w_ref[:, 2 * width : 3 * width]).astype(low_type)


def qkv_call(x, gain, w_first, heads_width, rows=512):
    total, width = x.shape
    row = pl.BlockSpec((rows, width), lambda i: (i, 0))
    return pl.pallas_call(
        qkv_kernel,
        grid=(total // rows,),
        in_specs=[row, whole((1, width)), whole(w_first.shape)],
        out_specs=[pl.BlockSpec((rows, heads_width), lambda i: (i, 0))] * 3,
        out_shape=[struct((total, heads_width))] * 3,
        compiler_params=params(),
        name="qkv",
    )(x, gain, w_first)


def attend_kernel(
    len_ref, table_ref, q_ref, k_ref, v_ref, o_ref, lse_ref, near_ref, *, rows
):
    pair, doc = pl.program_id(0), pl.program_id(1)

    @pl.when(doc == 0)
    def _():
        fill_tiles(near_ref, table_ref, pair, 1)

    seq = q_ref.shape[0]
    subs = seq // SUB
    first = lax.broadcasted_iota(jnp.int32, (1, 128), 1) < 64
    live = lax.broadcasted_iota(jnp.int32, (1, seq), 1) < len_ref[doc]
    one = jnp.ones((), low_type)
    k, v = k_ref[...], v_ref[...]
    v_ones = (jnp.where(first, v, one), jnp.where(first, one, v))
    for block in range(seq // rows):
        span = slice(block * rows, (block + 1) * rows)
        q = q_ref[span, :]
        outs, tops = [], []
        for h in range(2):
            q_one = jnp.where(first == (h == 0), q, jnp.zeros((), low_type))
            raw = dot(q_one, k, NT)
            strips = []
            for a in range(rows // SUB):
                at = block * (rows // SUB) + a
                strip = raw[a * SUB : (a + 1) * SUB]
                low, high = max(at - 1, 0), min(at + 2, subs)
                parts = []
                if low > 0:
                    parts.append(strip[:, : low * SUB] + table_ref[2 * pair + h, 15])
                for b in range(low, high):
                    parts.append(strip[:, b * SUB : (b + 1) * SUB] + near_ref[h, b - at + 1])
                if high < subs:
                    parts.append(strip[:, high * SUB :] + table_ref[2 * pair + h, 31])
                strips.append(jnp.concatenate(parts, 1))
            scores = jnp.where(live, jnp.concatenate(strips, 0), NEG)
            top = jnp.max(scores, 1, keepdims=True)
            outs.append(dot(jnp.exp2(scores - top).astype(low_type), v_ones[h]))
            tops.append(top)
        total = jnp.where(first, pltpu.roll(outs[0], 64, 1), pltpu.roll(outs[1], 64, 1))
        o_ref[span, :] = (jnp.where(first, outs[0], outs[1]) / total).astype(low_type)
        log_total = (jnp.where(first, tops[0], tops[1]) + jnp.log2(total)).T
        lse_ref[0, 0, 0:1, span] = log_total[0:1]
        lse_ref[0, 0, 1:2, span] = log_total[64:65]


def attend_call(lengths, table, q, k, v, rows=512):
    docs, (total, width) = lengths.shape[0], q.shape
    seq, pairs = total // docs, width // 128
    slab = pl.BlockSpec((seq, 128), lambda p, d: (d, p))
    return pl.pallas_call(
        functools.partial(attend_kernel, rows=rows),
        grid=(pairs, docs),
        in_specs=[
            SMEM,
            SMEM,
            slab,
            slab,
            slab,
        ],
        out_specs=[slab, pl.BlockSpec((1, 1, 2, seq), lambda p, d: (d, p, 0, 0))],
        out_shape=[struct((total, width)), struct((docs, pairs, 2, seq), f32)],
        scratch_shapes=[pltpu.VMEM((2, 3, SUB, SUB), f32)],
        compiler_params=params(),
        name="attend",
    )(lengths, table, q, k, v)


CHUNKS = 4
AHEAD = 2


def second_pieces(w_out, w_in, w_down):
    chunk = w_in.shape[1] // CHUNKS
    parts = [w_out]
    for at in range(0, CHUNKS * chunk, chunk):
        parts += [w_in[:, at : at + chunk], w_down[:, at : at + chunk]]
    return jnp.concatenate(parts, 1)


def split_hidden(grads):
    chunk = grads.shape[1] // (2 * CHUNKS)
    parts = [grads[:, at * chunk : (at + 1) * chunk] for at in range(2 * CHUNKS)]
    return jnp.concatenate(parts[0::2], 1), jnp.concatenate(parts[1::2], 1)


def middle_kernel(
    len_ref,
    x_ref,
    heads_ref,
    cot_ref,
    gain_ref,
    w_out,
    w_hbm,
    mixed_ref,
    hgrad_ref,
    mid_ref,
    g_out,
    g_ref,
    gn_ref,
    scratch,
    *,
    seq,
    before_chunk,
):
    low_all, grad_all, normed_all, inverse_all, mixed_all, back_all = scratch[:6]
    act_all, up_all, g_buf, acc_gain, g_sem, w_all, w_sem = scratch[6:]
    step = pl.program_id(0)
    rows, width = x_ref.shape
    total = low_all.shape[0]
    chunk = w_all.shape[1] // (2 * CHUNKS)
    fine, block = total // rows, MIDDLE_BLOCK
    coarse = total // block
    begin = fine
    finish = fine + CHUNKS * coarse

    @pl.when(step < begin)
    def _():
        span = pl.ds(pl.multiple_of(step * rows, rows), rows)
        per = seq // rows
        place = lax.rem(step, per) * rows + lax.broadcasted_iota(jnp.int32, (rows, 1), 0)
        residual = x_ref[...].astype(f32) + dot(heads_ref[...], w_out[...])
        normed, inverse = norm_rows(residual)
        mixed_all[span, :] = residual
        back_all[span, :] = jnp.zeros_like(residual)
        normed_all[span, :] = normed.astype(low_type)
        inverse_all[span, :] = jnp.broadcast_to(inverse, (rows, 128))
        low_all[span, :] = (normed * gain_ref[...]).astype(low_type)
        grad_all[span, :] = jnp.where(
            place < len_ref[jnp.minimum(step // per, len_ref.shape[0] - 1)],
            cot_ref[...],
            jnp.zeros((), low_type),
        )

    def store(at):
        begins = pl.multiple_of(at * (2 * chunk), 128)
        slot = lax.rem(at, 2)
        return pltpu.make_async_copy(
            g_buf.at[slot], g_ref.at[:, pl.ds(begins, 2 * chunk)], g_sem.at[slot]
        )

    ready = w_hbm.shape[1] - width
    take = pltpu.make_async_copy(w_hbm.at[:, width:], w_all.at[:, :ready], w_sem)

    @pl.when(step == 0)
    def _():
        take.start()

    at = jnp.maximum(step - begin, 0) // coarse

    @pl.when(step == begin)
    def _():
        take.wait()

    for index in range(CHUNKS):

        @pl.when(step == begin + index * coarse)
        def _(index=index):
            before_chunk(index)

    @pl.when((step >= begin) & (step < finish))
    def _():
        span = pl.ds(pl.multiple_of((step - begin - at * coarse) * block, block), block)
        w_up = w_all[:, pl.ds(pl.multiple_of(at * (2 * chunk), 128), chunk)]
        w_down = w_all[:, pl.ds(pl.multiple_of(at * (2 * chunk) + chunk, 128), chunk)]
        u = dot(low_all[span, :], w_up)
        square = u * u
        bend = jnp.tanh(u * (GELU_A + GELU_A * GELU_B * square))
        half = 0.5 + 0.5 * bend
        act = (u * half).astype(low_type)
        slope = half + (0.5 * u) * (1 - bend * bend) * (GELU_A + 3 * GELU_A * GELU_B * square)
        up_grad = (dot(grad_all[span, :], w_down) * slope).astype(low_type)
        act_all[span, :] = act
        up_all[span, :] = up_grad
        mixed_all[span, :] += dot(act, w_down, NT)
        back_all[span, :] += dot(up_grad, w_up, NT)

    @pl.when((step >= begin) & (step < finish) & (step - begin == at * coarse + coarse - 1))
    def _():
        slot = lax.rem(at, 2)

        @pl.when(at >= 2)
        def _():
            store(at - 2).wait()

        g_buf[slot, :, :chunk] = dot(low_all[...], up_all[...], TN).astype(low_type)
        g_buf[slot, :, chunk:] = dot(grad_all[...], act_all[...], TN).astype(low_type)
        store(at).start()

    @pl.when(step >= finish)
    def _():
        span = pl.ds(pl.multiple_of((step - finish) * rows, rows), rows)
        mixed_ref[...] = mixed_all[span, :].astype(low_type)
        normed, back = normed_all[span, :].astype(f32), back_all[span, :]
        scaled = back * gain_ref[...]
        inner = jnp.mean(scaled * normed, -1, keepdims=True)
        inverse = inverse_all[span, :][:, :1]
        mid = grad_all[span, :].astype(f32) + inverse * (scaled - normed * inner)
        mid = mid.astype(low_type)
        part = jnp.sum((back * normed).reshape(rows // 8, 8, width), 0)
        acc_gain[...] = jnp.where(step == finish, part, acc_gain[...] + part)
        mid_ref[...] = mid
        act_all[span, :width] = mid
        up_all[span, :width] = heads_ref[...]
        hgrad_ref[...] = dot(mid, w_out[...], NT).astype(low_type)

    @pl.when(step == pl.num_programs(0) - 1)
    def _():
        g_out[...] = dot(up_all[:, :width], act_all[:, :width], TN).astype(low_type)
        gn_ref[...] = jnp.sum(acc_gain[...], 0, keepdims=True)
        for at in range(CHUNKS - 2, CHUNKS):
            store(at).wait()


MIDDLE_BLOCK = 512


def middle_plain_kernel(*refs, seq):
    w_ref, w_hbm, rest = refs[5], refs[6], refs[7:]
    middle_kernel(
        *refs[:5],
        w_ref,
        w_hbm,
        *rest[:6],
        rest[6:],
        seq=seq,
        before_chunk=lambda at: None,
    )


def middle_send_kernel(*refs, seq):
    w_ref, w_hbm, pair_ref, rest = refs[5], refs[6], refs[7], refs[8:]
    w_all, sems = rest[17], rest[19:]
    place = Place()
    ahead = w_hbm.shape[1]
    late = w_all.at[:, ahead - refs[1].shape[1] :]
    gathers = gather_parts(place, pair_ref.at[:, ahead:], late, sems)
    stages = [gather.stages() for gather in gathers]
    planned = {(part, index) for _, part, index in MIDDLE_PLAN}
    step = pl.program_id(0)

    @pl.when(step == 0)
    def _():
        place.greet()

    for when, part, index in MIDDLE_PLAN:

        @pl.when(step == when)
        def _(part=part, index=index):
            stages[part][index]()

    def before_chunk(at):
        part = (at - AHEAD) * PARTS // (CHUNKS - AHEAD)
        if at >= AHEAD and part * (CHUNKS - AHEAD) == (at - AHEAD) * PARTS:
            for index in range(len(stages[part])):
                if (part, index) not in planned:
                    stages[part][index]()

    middle_kernel(
        *refs[:5],
        w_ref,
        w_hbm,
        *rest[:6],
        rest[6:19],
        seq=seq,
        before_chunk=before_chunk,
    )

    @pl.when(step == pl.num_programs(0) - 1)
    def _():
        for gather in gathers:
            gather.drain()


MIDDLE_PLAN = (
    (0, 0, 0), (4, 1, 0), (5, 0, 1), (6, 1, 1), (7, 0, 2), (8, 1, 2),
    (9, 0, 3), (10, 1, 3), (11, 0, 4), (13, 1, 4),
)


def middle_call(lengths, x, heads, cot, gain, w_second, pair=None, rows=512):
    total, width = x.shape
    columns = w_second.shape[1] if pair is None else pair.shape[1]
    chunk = (columns - width) // (2 * CHUNKS)
    fine = total // rows
    steps = 2 * fine + CHUNKS * (total // MIDDLE_BLOCK)
    early = pl.BlockSpec((rows, width), lambda i: (jnp.minimum(i, fine - 1), 0))
    late = pl.BlockSpec((rows, width), lambda i: (jnp.maximum(i - (steps - fine), 0), 0))
    ends = pl.BlockSpec(
        (rows, width),
        lambda i: (jnp.where(i < steps - fine, jnp.minimum(i, fine - 1), i - (steps - fine)), 0),
    )
    square = (width, 2 * chunk)
    scratch = [
        pltpu.VMEM((total, width), low_type),
        pltpu.VMEM((total, width), low_type),
        pltpu.VMEM((total, width), low_type),
        pltpu.VMEM((total, 128), f32),
        pltpu.VMEM((total, width), f32),
        pltpu.VMEM((total, width), f32),
        pltpu.VMEM((total, max(chunk, width)), low_type),
        pltpu.VMEM((total, max(chunk, width)), low_type),
        pltpu.VMEM((2,) + square, low_type),
        pltpu.VMEM((8, width), f32),
        DMA((2,)),
        pltpu.VMEM((width, columns - width), low_type),
        DMA,
    ]
    kernel, compiler, operands = middle_plain_kernel, params(), []
    if pair is not None:
        kernel, compiler, operands = middle_send_kernel, comm_params(5), [pair]
        scratch += PARTS * Gather.scratch(lax.axis_size("dp"))
    square_out = (width, width)
    first_block = pl.BlockSpec(
        square_out, lambda i: (0, 0), pipeline_mode=pl.Buffered(1)
    )
    return pl.pallas_call(
        functools.partial(kernel, seq=total // lengths.shape[0]),
        grid=(steps,),
        in_specs=[SMEM, early, ends, early, whole((1, width)), first_block, ANY]
        + [whole(operand.shape) for operand in operands],
        out_specs=[late, late, late, whole(square_out), ANY, whole((1, width))],
        out_shape=[struct((total, width))] * 3
        + [
            struct(square_out),
            struct((width, CHUNKS * 2 * chunk)),
            struct((1, width), f32),
        ],
        scratch_shapes=scratch,
        compiler_params=compiler,
        name="middle",
    )(lengths, x, heads, cot, gain, w_second, w_second, *operands)


def attend_back_kernel(
    len_ref,
    table_ref,
    q_ref,
    k_ref,
    v_ref,
    grad_ref,
    o_ref,
    lse_ref,
    dq_ref,
    dk_ref,
    dv_ref,
    table_sum,
    near_ref,
    near_sum,
    far_sum,
    acc,
    *,
    keys,
    queries,
):
    pair, doc = pl.program_id(0), pl.program_id(1)
    seq = q_ref.shape[0]
    first = lax.broadcasted_iota(jnp.int32, (1, 128), 1) < 64
    zero = jnp.zeros((), low_type)

    def halves(x):
        return jnp.where(first, x, zero), jnp.where(first, zero, x)

    grad = grad_ref[...]
    q_one, g_one = halves(q_ref[...]), halves(grad)
    product = grad.astype(f32) * o_ref[...].astype(f32)
    upper = product.astype(low_type)
    lower = (product - upper.astype(f32)).astype(low_type)
    row = lax.broadcasted_iota(jnp.int32, (16, 128), 0)
    column = lax.broadcasted_iota(jnp.int32, (16, 128), 1)
    member = (row == column // 64).astype(f32).astype(low_type)
    delta = dot(member, upper, NT) + dot(member, lower, NT)

    @pl.when(doc == 0)
    def _():
        fill_tiles(near_ref, table_ref, pair, 0)
        near_sum[...] = jnp.zeros_like(near_sum)
        far_sum[...] = jnp.zeros_like(far_sum)

    acc[...] = jnp.zeros_like(acc)
    for kb in range(seq // keys):
        held = slice(kb * keys, (kb + 1) * keys)
        k, v = k_ref[held, :], v_ref[held, :]
        k_one = halves(k)
        live = (kb * keys + lax.broadcasted_iota(jnp.int32, (keys, 1), 0)) < len_ref[doc]
        dk = jnp.zeros((keys, 128), f32)
        dv = jnp.zeros((keys, 128), f32)
        for qb in range(seq // queries):
            span = slice(qb * queries, (qb + 1) * queries)
            dq = None
            for h in range(2):
                scores = dot(k, q_one[h][span], NT)
                prob_grad = dot(v, g_one[h][span], NT)
                lse = lse_ref[0, 0, h : h + 1, span]
                lse_side = (lse - table_ref[2 * pair + h, 15], lse - table_ref[2 * pair + h, 31])
                row_delta = delta[h : h + 1, span]
                prob_rows, grad_rows = [], []
                for a in range(keys // SUB):
                    down = slice(a * SUB, (a + 1) * SUB)
                    probs, grads = [], []
                    for b in range(queries // SUB):
                        across = slice(b * SUB, (b + 1) * SUB)
                        apart = kb * (keys // SUB) + a - qb * (queries // SUB) - b
                        tile = scores[down, across]
                        if abs(apart) <= 1:
                            tile = tile + near_ref[h, apart + 1] - lse[:, across]
                        else:
                            tile = tile - lse_side[int(apart > 0)][:, across]
                        prob = jnp.where(live[down], jnp.exp2(tile), 0.0)
                        score_grad = prob * (prob_grad[down, across] - row_delta[:, across])
                        if abs(apart) <= 1:
                            near_sum[h, apart + 1] += score_grad
                        else:
                            far_sum[h, int(apart > 0)] += jnp.sum(
                                score_grad.reshape(SUB // 8, 8, SUB), 0
                            )
                        probs.append(prob.astype(low_type))
                        grads.append(score_grad.astype(low_type))
                    prob_rows.append(jnp.concatenate(probs, 1))
                    grad_rows.append(jnp.concatenate(grads, 1))
                prob_low = jnp.concatenate(prob_rows, 0)
                grad_low = jnp.concatenate(grad_rows, 0)
                dv = dv + dot(prob_low, g_one[h][span])
                dk = dk + dot(grad_low, q_one[h][span])
                part = dot(grad_low, k_one[h], TN)
                dq = part if dq is None else dq + part
            acc[span, :] += dq
        dv_ref[held, :] = dv.astype(low_type)
        dk_ref[held, :] = (dk * (1 / LOG2E)).astype(low_type)
    dq_ref[...] = (acc[...] * 0.125).astype(low_type)

    @pl.when(doc == pl.num_programs(1) - 1)
    def _():
        sums = {}
        for apart in (-1, 0, 1):
            buckets = tile_buckets(apart, 0)
            masks = [(b, buckets == b) for b in tile_range(apart)]
            for h in range(2):
                tile = near_sum[h, apart + 1]
                for b, mask in masks:
                    part = jnp.sum(jnp.where(mask, tile, 0.0), 0, keepdims=True)
                    sums[h, b] = sums[h, b] + part if (h, b) in sums else part
        for h in range(2):
            for side, b in enumerate((15, 31)):
                sums[h, b] = sums[h, b] + jnp.sum(far_sum[h, side], 0, keepdims=True)
            for b in range(32):
                table_sum[h, b : b + 1] = sums[h, b]


def attend_back_call(lengths, table, q, k, v, grad, o, lse, keys=256, queries=1024):
    docs, (total, width) = lengths.shape[0], q.shape
    seq, pairs = total // docs, width // 128
    queries = min(queries, seq)
    slab = pl.BlockSpec((seq, 128), lambda p, d: (d, p))
    return pl.pallas_call(
        functools.partial(attend_back_kernel, keys=keys, queries=queries),
        grid=(pairs, docs),
        in_specs=[
            SMEM,
            SMEM,
            slab,
            slab,
            slab,
            slab,
            slab,
            pl.BlockSpec((1, 1, 2, seq), lambda p, d: (d, p, 0, 0)),
        ],
        out_specs=[slab, slab, slab, pl.BlockSpec((2, 32, SUB), lambda p, d: (p, 0, 0))],
        out_shape=[struct((total, width))] * 3 + [struct((2 * pairs, 32, SUB), f32)],
        scratch_shapes=[
            pltpu.VMEM((2, 3, SUB, SUB), f32),
            pltpu.VMEM((2, 3, SUB, SUB), f32),
            pltpu.VMEM((2, 2, 8, SUB), f32),
            pltpu.VMEM((seq, 128), f32),
        ],
        compiler_params=params(),
        name="attend_back",
    )(lengths, table, q, k, v, grad, o, lse)


def last_kernel(
    x_ref,
    dq_ref,
    dk_ref,
    dv_ref,
    mid_ref,
    gain_ref,
    w_ref,
    gt_ref,
    gw_ref,
    gn_ref,
    acc,
    acc_gain,
):
    step = pl.program_id(0)
    rows, width = x_ref.shape

    @pl.when(step == 0)
    def _():
        acc[...] = jnp.zeros_like(acc)
        acc_gain[...] = jnp.zeros_like(acc_gain)

    gain = gain_ref[...]
    normed, inverse = norm_rows(x_ref[...].astype(f32))
    low = (normed * gain).astype(low_type)
    normed_grad = None
    for index, ref in enumerate((dq_ref, dk_ref, dv_ref)):
        part = slice(index * width, (index + 1) * width)
        grad = ref[...]
        acc[:, part] += dot(low, grad, TN)
        back = dot(grad, w_ref[:, part], NT)
        normed_grad = back if normed_grad is None else normed_grad + back
    acc_gain[...] += jnp.sum((normed_grad * normed).reshape(rows // 8, 8, width), 0)
    scaled = normed_grad * gain
    inner = jnp.mean(scaled * normed, -1, keepdims=True)
    gt_ref[...] = (mid_ref[...].astype(f32) + inverse * (scaled - normed * inner)).astype(low_type)

    @pl.when(step == pl.num_programs(0) - 1)
    def _():
        gw_ref[...] = acc[...].astype(low_type)
        gn_ref[...] = jnp.sum(acc_gain[...], 0, keepdims=True)


def last_call(x, dq, dk, dv, mid, gain, w_first, rows=512):
    total, width = x.shape
    row = pl.BlockSpec((rows, width), lambda i: (i, 0))
    grads = (width, 3 * width)
    return pl.pallas_call(
        last_kernel,
        grid=(total // rows,),
        in_specs=[row] * 5 + [whole((1, width)), whole(w_first.shape)],
        out_specs=[row, whole(grads), whole((1, width))],
        out_shape=[struct((total, width)), struct(grads), struct((1, width), f32)],
        scratch_shapes=[pltpu.VMEM(grads, f32), pltpu.VMEM((8, width), f32)],
        compiler_params=params(),
        name="last",
    )(x, dq, dk, dv, mid, gain, w_first)


MESH_ID = pl.DeviceIdType.MESH
ANY = pl.BlockSpec(memory_space=pl.ANY)
VMEM_WHOLE = pl.BlockSpec(memory_space=pltpu.VMEM)
DMA = pltpu.SemaphoreType.DMA
SPARE = 128


class Place:
    def __init__(self):
        self.dp, self.y = lax.axis_index("dp"), lax.axis_index("blk")
        self.depth = lax.axis_size("dp") // 4
        self.z = self.dp // 4
        self.x = lax.rem(self.dp // 2, 2)
        self.core = lax.rem(self.dp, 2)
        self.hops = sorted(range(1, self.depth), key=lambda hop: min(hop, self.depth - hop))

    def unit(self, z, x, core):
        return (z * 2 + x) * 2 + core

    def z_after(self, hop):
        return lax.rem(self.z + hop, self.depth)

    def z_before(self, hop):
        return lax.rem(self.z + self.depth - hop, self.depth)

    def along_z(self, hop):
        return (self.unit(self.z_after(hop), self.x, self.core), self.y)

    def over_x(self):
        return (self.unit(self.z, 1 - self.x, self.core), self.y)

    def over_core(self):
        return (self.unit(self.z, self.x, 1 - self.core), self.y)

    def over_y(self):
        return (self.dp, 1 - self.y)

    def greet(self):
        barrier = pltpu.get_barrier_semaphore()
        peers = [self.over_x(), self.over_core(), self.over_y()]
        peers += [self.along_z(hop) for hop in self.hops]
        for peer in peers:
            pl.semaphore_signal(barrier, device_id=peer, device_id_type=MESH_ID)
        pl.semaphore_wait(barrier, len(peers))


def remote(source, target, send, recv, device):
    return pltpu.make_async_remote_copy(
        src_ref=source,
        dst_ref=target,
        send_sem=send,
        recv_sem=recv,
        device_id=device,
        device_id_type=MESH_ID,
    )


class Meet:
    def __init__(self, place, shard, other, sem):
        self.place, self.shard, self.other, self.sem = place, shard, other, sem

    @staticmethod
    def scratch(own_rows, columns):
        block = (own_rows + -own_rows % 16, columns)
        return [pltpu.VMEM(block, low_type), pltpu.VMEM(block, low_type), DMA((2,))]

    def copy(self):
        return remote(self.shard, self.other, self.sem.at[0], self.sem.at[1], self.place.over_y())

    def start(self, parts):
        at = 0
        for ref in parts:
            rows, columns = ref.shape
            self.shard[:rows, at : at + columns] = ref[...]
            at += columns
        self.copy().start()

    def finish(self, pair):
        self.copy().wait()
        half = pair.shape[0] // 2
        mine = self.shard[:half].astype(f32)
        theirs = self.other[:half].astype(f32)
        first = self.place.y == 0
        pair[...] = jnp.concatenate(
            [jnp.where(first, mine, theirs), jnp.where(first, theirs, mine)], 0
        ).astype(low_type)


class Gather:
    def __init__(self, place, pair, full, sems):
        self.place, self.pair, self.full = place, pair, full
        self.send_sem, self.recv_sem, self.put_sem = sems
        self.rows = pair.shape[0]
        self.mine = place.unit(place.z, place.x, place.core)
        self.has_left, self.has_right = place.z > 0, place.z < place.depth - 1

    @staticmethod
    def scratch(units):
        return [DMA((units, 4)), DMA((units,)), DMA]

    def at(self, u):
        return self.full.at[pl.ds(pl.multiple_of(u * self.rows, 16), self.rows)]

    def send(self, u, kind, source=None):
        place = self.place
        device = {
            "left": (place.dp - 4, place.y),
            "right": (place.dp + 4, place.y),
            "x": place.over_x(),
            "core": place.over_core(),
        }[kind]
        slot = ("left", "right", "x", "core").index(kind)
        source = self.at(u) if source is None else source
        return remote(source, self.at(u), self.send_sem.at[u, slot], self.recv_sem.at[u], device)

    def put(self):
        return pltpu.make_async_copy(self.pair, self.at(self.mine), self.put_sem)

    def spread(self):
        for kind, there in (("right", self.has_right), ("left", self.has_left)):

            @pl.when(there)
            def _(kind=kind):
                self.send(self.mine, kind, self.pair).start()

        self.send(self.mine, "x", self.pair).start()
        self.send(self.mine, "core", self.pair).start()
        self.put().start()

    def from_z(self, hop):
        place = self.place
        for kind, z, onward in (
            ("right", place.z - hop, self.has_right),
            ("left", place.z + hop, self.has_left),
        ):

            @pl.when((z >= 0) & (z < place.depth))
            def _(kind=kind, z=z, onward=onward):
                u = place.unit(z, place.x, place.core)
                self.send(u, "core").wait_recv()

                @pl.when(onward)
                def _():
                    self.send(u, kind).start()

                self.send(u, "x").start()
                self.send(u, "core").start()

    def from_x(self, hop):
        place = self.place
        for z in (place.z - hop, place.z + hop)[: 1 + min(hop, 1)]:

            @pl.when((z >= 0) & (z < place.depth))
            def _(z=z):
                u = place.unit(z, 1 - place.x, place.core)
                self.send(u, "core").wait_recv()
                self.send(u, "core").start()

    def from_core(self):
        place = self.place
        for z in range(place.depth):
            for x in range(2):
                self.send(place.unit(z, x, 1 - place.core), "core").wait_recv()
        self.put().wait()

    def stages(self):
        def at_hop(hop):
            if hop < self.place.depth:
                self.from_z(hop)
            self.from_x(hop - 1)

        out = [self.spread]
        out += [lambda hop=hop: at_hop(hop) for hop in range(1, self.place.depth + 1)]
        return out + [self.from_core]

    def drain(self):
        place = self.place
        for z in range(place.depth):
            u = place.unit(z, place.x, place.core)
            self.send(u, "x").wait_send()
            self.send(u, "core").wait_send()

            @pl.when((place.z >= z) & self.has_right)
            def _(u=u):
                self.send(u, "right").wait_send()

            @pl.when((place.z <= z) & self.has_left)
            def _(u=u):
                self.send(u, "left").wait_send()

            self.send(place.unit(z, 1 - place.x, place.core), "core").wait_send()


PARTS = 2


def gather_parts(place, pair, full, sems):
    size = full.shape[1] // PARTS
    out = []
    for at in range(PARTS):
        span = slice(at * size, (at + 1) * size)
        out.append(Gather(place, pair.at[:, span], full.at[:, span], sems[3 * at : 3 * at + 3]))
    return out


class Scatter:
    def __init__(self, place, full, scratch, source=None):
        self.place, self.full = place, full
        self.source = full if source is None else source
        self.core_buf, self.x_send, self.x_buf, self.z_send, self.z_buf = scratch[:5]
        self.y_send, self.y_buf = scratch[5:7]
        self.core_sem, self.x_sem, self.z_sem, self.y_sem = scratch[7:]
        self.rows = self.x_send.shape[1]
        self.order = place.hops + [0]

    @staticmethod
    def scratch(own_rows, columns, units, lead=()):
        depth, unit = units // 4, (2 * own_rows, columns)
        edge = lead + (own_rows + -own_rows % 16, columns)
        return [
            pltpu.VMEM(lead + (2, depth) + unit, low_type),
            pltpu.VMEM(lead + (depth,) + unit, low_type),
            pltpu.VMEM(lead + (depth,) + unit, low_type),
            pltpu.VMEM(lead + (depth,) + unit, low_type),
            pltpu.VMEM(lead + (depth,) + unit, low_type),
            pltpu.VMEM(edge, low_type),
            pltpu.VMEM(edge, low_type),
            DMA(lead + (2, 2, depth)),
            DMA(lead + (2, depth)),
            DMA(lead + (2, depth)),
            DMA(lead + (2,)),
        ]

    def at(self, ref, z, x, core):
        u = self.place.unit(z, x, core)
        return ref.at[pl.ds(pl.multiple_of(u * self.rows, 16), self.rows)]

    def x_of(self, side):
        return self.place.x if side == 0 else 1 - self.place.x

    def to_core(self, side, hop):
        place = self.place
        return remote(
            self.at(self.source, place.z_after(hop), self.x_of(side), 1 - place.core),
            self.core_buf.at[side, hop],
            self.core_sem.at[0, side, hop],
            self.core_sem.at[1, side, hop],
            place.over_core(),
        )

    def to_x(self, hop):
        return remote(
            self.x_send.at[hop],
            self.x_buf.at[hop],
            self.x_sem.at[0, hop],
            self.x_sem.at[1, hop],
            self.place.over_x(),
        )

    def to_z(self, hop):
        return remote(
            self.z_send.at[hop],
            self.z_buf.at[hop],
            self.z_sem.at[0, hop],
            self.z_sem.at[1, hop],
            self.place.along_z(hop),
        )

    def to_y(self):
        return remote(
            self.y_send, self.y_buf, self.y_sem.at[0], self.y_sem.at[1], self.place.over_y()
        )

    def start(self):
        for side in (1, 0):
            for hop in self.order:
                self.to_core(side, hop).start()

    def mine(self, side, hop):
        place = self.place
        self.to_core(side, hop).wait_recv()
        own = self.at(self.full, place.z_after(hop), self.x_of(side), place.core)
        return own[...].astype(f32) + self.core_buf[side, hop].astype(f32)

    def stage_x(self, hop):
        self.x_send[hop] = self.mine(1, hop).astype(low_type)
        self.to_x(hop).start()

    def stage_z(self, hop):
        part = self.mine(0, hop)
        self.to_x(hop).wait_recv()
        part = part + self.x_buf[hop].astype(f32)
        self.z_send[hop] = part.astype(low_type)
        if hop:
            self.to_z(hop).start()

    def stage_y(self):
        total = self.z_send[0].astype(f32)
        for hop in self.place.hops:
            self.to_z(hop).wait_recv()
            total = total + self.z_buf[hop].astype(f32)
        half = self.rows // 2
        first = self.place.y == 0
        self.y_send[:half] = jnp.where(first, total[half:], total[:half]).astype(low_type)
        self.to_y().start()
        return jnp.where(first, total[:half], total[half:])

    def finish(self, kept):
        self.to_y().wait()
        return kept + self.y_buf[: kept.shape[0]].astype(f32)

    def drain(self):
        for hop in self.order:
            for side in (1, 0):
                self.to_core(side, hop).wait_send()
            self.to_x(hop).wait_send()
            if hop:
                self.to_z(hop).wait_send()


class Exchange:
    def __init__(self, place, send, recv, sem):
        self.send, self.recv, self.sem = send, recv, sem
        self.targets = [place.over_core(), place.over_x(), place.over_y()]
        span = 1
        while span < place.depth:
            flip = place.z + span - 2 * span * lax.rem(place.z // span, 2)
            self.targets.append((place.unit(flip, place.x, place.core), place.y))
            span *= 2

    @staticmethod
    def rounds(units):
        return 3 + (units // 4 - 1).bit_length()

    @staticmethod
    def scratch(shape, units):
        rounds = Exchange.rounds(units)
        return [
            pltpu.VMEM((rounds,) + shape, f32),
            pltpu.VMEM((rounds,) + shape, f32),
            DMA((2, rounds)),
        ]

    def copy(self, at):
        return remote(
            self.send.at[at], self.recv.at[at], self.sem.at[0, at], self.sem.at[1, at], self.targets[at]
        )

    def start(self, at, value):
        self.send[at] = value
        self.copy(at).start()

    def finish(self, at):
        self.copy(at).wait()
        return self.send[at] + self.recv[at]


def comm_params(collective):
    return pltpu.CompilerParams(
        collective_id=collective, has_side_effects=True, vmem_limit_bytes=VMEM
    )


def first_kernel(
    wq_ref,
    wk_ref,
    wv_ref,
    gains_ref,
    second_refs,
    tokens_ref,
    q_ref,
    k_ref,
    v_ref,
    x_ref,
    w_ref,
    gain_ref,
    second_pair,
    w_all,
    x_in,
    stage,
    pair,
    *rest,
):
    swap_sem, load_sem, save_sem, stage_sem, w_sem = rest[9:]
    place = Place()
    per, seq, width = x_ref.shape
    rows = tokens_ref.shape[1]
    gather = Gather(place, pair, w_all, rest[6:9])
    meet, second_meet = Meet(place, *rest[:3]), Meet(place, *rest[3:6])
    place.greet()

    def swap(doc):
        return remote(
            tokens_ref.at[(1 - place.y) * per + doc],
            x_in.at[per + doc],
            swap_sem.at[0, doc],
            swap_sem.at[1, doc],
            place.over_y(),
        )

    def load(doc):
        return pltpu.make_async_copy(
            tokens_ref.at[place.y * per + doc], x_in.at[doc], load_sem.at[doc]
        )

    def start_of(block):
        y = jnp.where(block < per, place.y, 1 - place.y)
        return pl.multiple_of(y * rows, 16)

    def save(block):
        return pltpu.make_async_copy(
            x_in.at[block],
            x_ref.at[lax.rem(block, per), pl.ds(start_of(block), rows)],
            save_sem.at[block],
        )

    def store(block, index):
        target = (q_ref, k_ref, v_ref)[index]
        begin = pl.multiple_of(lax.rem(block, per) * seq + start_of(block), 16)
        slot = lax.rem(block, 2)
        return pltpu.make_async_copy(
            stage.at[slot, index], target.at[pl.ds(begin, rows)], stage_sem.at[slot, index]
        )

    meet.start((wq_ref, wk_ref, wv_ref, gains_ref))
    for doc in range(per):
        load(doc).start()
        swap(doc).start()
    meet.finish(pair)
    stages = gather.stages()
    stages[0]()
    out_ref, in_ref, down_ref = second_refs
    chunk = in_ref.shape[1] // CHUNKS
    parts = [out_ref]
    for at in range(CHUNKS):
        span = slice(at * chunk, (at + 1) * chunk)
        parts += [in_ref.at[:, span], down_ref.at[:, span]]
    second_meet.start(parts)
    for step in stages[1:]:
        step()
    keep = pltpu.make_async_copy(w_all, w_ref, w_sem)
    keep.start()
    gains = w_all[:, 3 * width :].astype(f32).T
    gain_ref[...] = gains[: gain_ref.shape[0]]
    gain = gains[0:1]

    def project(block, _):
        @pl.when(block < per)
        def _():
            load(block).wait()

        @pl.when(block >= per)
        def _():
            swap(block - per).wait_recv()

        save(block).start()
        normed, _ = norm_rows(x_in[block].astype(f32))
        low = (normed * gain).astype(low_type)
        slot = lax.rem(block, 2)
        for index in range(3):
            part = dot(low, w_all[:, index * width : (index + 1) * width])
            if index == 0:
                part = part * (0.125 * LOG2E)

            @pl.when(block >= 2)
            def _(index=index):
                store(block - 2, index).wait()

            stage[slot, index] = part.astype(low_type)
            store(block, index).start()
        return 0

    lax.fori_loop(0, 2 * per, project, 0)
    second_meet.finish(second_pair)
    for block in range(2 * per):
        save(block).wait()
        if block >= 2 * per - 2:
            for index in range(3):
                store(block, index).wait()
    keep.wait()
    gather.drain()
    for doc in range(per):
        swap(doc).wait_send()


def first_call(firsts, gains, seconds, tokens, ways):
    units = lax.axis_size("dp")
    count, rows, width = tokens.shape
    own_rows = gains.shape[0]
    columns = sum(w.shape[1] for w in firsts) + gains.shape[1]
    second_columns = sum(w.shape[1] for w in seconds)
    per = count // ways
    total = per * rows * ways

    def kernel(*refs):
        begin = len(firsts) + 1
        end = begin + len(seconds)
        first_kernel(*refs[:begin], refs[begin:end], *refs[end:])

    return pl.pallas_call(
        kernel,
        in_specs=[VMEM_WHOLE] * (len(firsts) + 1 + len(seconds)) + [ANY],
        out_specs=[ANY] * 5 + [VMEM_WHOLE] * 2,
        out_shape=[struct((total, width))] * 3
        + [
            struct((per, rows * ways, width)),
            struct((units * ways * own_rows, columns)),
            struct((8, width), f32),
            struct((ways * own_rows, second_columns)),
        ],
        scratch_shapes=[
            pltpu.VMEM((units * ways * own_rows, columns), low_type),
            pltpu.VMEM((2 * per, rows, width), low_type),
            pltpu.VMEM((2, 3, rows, width), low_type),
            pltpu.VMEM((ways * own_rows, columns), low_type),
        ]
        + Meet.scratch(own_rows, columns)
        + Meet.scratch(own_rows, second_columns)
        + Gather.scratch(units)
        + [DMA((2, per)), DMA((per,)), DMA((2 * per,)), DMA((2, 3)), DMA],
        compiler_params=comm_params(1),
        name="first",
    )(*firsts, gains, *seconds, tokens)


def attend_send_kernel(
    len_ref,
    table_ref,
    q_ref,
    k_ref,
    v_ref,
    pair_ref,
    cot_ref,
    o_ref,
    lse_ref,
    w_ref,
    cot_doc,
    near_ref,
    cot_in,
    *rest,
    rows,
):
    place = Place()
    gathers = gather_parts(place, pair_ref.at[:, : w_ref.shape[1]], w_ref, rest[:-2])
    swap_sem, load_sem = rest[-2:]
    per, part = cot_doc.shape[0], cot_ref.shape[1]
    step = pl.program_id(0) * pl.num_programs(1) + pl.program_id(1)
    last = pl.num_programs(0) * pl.num_programs(1) - 1
    stages = [gather.stages() for gather in gathers]

    def swap(doc):
        return remote(
            cot_ref.at[(1 - place.y) * per + doc],
            cot_doc.at[doc, pl.ds(pl.multiple_of(place.y * part, 16), part)],
            swap_sem.at[0, doc],
            swap_sem.at[1, doc],
            place.over_y(),
        )

    def load(doc):
        return pltpu.make_async_copy(
            cot_ref.at[place.y * per + doc], cot_in.at[doc], load_sem.at[0, doc]
        )

    def save(doc):
        return pltpu.make_async_copy(
            cot_in.at[doc],
            cot_doc.at[doc, pl.ds(pl.multiple_of(place.y * part, 16), part)],
            load_sem.at[1, doc],
        )

    @pl.when(step == 0)
    def _():
        place.greet()
        for doc in range(per):
            load(doc).start()

    for at, piece, index in SEND_PLAN:

        @pl.when(step == at)
        def _(piece=piece, index=index):
            stages[piece][index]()

    @pl.when(step == 1)
    def _():
        for doc in range(per):
            swap(doc).start()
            load(doc).wait()
            save(doc).start()

    attend_kernel(len_ref, table_ref, q_ref, k_ref, v_ref, o_ref, lse_ref, near_ref, rows=rows)

    @pl.when(step == last)
    def _():
        done = {(piece, index) for _, piece, index in SEND_PLAN}
        for index in range(len(stages[0])):
            for piece in range(PARTS):
                if (piece, index) not in done:
                    stages[piece][index]()
        for gather in gathers:
            gather.drain()
        for doc in range(per):
            save(doc).wait()
            swap(doc).wait()


SEND_PLAN = (
    (0, 0, 0), (1, 1, 0), (3, 0, 1), (4, 1, 1), (5, 0, 2), (6, 1, 2),
    (7, 0, 3), (8, 1, 3), (9, 0, 4), (10, 1, 4), (11, 0, 5),
)


def attend_send_call(lengths, table, q, k, v, pair, columns, cot, rows=512):
    units = lax.axis_size("dp")
    docs, (total, width) = lengths.shape[0], q.shape
    seq, pairs = total // docs, width // 128
    slab = pl.BlockSpec((seq, 128), lambda p, d: (d, p))
    return pl.pallas_call(
        functools.partial(attend_send_kernel, rows=rows),
        grid=(pairs, docs),
        in_specs=[SMEM, SMEM, slab, slab, slab, whole(pair.shape), ANY],
        out_specs=[slab, pl.BlockSpec((1, 1, 2, seq), lambda p, d: (d, p, 0, 0)), ANY, ANY],
        out_shape=[
            struct((total, width)),
            struct((docs, pairs, 2, seq), f32),
            struct((units * pair.shape[0], columns)),
            struct((docs, seq, width)),
        ],
        scratch_shapes=[
            pltpu.VMEM((2, 3, SUB, SUB), f32),
            pltpu.VMEM((docs, cot.shape[1], width), low_type),
        ]
        + PARTS * Gather.scratch(units)
        + [DMA((2, docs)), DMA((2, docs))],
        compiler_params=comm_params(3),
        name="attend",
    )(lengths, table, q, k, v, pair, cot)


def back_send_kernel(
    len_ref,
    table_ref,
    q_ref,
    k_ref,
    v_ref,
    grad_ref,
    o_ref,
    lse_ref,
    g_ref,
    mixed_ref,
    dq_ref,
    dk_ref,
    dv_ref,
    table_sum,
    gw_ref,
    mixed_out,
    near_ref,
    near_sum,
    far_sum,
    acc,
    grads,
    mixed_in,
    kept,
    *rest,
    keys,
    queries,
    steps,
):
    place = Place()
    size = grads.shape[1] // CHUNKS
    grads_sem, swap_sem, load_sem = rest[11:]

    def scatter(at):
        span = pl.ds(pl.multiple_of(at * size, 128), size)
        return Scatter(
            place, grads.at[:, span], [ref.at[at] for ref in rest[:11]], g_ref.at[:, span]
        )

    per, part = mixed_ref.shape[0], mixed_out.shape[1]
    step = pl.program_id(0) * pl.num_programs(1) + pl.program_id(1)
    last = pl.num_programs(0) * pl.num_programs(1) - 1

    def swap(doc):
        return remote(
            mixed_ref.at[doc, pl.ds(pl.multiple_of((1 - place.y) * part, 16), part)],
            mixed_out.at[place.y * per + doc],
            swap_sem.at[0, doc],
            swap_sem.at[1, doc],
            place.over_y(),
        )

    def load(doc):
        return pltpu.make_async_copy(
            mixed_ref.at[doc, pl.ds(pl.multiple_of(place.y * part, 16), part)],
            mixed_in.at[doc],
            load_sem.at[0, doc],
        )

    def save(doc):
        return pltpu.make_async_copy(
            mixed_in.at[doc], mixed_out.at[place.y * per + doc], load_sem.at[1, doc]
        )

    take = pltpu.make_async_copy(g_ref, grads, grads_sem)

    @pl.when(step == 0)
    def _():
        place.greet()
        for at in range(CHUNKS):
            scatter(at).start()
        take.start()
        for doc in range(per):
            load(doc).start()
            swap(doc).start()

    @pl.when(step == 1)
    def _():
        take.wait()

    def every_other(first, work):
        at = (step - first) // 2

        @pl.when((step >= first) & (at < CHUNKS) & (step == first + 2 * at))
        def _():
            work(at)

    def x_stages(at):
        for hop in place.hops + [0]:
            scatter(at).stage_x(hop)

    def z_stages(at):
        for hop in place.hops + [0]:
            scatter(at).stage_z(hop)

    def y_stage(at):
        kept[at] = scatter(at).stage_y()

    def finish(at):
        gw_ref[:, pl.ds(pl.multiple_of(at * size, 128), size)] = scatter(at).finish(kept[at])

    every_other(1, x_stages)
    every_other(3, z_stages)
    every_other(5, y_stage)
    every_other(6, finish)

    @pl.when(step == 3)
    def _():
        for doc in range(per):
            load(doc).wait()
            save(doc).start()

    attend_back_kernel(
        len_ref,
        table_ref,
        q_ref,
        k_ref,
        v_ref,
        grad_ref,
        o_ref,
        lse_ref,
        dq_ref,
        dk_ref,
        dv_ref,
        table_sum,
        near_ref,
        near_sum,
        far_sum,
        acc,
        keys=keys,
        queries=queries,
    )

    @pl.when(step == last)
    def _():
        for at in range(CHUNKS):
            for first, work in ((1, x_stages), (3, z_stages), (5, y_stage), (6, finish)):
                if first + 2 * at >= steps:
                    work(at)
        for at in range(CHUNKS):
            scatter(at).drain()
        for doc in range(per):
            save(doc).wait()
            swap(doc).wait()


def back_send_call(lengths, table, q, k, v, grad, o, lse, g, mixed, keys=256, queries=1024):
    units = lax.axis_size("dp")
    docs, (total, width) = lengths.shape[0], q.shape
    seq, pairs = total // docs, width // 128
    columns = g.shape[1]
    own = g.shape[0] // (2 * units)
    slab = pl.BlockSpec((seq, 128), lambda p, d: (d, p))
    return pl.pallas_call(
        functools.partial(
            back_send_kernel, keys=keys, queries=min(queries, seq), steps=pairs * docs
        ),
        grid=(pairs, docs),
        in_specs=[
            SMEM,
            SMEM,
            slab,
            slab,
            slab,
            slab,
            slab,
            pl.BlockSpec((1, 1, 2, seq), lambda p, d: (d, p, 0, 0)),
            ANY,
            ANY,
        ],
        out_specs=[
            slab,
            slab,
            slab,
            pl.BlockSpec((2, 32, SUB), lambda p, d: (p, 0, 0)),
            whole((own, columns)),
            ANY,
        ],
        out_shape=[struct((total, width))] * 3
        + [
            struct((2 * pairs, 32, SUB), f32),
            struct((own, columns), f32),
            struct((2 * docs, seq // 2, width)),
        ],
        scratch_shapes=[
            pltpu.VMEM((2, 3, SUB, SUB), f32),
            pltpu.VMEM((2, 3, SUB, SUB), f32),
            pltpu.VMEM((2, 2, 8, SUB), f32),
            pltpu.VMEM((seq, 128), f32),
            pltpu.VMEM(g.shape, low_type),
            pltpu.VMEM((docs, seq // 2, width), low_type),
            pltpu.VMEM((CHUNKS, own, columns // CHUNKS), f32),
        ]
        + Scatter.scratch(own, columns // CHUNKS, units, (CHUNKS,))
        + [DMA, DMA((2, docs)), DMA((2, docs))],
        compiler_params=comm_params(4),
        name="attend_back",
    )(lengths, table, q, k, v, grad, o, lse, g, mixed.reshape(docs, seq, width))


def end_kernel(
    x_ref,
    dq_ref,
    dk_ref,
    dv_ref,
    mid_ref,
    w_ref,
    gain_ref,
    table_ref,
    wq_ref,
    wk_ref,
    wv_ref,
    w_in_ref,
    g_hidden_ref,
    g_out,
    gw_ref,
    gt_ref,
    small_ref,
    gains_ref,
    rows_in,
    low_all,
    grads,
    gt,
    *rest,
):
    place = Place()
    count, rows, width = gt_ref.shape
    per = count // 2
    seq = 2 * rows
    scatter_refs, kept = rest[:11], rest[11]
    small_send, small_recv, small_sem, load_sem, gt_sem = rest[12:]
    exchange = Exchange(place, small_send, small_recv, small_sem)
    sources = (x_ref, dq_ref, dk_ref, dv_ref, mid_ref)

    def scatter(at):
        return Scatter(place, grads.at[at], [ref.at[at] for ref in scatter_refs])

    def load(block, index):
        y = jnp.where(block < per, 1 - place.y, place.y)
        begin = pl.multiple_of(lax.rem(block, per) * seq + y * rows, 16)
        return pltpu.make_async_copy(
            sources[index].at[pl.ds(begin, rows)],
            rows_in.at[index, block],
            load_sem.at[block, index],
        )

    def give_away(block):
        return remote(
            gt.at[block],
            gt_ref.at[place.y * per + block],
            gt_sem.at[0, block],
            gt_sem.at[1, block],
            place.over_y(),
        )

    def give_home(block):
        return pltpu.make_async_copy(
            gt.at[block], gt_ref.at[place.y * per + block - per], gt_sem.at[0, block]
        )

    take = pltpu.make_async_copy(g_out, grads.at[0], load_sem.at[2 * per, 0])
    for index in range(5):
        load(0, index).start()
    take.start()
    for index in range(5):
        for block in range(1, 2 * per):
            load(block, index).start()
    place.greet()
    gain = gain_ref[0:1]
    take.wait()
    scatter(0).start()
    heads, buckets = table_ref.shape[:2]
    small_send[0] = jnp.zeros(small_ref.shape, f32)
    small_send[0, :heads, :buckets] = jnp.sum(table_ref[...], 2)
    exchange.copy(0).start()
    chunk = g_hidden_ref.shape[1] // (2 * CHUNKS)
    sum_second = jnp.zeros((gains_ref.shape[0], chunk), f32)
    for at in range(CHUNKS):
        sum_second += (
            g_hidden_ref[:, 2 * at * chunk : (2 * at + 1) * chunk]
            * w_in_ref[:, at * chunk : (at + 1) * chunk].astype(f32)
        )
    rounds = len(exchange.targets)

    def exchange_round(at):
        value = exchange.finish(at)
        if at < rounds - 1:
            exchange.start(at + 1, value)
        else:
            small_ref[...] = value

    def low_rows(block, _):
        @pl.when(block > 0)
        def _():
            load(block, 0).wait()

        normed, _ = norm_rows(rows_in[0, block].astype(f32))
        low_all[block] = (normed * gain).astype(low_type)
        return 0

    def rows_back(block):
        normed, inverse = norm_rows(rows_in[0, block].astype(f32))
        normed_grad = None
        for index in range(3):
            part = dot(
                rows_in[1 + index, block], w_ref[:, index * width : (index + 1) * width], NT
            )
            normed_grad = part if normed_grad is None else normed_grad + part
        scaled = normed_grad * gain
        inner = jnp.mean(scaled * normed, -1, keepdims=True)
        mid = rows_in[4, block].astype(f32)
        gt[block] = (mid + inverse * (scaled - normed * inner)).astype(low_type)

        @pl.when(block < per)
        def _():
            give_away(block).start()

        @pl.when(block >= per)
        def _():
            give_home(block).start()

    def weights_back(at):
        grads[at] = dot(
            low_all[...].reshape(2 * per * rows, width),
            rows_in[at].reshape(2 * per * rows, width),
            TN,
        ).astype(low_type)
        scatter(at).start()

    def during(at, first, last, work):
        @pl.when((at >= first) & (at <= last))
        def _():
            work(at)

    def x_stages(at):
        for hop in place.hops + [0]:
            scatter(at).stage_x(hop)

    def z_stages(at):
        for hop in place.hops + [0]:
            scatter(at).stage_z(hop)

    def y_stage(at):
        kept[at] = scatter(at).stage_y()

    def finish(at):
        gw_ref[at] = scatter(at).finish(kept[at])

    def project_step(at, _):
        weights_back(at)
        x_stages(at - 1)
        for index in range(2):
            during(at, index + 2, index + 2, lambda _, index=index: exchange_round(index))
        return 0

    def rows_step(block, _):
        rows_back(block)
        during(block, 1, 1, lambda _: x_stages(3))
        during(block, 1, 1, lambda _: z_stages(0))
        during(block, 1, 3, z_stages)
        during(block - 2, 0, 0, y_stage)
        during(block - 1, 1, 2, y_stage)
        during(block - 3, 0, 0, finish)
        for index in range(2, rounds):
            during(block, index - 1, index - 1, lambda _, index=index: exchange_round(index))
        return 0

    for index in range(5):
        load(0, index).wait()
    rows_back(0)
    lax.fori_loop(0, 2 * per, low_rows, 0)
    for index in range(1, 5):
        for block in range(1, 2 * per):
            load(block, index).wait()
    lax.fori_loop(1, 4, project_step, 0)
    lax.fori_loop(1, 2 * per, rows_step, 0)
    y_stage(3)
    finish(1)
    finish(2)
    finish(3)
    sum_first = jnp.zeros((gains_ref.shape[0], width), f32)
    for at, ref in enumerate((wq_ref, wk_ref, wv_ref)):
        sum_first += gw_ref[1 + at] * ref[...].astype(f32)
    lane = lax.broadcasted_iota(jnp.int32, (1, 128), 1)
    gains_ref[...] = jnp.where(
        lane == 0,
        jnp.sum(sum_first, 1, keepdims=True),
        jnp.sum(sum_second, 1, keepdims=True),
    )

    def drain(at, _):
        scatter(at).drain()
        return 0

    lax.fori_loop(0, 4, drain, 0)
    for block in range(per):
        give_away(block).wait()
        give_home(per + block).wait()


def end_call(x, dq, dk, dv, mid, w_first, gains, table, own_weights, g_hidden, g_out, docs, ways):
    units = lax.axis_size("dp")
    total, width = x.shape
    own = width // (units * ways)
    rows = total // (docs * ways)
    small = (table.shape[0] + -table.shape[0] % 8, 128)
    return pl.pallas_call(
        end_kernel,
        in_specs=[ANY] * 5 + [VMEM_WHOLE] * 8 + [ANY],
        out_specs=[VMEM_WHOLE, ANY, VMEM_WHOLE, VMEM_WHOLE],
        out_shape=[
            struct((4, own, width), f32),
            struct((docs * ways, rows, width)),
            struct(small, f32),
            struct((own, 128), f32),
        ],
        scratch_shapes=[
            pltpu.VMEM((5, docs * ways, rows, width), low_type),
            pltpu.VMEM((docs * ways, rows, width), low_type),
            pltpu.VMEM((4, width, width), low_type),
            pltpu.VMEM((docs * ways, rows, width), low_type),
        ]
        + Scatter.scratch(own, width, units, (4,))
        + [pltpu.VMEM((4, own, width), f32)]
        + Exchange.scratch(small, units)
        + [DMA((docs * ways + 1, 5)), DMA((2, docs * ways))],
        compiler_params=comm_params(2),
        name="end",
    )(x, dq, dk, dv, mid, w_first, gains, table, *own_weights, g_hidden, g_out)


def sharing(count):
    ways = lax.axis_size("blk")
    return max(1, count // ways), max(1, ways // count)


def to_documents(x):
    count, rows, width = x.shape
    ways, me = lax.axis_size("blk"), lax.axis_index("blk")
    per, share = sharing(count)
    if share > 1:
        everything = lax.all_gather(x, "blk", axis=1, tiled=True)
        return lax.dynamic_index_in_dim(everything, me // share, 0, keepdims=False)
    out = jnp.zeros((per, ways * rows, width), x.dtype)
    for hop in range(ways):
        piece = lax.dynamic_slice_in_dim(x, lax.rem(me + hop, ways) * per, per, 0)
        if hop:
            piece = lax.ppermute(piece, "blk", [(i, (i + hop) % ways) for i in range(ways)])
        source = lax.rem(me - hop + ways, ways)
        out = lax.dynamic_update_slice_in_dim(out, piece, source * rows, 1)
    return out.reshape(per * ways * rows, width)


def from_documents(y, count):
    ways, me = lax.axis_size("blk"), lax.axis_index("blk")
    per, share = sharing(count)
    width = y.shape[1]
    if share > 1:
        everything = lax.all_gather(y, "blk", axis=0, tiled=True).reshape(count, -1, width)
        rows = everything.shape[1] // ways
        return lax.dynamic_slice_in_dim(everything, me * rows, rows, 1)
    y = y.reshape(per, -1, width)
    rows = y.shape[1] // ways
    out = jnp.zeros((count, rows, width), y.dtype)
    for hop in range(ways):
        piece = lax.dynamic_slice_in_dim(y, lax.rem(me + hop, ways) * rows, rows, 1)
        if hop:
            piece = lax.ppermute(piece, "blk", [(i, (i + hop) % ways) for i in range(ways)])
        source = lax.rem(me - hop + ways, ways)
        out = lax.dynamic_update_slice_in_dim(out, piece, source * per, 0)
    return out


def among(y, share, split, concat):
    if share == 1:
        return y
    ways = lax.axis_size("blk")
    groups = [list(range(at, at + share)) for at in range(0, ways, share)]
    return lax.all_to_all(
        y, "blk", split, concat, axis_index_groups=groups, tiled=True
    )


def my_share(y, share, axis):
    if share == 1:
        return y
    size = y.shape[axis] // share
    at = lax.rem(lax.axis_index("blk"), share) * size
    return lax.dynamic_slice_in_dim(y, at, size, axis)


def body(
    tokens,
    lengths,
    norm1_gain,
    w_query,
    w_key,
    w_value,
    w_out,
    rel_table,
    norm2_gain,
    w_in,
    w_down,
    cotangent,
):
    micro, docs, rows, width = tokens.shape
    count = micro * docs
    per, share = sharing(count)
    both = ("dp", "blk")
    direct = lax.axis_size("blk") == 2 and per * 2 == count and lax.axis_size("dp") % 4 == 0
    gains = jnp.pad(jnp.stack([norm1_gain, norm2_gain], 1), ((0, 0), (0, SPARE - 2)))
    firsts, seconds = (w_query, w_key, w_value), (w_out, w_in, w_down)
    tokens_here = tokens.reshape(count, rows, width)
    cot_here = cotangent.reshape(count, rows, width)
    if direct:
        q, k, v, x, w_first, gain_rows, pair = first_call(
            firsts, gains, seconds, tokens_here, 2
        )
        x = x.reshape(-1, width)
    else:
        pair = None
        w_second = lax.all_gather(second_pieces(*seconds), both, axis=0, tiled=True)
        w_first = lax.all_gather(
            jnp.concatenate(firsts + (gains,), 1), both, axis=0, tiled=True
        )
        x = to_documents(tokens_here)
        gain_rows = w_first[:, 3 * width : 3 * width + 2].astype(f32).T
    gain_first, gain_second = gain_rows[:1], gain_rows[1:2]
    own = lax.dynamic_slice_in_dim(
        lengths.reshape(count), lax.axis_index("blk") // share * per, per, 0
    )
    x_rows = my_share(x, share, 0)
    own_rows, w_heads = own, w_first
    if share > 1:
        own_rows = own - lax.rem(lax.axis_index("blk"), share) * x_rows.shape[0]
        w_heads = jnp.concatenate(
            [my_share(w_first[:, i * width : (i + 1) * width], share, 1) for i in range(3)], 1
        )
    table = my_share((rel_table * LOG2E).T, share, 0)

    if direct:
        ahead = width + AHEAD * 2 * (w_in.shape[1] // CHUNKS)
        heads, lse, w_second, cot = attend_send_call(
            own, table, q, k, v, pair, ahead, cot_here
        )
        cot = cot.reshape(-1, width)
    else:
        q, k, v = qkv_call(x, gain_first, w_heads, width // share)
        heads, lse = attend_call(own, table, q, k, v)
        cot = my_share(to_documents(cot_here), share, 0)
    mixed, heads_grad, mid, g_out, g_hidden, gn_second = middle_call(
        own_rows, x_rows, among(heads, share, 0, 1), cot, gain_second, w_second, pair if AHEAD < CHUNKS else None
    )
    if direct:
        dq, dk, dv, table_sum, g_hidden, mixed = back_send_call(
            own, table, q, k, v, heads_grad, heads, lse, g_hidden, mixed
        )
    else:
        dq, dk, dv, table_sum = attend_back_call(
            own, table, q, k, v, among(heads_grad, share, 1, 0), heads, lse
        )
        mixed = from_documents(mixed, count)
        g_out = lax.psum_scatter(g_out, both, scatter_dimension=0, tiled=True).astype(f32)
        g_hidden = lax.psum_scatter(g_hidden, both, scatter_dimension=0, tiled=True).astype(f32)
    dq, dk, dv = (among(grad, share, 0, 1) for grad in (dq, dk, dv))
    head_count, bucket_count = rel_table.shape[1], rel_table.shape[0]
    if direct:
        g_first, grad_tokens, small, gains = end_call(
            x,
            dq,
            dk,
            dv,
            mid,
            w_first,
            gain_rows,
            table_sum,
            firsts + (w_in,),
            g_hidden,
            g_out,
            per,
            2,
        )
        grad_table = small[:head_count, :bucket_count].T
        gains = (gains[:, 0] / norm1_gain.astype(f32), gains[:, 1] / norm2_gain.astype(f32))
    else:
        grad_tokens, g_first, gn_first = last_call(
            x_rows, dq, dk, dv, mid, gain_first, w_first
        )
        grad_tokens = from_documents(grad_tokens, count)
        g_first = lax.psum_scatter(g_first, both, scatter_dimension=0, tiled=True).astype(f32)
        gains = lax.psum_scatter(
            jnp.concatenate([gn_first, gn_second], 0), both, scatter_dimension=1, tiled=True
        )
        table_sum = jnp.sum(table_sum, 2)
        if share > 1:
            at = lax.rem(lax.axis_index("blk"), share) * table_sum.shape[0]
            table_sum = lax.dynamic_update_slice_in_dim(
                jnp.zeros(rel_table.T.shape, f32), table_sum, at, 0
            )
        grad_table = lax.psum(table_sum, both).T
    if direct:
        g_out, grad_query, grad_key, grad_value = g_first
    else:
        grad_query, grad_key, grad_value = (
            g_first[:, i * width : (i + 1) * width] for i in range(3)
        )
    grad_in, grad_down = split_hidden(g_hidden)
    return (
        mixed.reshape(tokens.shape),
        grad_tokens.reshape(tokens.shape),
        gains[0],
        grad_query,
        grad_key,
        grad_value,
        g_out,
        grad_table,
        gains[1],
        grad_in,
        grad_down,
    )


def solution(mesh):
    rows = P(None, "dp", "blk", None)
    weight = P(("dp", "blk"), None)
    gain = P(("dp", "blk"))
    return jax.shard_map(
        body,
        mesh=mesh,
        in_specs=(
            rows,
            P(None, "dp"),
            gain,
            weight,
            weight,
            weight,
            weight,
            P(),
            gain,
            weight,
            weight,
            rows,
        ),
        out_specs=(rows, rows, gain, weight, weight, weight, weight, P(), gain, weight, weight),
        check_vma=False,
    )
```

```python
import functools

import jax
import jax.numpy as jnp
from jax import lax
from jax.experimental import pallas as pl
from jax.experimental.pallas import tpu as pltpu
from jax.sharding import PartitionSpec as P

EPS = 1e-06
NEG = -1e30
LIMITS = (12, 16, 23, 32, 46, 64, 91)
SUB = 128
LOG2E = 1.4426950408889634
GELU_A = 0.7978845608028654
GELU_B = 0.044715
VMEM = 62 * 2**20
NN = (((1,), (0,)), ((), ()))
NT = (((1,), (1,)), ((), ()))
TN = (((0,), (0,)), ((), ()))
low_type = jnp.bfloat16
f32 = jnp.float32


def dot(left, right, dims=NN):
    return lax.dot_general(left, right, dims, preferred_element_type=f32)


def bucket_of(relative):
    distance = jnp.abs(relative)
    far_bucket = 8 + sum(((distance >= border).astype(jnp.int32) for border in LIMITS))
    bucket = jnp.where(distance < 8, distance, far_bucket)
    return bucket + 16 * (relative > 0).astype(jnp.int32)


def norm_rows(rows):
    inverse = lax.rsqrt(jnp.mean(rows * rows, -1, keepdims=True) + EPS)
    return rows * inverse, inverse


def whole(shape):
    return pl.BlockSpec(shape, lambda *_: (0,) * len(shape), pipeline_mode=pl.Buffered(1))


def params():
    return pltpu.CompilerParams(vmem_limit_bytes=VMEM)


def struct(shape, dtype=low_type):
    return jax.ShapeDtypeStruct(shape, dtype)


SMEM = pl.BlockSpec(memory_space=pltpu.SMEM)


BAND = 4 * SUB


def band_buckets(keys_are_rows):
    at = lax.broadcasted_iota(jnp.int32, (1, BAND), 1)
    apart = jnp.where(at < 3 * SUB, at, at - BAND) - SUB
    return bucket_of(-apart if keys_are_rows else apart)


def tile_columns(apart, keys_are_rows):
    at = SUB * (1 - apart if keys_are_rows else 1 + apart)
    return slice(at, at + SUB)


def fill_tiles(near, table_ref, pair, keys_are_rows):
    buckets = band_buckets(keys_are_rows)
    for h in range(2):
        line = jnp.zeros((1, BAND), f32)
        for b in range(32):
            line = jnp.where(buckets == b, table_ref[2 * pair + h, b], line)
        band = pltpu.roll(
            jnp.broadcast_to(line, (SUB, BAND)), 0, 1, stride=1, stride_axis=0
        )
        for apart in (-1, 0, 1):
            near[h, apart + 1] = band[:, tile_columns(apart, keys_are_rows)]


def band_sums(tiles):
    band = jnp.concatenate([tiles[2], tiles[1], tiles[0], jnp.zeros((SUB, SUB), f32)], 1)
    out = band[:8]
    for at in range(8, SUB, 8):
        out = out + pltpu.roll(band[at : at + 8], BAND - at, 1)
    row = lax.broadcasted_iota(jnp.int32, out.shape, 0)
    for bit in (1, 2, 4):
        out = jnp.where((row & bit) != 0, pltpu.roll(out, BAND - bit, 1), out)
    return jnp.sum(out, 0, keepdims=True)


def bucket_sums(sums, count):
    buckets = band_buckets(True)
    lane = lax.broadcasted_iota(jnp.int32, (1, SUB), 1)
    out = jnp.zeros((sums.shape[0], SUB), f32)
    for b in range(count):
        part = jnp.sum(jnp.where(buckets == b, sums, 0.0), 1, keepdims=True)
        out = jnp.where(lane == b, part, out)
    return out


def qkv_kernel(x_ref, gain_ref, w_ref, q_ref, k_ref, v_ref):
    width = q_ref.shape[1]
    normed, _ = norm_rows(x_ref[...].astype(f32))
    low = (normed * gain_ref[...]).astype(low_type)
    q_ref[...] = (dot(low, w_ref[:, :width]) * (0.125 * LOG2E)).astype(low_type)
    k_ref[...] = dot(low, w_ref[:, width : 2 * width]).astype(low_type)
    v_ref[...] = dot(low, w_ref[:, 2 * width : 3 * width]).astype(low_type)


def qkv_call(x, gain, w_first, heads_width, rows=512):
    total, width = x.shape
    row = pl.BlockSpec((rows, width), lambda i: (i, 0))
    return pl.pallas_call(
        qkv_kernel,
        grid=(total // rows,),
        in_specs=[row, whole((1, width)), whole(w_first.shape)],
        out_specs=[pl.BlockSpec((rows, heads_width), lambda i: (i, 0))] * 3,
        out_shape=[struct((total, heads_width))] * 3,
        compiler_params=params(),
        name="qkv",
    )(x, gain, w_first)


def attend_kernel(
    len_ref, table_ref, q_ref, k_ref, v_ref, o_ref, lse_ref, near_ref, *, rows
):
    pair, doc = pl.program_id(0), pl.program_id(1)

    @pl.when(doc == 0)
    def _():
        fill_tiles(near_ref, table_ref, pair, False)

    seq = q_ref.shape[0]
    subs = seq // SUB
    first = lax.broadcasted_iota(jnp.int32, (1, 128), 1) < 64
    live = lax.broadcasted_iota(jnp.int32, (1, seq), 1) < len_ref[doc]
    one = jnp.ones((), low_type)
    k, v = k_ref[...], v_ref[...]
    v_ones = (jnp.where(first, v, one), jnp.where(first, one, v))
    for block in range(seq // rows):
        span = slice(block * rows, (block + 1) * rows)
        q = q_ref[span, :]
        outs, tops = [], []
        for h in range(2):
            q_one = jnp.where(first == (h == 0), q, jnp.zeros((), low_type))
            raw = dot(q_one, k, NT)
            strips = []
            for a in range(rows // SUB):
                at = block * (rows // SUB) + a
                strip = raw[a * SUB : (a + 1) * SUB]
                low, high = max(at - 1, 0), min(at + 2, subs)
                parts = []
                if low > 0:
                    parts.append(strip[:, : low * SUB] + table_ref[2 * pair + h, 15])
                for b in range(low, high):
                    parts.append(strip[:, b * SUB : (b + 1) * SUB] + near_ref[h, b - at + 1])
                if high < subs:
                    parts.append(strip[:, high * SUB :] + table_ref[2 * pair + h, 31])
                strips.append(jnp.concatenate(parts, 1))
            scores = jnp.where(live, jnp.concatenate(strips, 0), NEG)
            top = jnp.max(scores, 1, keepdims=True)
            outs.append(dot(jnp.exp2(scores - top).astype(low_type), v_ones[h]))
            tops.append(top)
        total = jnp.where(first, pltpu.roll(outs[0], 64, 1), pltpu.roll(outs[1], 64, 1))
        o_ref[span, :] = (jnp.where(first, outs[0], outs[1]) / total).astype(low_type)
        log_total = (jnp.where(first, tops[0], tops[1]) + jnp.log2(total)).T
        lse_ref[0, 0, 0:1, span] = log_total[0:1]
        lse_ref[0, 0, 1:2, span] = log_total[64:65]


def attend_call(lengths, table, q, k, v, rows=512):
    docs, (total, width) = lengths.shape[0], q.shape
    seq, pairs = total // docs, width // 128
    slab = pl.BlockSpec((seq, 128), lambda p, d: (d, p))
    return pl.pallas_call(
        functools.partial(attend_kernel, rows=rows),
        grid=(pairs, docs),
        in_specs=[
            SMEM,
            SMEM,
            slab,
            slab,
            slab,
        ],
        out_specs=[slab, pl.BlockSpec((1, 1, 2, seq), lambda p, d: (d, p, 0, 0))],
        out_shape=[struct((total, width)), struct((docs, pairs, 2, seq), f32)],
        scratch_shapes=[pltpu.VMEM((2, 3, SUB, SUB), f32)],
        compiler_params=params(),
        name="attend",
    )(lengths, table, q, k, v)


CHUNKS = 4
AHEAD = 2


def second_pieces(w_out, w_in, w_down):
    chunk = w_in.shape[1] // CHUNKS
    parts = [w_out]
    for at in range(0, CHUNKS * chunk, chunk):
        parts += [w_in[:, at : at + chunk], w_down[:, at : at + chunk]]
    return jnp.concatenate(parts, 1)


def split_hidden(grads):
    chunk = grads.shape[1] // (2 * CHUNKS)
    parts = [grads[:, at * chunk : (at + 1) * chunk] for at in range(2 * CHUNKS)]
    return jnp.concatenate(parts[0::2], 1), jnp.concatenate(parts[1::2], 1)


def middle_kernel(
    len_ref,
    x_ref,
    heads_ref,
    cot_ref,
    gain_ref,
    w_out,
    w_hbm,
    mixed_ref,
    hgrad_ref,
    mid_ref,
    g_out,
    g_ref,
    gn_ref,
    scratch,
    *,
    seq,
    before_chunk,
):
    low_all, grad_all, normed_all, inverse_all, mixed_all, back_all = scratch[:6]
    act_all, up_all, g_buf, acc_gain, g_sem, w_all, w_sem = scratch[6:]
    step = pl.program_id(0)
    rows, width = x_ref.shape
    total = low_all.shape[0]
    chunk = w_all.shape[1] // (2 * CHUNKS)
    fine, block = total // rows, MIDDLE_BLOCK
    coarse = total // block
    begin = fine
    finish = fine + CHUNKS * coarse

    @pl.when(step < begin)
    def _():
        span = pl.ds(pl.multiple_of(step * rows, rows), rows)
        per = seq // rows
        place = lax.rem(step, per) * rows + lax.broadcasted_iota(jnp.int32, (rows, 1), 0)
        residual = x_ref[...].astype(f32) + dot(heads_ref[...], w_out[...])
        normed, inverse = norm_rows(residual)
        mixed_all[span, :] = residual
        back_all[span, :] = jnp.zeros_like(residual)
        normed_all[span, :] = normed.astype(low_type)
        inverse_all[span, :] = jnp.broadcast_to(inverse, (rows, 128))
        low_all[span, :] = (normed * gain_ref[...]).astype(low_type)
        grad_all[span, :] = jnp.where(
            place < len_ref[jnp.minimum(step // per, len_ref.shape[0] - 1)],
            cot_ref[...],
            jnp.zeros((), low_type),
        )

    def store(at):
        begins = pl.multiple_of(at * (2 * chunk), 128)
        slot = lax.rem(at, 2)
        return pltpu.make_async_copy(
            g_buf.at[slot], g_ref.at[:, pl.ds(begins, 2 * chunk)], g_sem.at[slot]
        )

    ready = w_hbm.shape[1] - width
    take = pltpu.make_async_copy(w_hbm.at[:, width:], w_all.at[:, :ready], w_sem)

    @pl.when(step == 0)
    def _():
        take.start()

    at = jnp.maximum(step - begin, 0) // coarse

    @pl.when(step == begin)
    def _():
        take.wait()

    for index in range(CHUNKS):

        @pl.when(step == begin + index * coarse)
        def _(index=index):
            before_chunk(index)

    @pl.when((step >= begin) & (step < finish))
    def _():
        span = pl.ds(pl.multiple_of((step - begin - at * coarse) * block, block), block)
        w_up = w_all[:, pl.ds(pl.multiple_of(at * (2 * chunk), 128), chunk)]
        w_down = w_all[:, pl.ds(pl.multiple_of(at * (2 * chunk) + chunk, 128), chunk)]
        u = dot(low_all[span, :], w_up)
        square = u * u
        bend = jnp.tanh(u * (GELU_A + GELU_A * GELU_B * square))
        half = 0.5 + 0.5 * bend
        act = (u * half).astype(low_type)
        slope = half + (0.5 * u) * (1 - bend * bend) * (GELU_A + 3 * GELU_A * GELU_B * square)
        up_grad = (dot(grad_all[span, :], w_down) * slope).astype(low_type)
        act_all[span, :] = act
        up_all[span, :] = up_grad
        mixed_all[span, :] += dot(act, w_down, NT)
        back_all[span, :] += dot(up_grad, w_up, NT)

    @pl.when((step >= begin) & (step < finish) & (step - begin == at * coarse + coarse - 1))
    def _():
        slot = lax.rem(at, 2)

        @pl.when(at >= 2)
        def _():
            store(at - 2).wait()

        g_buf[slot, :, :chunk] = dot(low_all[...], up_all[...], TN).astype(low_type)
        g_buf[slot, :, chunk:] = dot(grad_all[...], act_all[...], TN).astype(low_type)
        store(at).start()

    @pl.when(step >= finish)
    def _():
        span = pl.ds(pl.multiple_of((step - finish) * rows, rows), rows)
        mixed_ref[...] = mixed_all[span, :].astype(low_type)
        normed, back = normed_all[span, :].astype(f32), back_all[span, :]
        scaled = back * gain_ref[...]
        inner = jnp.mean(scaled * normed, -1, keepdims=True)
        inverse = inverse_all[span, :][:, :1]
        mid = grad_all[span, :].astype(f32) + inverse * (scaled - normed * inner)
        mid = mid.astype(low_type)
        part = jnp.sum((back * normed).reshape(rows // 8, 8, width), 0)
        acc_gain[...] = jnp.where(step == finish, part, acc_gain[...] + part)
        mid_ref[...] = mid
        act_all[span, :width] = mid
        up_all[span, :width] = heads_ref[...]
        hgrad_ref[...] = dot(mid, w_out[...], NT).astype(low_type)

    @pl.when(step == pl.num_programs(0) - 1)
    def _():
        g_out[...] = dot(up_all[:, :width], act_all[:, :width], TN).astype(low_type)
        gn_ref[...] = jnp.sum(acc_gain[...], 0, keepdims=True)
        for at in range(CHUNKS - 2, CHUNKS):
            store(at).wait()


MIDDLE_BLOCK = 512


def middle_plain_kernel(*refs, seq):
    w_ref, w_hbm, rest = refs[5], refs[6], refs[7:]
    middle_kernel(
        *refs[:5],
        w_ref,
        w_hbm,
        *rest[:6],
        rest[6:],
        seq=seq,
        before_chunk=lambda at: None,
    )


def middle_send_kernel(*refs, seq):
    w_ref, w_hbm, pair_ref, rest = refs[5], refs[6], refs[7], refs[8:]
    w_all, sems = rest[17], rest[19:]
    place = Place()
    late = w_all.at[:, w_hbm.shape[1] - refs[1].shape[1] :]
    gathers = gather_parts(place, pair_ref, late, sems)
    stages = [gather.stages() for gather in gathers]
    planned = {(part, index) for _, part, index in MIDDLE_PLAN}
    step = pl.program_id(0)

    @pl.when(step == 0)
    def _():
        place.greet()

    for when, part, index in MIDDLE_PLAN:

        @pl.when(step == when)
        def _(part=part, index=index):
            stages[part][index]()

    def before_chunk(at):
        part = (at - AHEAD) * PARTS // (CHUNKS - AHEAD)
        if at >= AHEAD and part * (CHUNKS - AHEAD) == (at - AHEAD) * PARTS:
            for index in range(len(stages[part])):
                if (part, index) not in planned:
                    stages[part][index]()

    middle_kernel(
        *refs[:5],
        w_ref,
        w_hbm,
        *rest[:6],
        rest[6:19],
        seq=seq,
        before_chunk=before_chunk,
    )

    @pl.when(step == pl.num_programs(0) - 1)
    def _():
        for gather in gathers:
            gather.drain()


MIDDLE_PLAN = (
    (0, 0, 0), (4, 1, 0), (5, 0, 1), (6, 1, 1), (7, 0, 2), (8, 1, 2),
    (9, 0, 3), (10, 1, 3), (11, 0, 4), (13, 1, 4),
)


def middle_call(lengths, x, heads, cot, gain, w_second, pair=None, rows=512):
    total, width = x.shape
    columns = w_second.shape[1] + (0 if pair is None else pair.shape[1])
    chunk = (columns - width) // (2 * CHUNKS)
    fine = total // rows
    steps = 2 * fine + CHUNKS * (total // MIDDLE_BLOCK)
    early = pl.BlockSpec((rows, width), lambda i: (jnp.minimum(i, fine - 1), 0))
    late = pl.BlockSpec((rows, width), lambda i: (jnp.maximum(i - (steps - fine), 0), 0))
    ends = pl.BlockSpec(
        (rows, width),
        lambda i: (jnp.where(i < steps - fine, jnp.minimum(i, fine - 1), i - (steps - fine)), 0),
    )
    square = (width, 2 * chunk)
    scratch = [
        pltpu.VMEM((total, width), low_type),
        pltpu.VMEM((total, width), low_type),
        pltpu.VMEM((total, width), low_type),
        pltpu.VMEM((total, 128), f32),
        pltpu.VMEM((total, width), f32),
        pltpu.VMEM((total, width), f32),
        pltpu.VMEM((total, max(chunk, width)), low_type),
        pltpu.VMEM((total, max(chunk, width)), low_type),
        pltpu.VMEM((2,) + square, low_type),
        pltpu.VMEM((8, width), f32),
        DMA((2,)),
        pltpu.VMEM((width, columns - width), low_type),
        DMA,
    ]
    kernel, compiler, operands = middle_plain_kernel, params(), []
    if pair is not None:
        kernel, compiler, operands = middle_send_kernel, comm_params(5), [pair]
        scratch += PARTS * Gather.scratch(lax.axis_size("dp"))
    square_out = (width, width)
    first_block = pl.BlockSpec(
        square_out, lambda i: (0, 0), pipeline_mode=pl.Buffered(1)
    )
    return pl.pallas_call(
        functools.partial(kernel, seq=total // lengths.shape[0]),
        grid=(steps,),
        in_specs=[SMEM, early, ends, early, whole((1, width)), first_block, ANY]
        + [whole(operand.shape) for operand in operands],
        out_specs=[late, late, late, whole(square_out), ANY, whole((1, width))],
        out_shape=[struct((total, width))] * 3
        + [
            struct(square_out),
            struct((width, CHUNKS * 2 * chunk)),
            struct((1, width), f32),
        ],
        scratch_shapes=scratch,
        compiler_params=compiler,
        name="middle",
    )(lengths, x, heads, cot, gain, w_second, w_second, *operands)


def attend_back_kernel(
    len_ref,
    table_ref,
    q_ref,
    k_ref,
    v_ref,
    grad_ref,
    o_ref,
    lse_ref,
    dq_ref,
    dk_ref,
    dv_ref,
    table_sum,
    near_ref,
    near_sum,
    far_sum,
    acc,
    *,
    keys,
    queries,
):
    pair, doc = pl.program_id(0), pl.program_id(1)
    seq = q_ref.shape[0]
    first = lax.broadcasted_iota(jnp.int32, (1, 128), 1) < 64
    zero = jnp.zeros((), low_type)

    def halves(x):
        return jnp.where(first, x, zero), jnp.where(first, zero, x)

    grad = grad_ref[...]
    q_one, g_one = halves(q_ref[...]), halves(grad)
    product = grad.astype(f32) * o_ref[...].astype(f32)
    upper = product.astype(low_type)
    lower = (product - upper.astype(f32)).astype(low_type)
    row = lax.broadcasted_iota(jnp.int32, (16, 128), 0)
    column = lax.broadcasted_iota(jnp.int32, (16, 128), 1)
    member = (row == column // 64).astype(f32).astype(low_type)
    delta = dot(member, upper, NT) + dot(member, lower, NT)

    @pl.when(doc == 0)
    def _():
        fill_tiles(near_ref, table_ref, pair, True)
        near_sum[...] = jnp.zeros_like(near_sum)
        far_sum[...] = jnp.zeros_like(far_sum)

    for kb in range(seq // keys):
        held = slice(kb * keys, (kb + 1) * keys)
        k, v = k_ref[held, :], v_ref[held, :]
        k_turned = k.T
        live = (kb * keys + lax.broadcasted_iota(jnp.int32, (keys, 1), 0)) < len_ref[doc]
        dk = jnp.zeros((keys, 128), f32)
        dv = jnp.zeros((keys, 128), f32)
        for qb in range(seq // queries):
            span = slice(qb * queries, (qb + 1) * queries)
            for h in range(2):
                scores = dot(k, q_one[h][span], NT)
                prob_grad = dot(v, g_one[h][span], NT)
                lse = lse_ref[0, 0, h : h + 1, span]
                lse_side = (lse - table_ref[2 * pair + h, 15], lse - table_ref[2 * pair + h, 31])
                row_delta = delta[h : h + 1, span]
                prob_rows, grad_rows = [], []
                for a in range(keys // SUB):
                    down = slice(a * SUB, (a + 1) * SUB)
                    probs, grads = [], []
                    for b in range(queries // SUB):
                        across = slice(b * SUB, (b + 1) * SUB)
                        apart = kb * (keys // SUB) + a - qb * (queries // SUB) - b
                        tile = scores[down, across]
                        if abs(apart) <= 1:
                            tile = tile + near_ref[h, apart + 1] - lse[:, across]
                        else:
                            tile = tile - lse_side[int(apart > 0)][:, across]
                        prob = jnp.where(live[down], jnp.exp2(tile), 0.0)
                        score_grad = prob * (prob_grad[down, across] - row_delta[:, across])
                        if abs(apart) <= 1:
                            near_sum[h, apart + 1] += score_grad
                        else:
                            far_sum[h, int(apart > 0)] += jnp.sum(
                                score_grad.reshape(SUB // 8, 8, SUB), 0
                            )
                        probs.append(prob.astype(low_type))
                        grads.append(score_grad.astype(low_type))
                    prob_rows.append(jnp.concatenate(probs, 1))
                    grad_rows.append(jnp.concatenate(grads, 1))
                prob_low = jnp.concatenate(prob_rows, 0)
                grad_low = jnp.concatenate(grad_rows, 0)
                dv = dv + dot(prob_low, g_one[h][span])
                dk = dk + dot(grad_low, q_one[h][span])
                side = slice(64 * h, 64 * (h + 1))
                part = dot(k_turned[side], grad_low)
                if kb:
                    part = part + acc[side, span]
                acc[side, span] = part
        dv_ref[held, :] = dv.astype(low_type)
        dk_ref[held, :] = (dk * (1 / LOG2E)).astype(low_type)
    dq_ref[...] = (acc[...] * 0.125).T.astype(low_type)

    @pl.when(doc == pl.num_programs(1) - 1)
    def _():
        lane = lax.broadcasted_iota(jnp.int32, (1, BAND), 1)
        for h in range(2):
            left = jnp.sum(far_sum[h, 0], keepdims=True)
            right = jnp.sum(far_sum[h, 1], keepdims=True)
            sums = band_sums(near_sum[h])
            table_sum[0, h : h + 1] = (
                sums + jnp.where(lane == 3 * SUB - 1, left, 0.0) + jnp.where(lane == 0, right, 0.0)
            )


def attend_back_call(lengths, table, q, k, v, grad, o, lse, keys=512, queries=1024):
    docs, (total, width) = lengths.shape[0], q.shape
    seq, pairs = total // docs, width // 128
    queries = min(queries, seq)
    slab = pl.BlockSpec((seq, 128), lambda p, d: (d, p))
    return pl.pallas_call(
        functools.partial(attend_back_kernel, keys=keys, queries=queries),
        grid=(pairs, docs),
        in_specs=[
            SMEM,
            SMEM,
            slab,
            slab,
            slab,
            slab,
            slab,
            pl.BlockSpec((1, 1, 2, seq), lambda p, d: (d, p, 0, 0)),
        ],
        out_specs=[slab, slab, slab, pl.BlockSpec((1, 2, BAND), lambda p, d: (p, 0, 0))],
        out_shape=[struct((total, width))] * 3 + [struct((pairs, 2, BAND), f32)],
        scratch_shapes=back_scratch(seq),
        compiler_params=params(),
        name="attend_back",
    )(lengths, table, q, k, v, grad, o, lse)


def back_scratch(seq):
    return [
        pltpu.VMEM((2, 3, SUB, SUB), f32),
        pltpu.VMEM((2, 3, SUB, SUB), f32),
        pltpu.VMEM((2, 2, 8, SUB), f32),
        pltpu.VMEM((128, seq), f32),
    ]


def last_kernel(
    x_ref,
    dq_ref,
    dk_ref,
    dv_ref,
    mid_ref,
    gain_ref,
    w_ref,
    gt_ref,
    gw_ref,
    gn_ref,
    acc,
    acc_gain,
):
    step = pl.program_id(0)
    rows, width = x_ref.shape

    @pl.when(step == 0)
    def _():
        acc[...] = jnp.zeros_like(acc)
        acc_gain[...] = jnp.zeros_like(acc_gain)

    gain = gain_ref[...]
    normed, inverse = norm_rows(x_ref[...].astype(f32))
    low = (normed * gain).astype(low_type)
    normed_grad = None
    for index, ref in enumerate((dq_ref, dk_ref, dv_ref)):
        part = slice(index * width, (index + 1) * width)
        grad = ref[...]
        acc[:, part] += dot(low, grad, TN)
        back = dot(grad, w_ref[:, part], NT)
        normed_grad = back if normed_grad is None else normed_grad + back
    acc_gain[...] += jnp.sum((normed_grad * normed).reshape(rows // 8, 8, width), 0)
    scaled = normed_grad * gain
    inner = jnp.mean(scaled * normed, -1, keepdims=True)
    gt_ref[...] = (mid_ref[...].astype(f32) + inverse * (scaled - normed * inner)).astype(low_type)

    @pl.when(step == pl.num_programs(0) - 1)
    def _():
        gw_ref[...] = acc[...].astype(low_type)
        gn_ref[...] = jnp.sum(acc_gain[...], 0, keepdims=True)


def last_call(x, dq, dk, dv, mid, gain, w_first, rows=512):
    total, width = x.shape
    row = pl.BlockSpec((rows, width), lambda i: (i, 0))
    grads = (width, 3 * width)
    return pl.pallas_call(
        last_kernel,
        grid=(total // rows,),
        in_specs=[row] * 5 + [whole((1, width)), whole(w_first.shape)],
        out_specs=[row, whole(grads), whole((1, width))],
        out_shape=[struct((total, width)), struct(grads), struct((1, width), f32)],
        scratch_shapes=[pltpu.VMEM(grads, f32), pltpu.VMEM((8, width), f32)],
        compiler_params=params(),
        name="last",
    )(x, dq, dk, dv, mid, gain, w_first)


MESH_ID = pl.DeviceIdType.MESH
ANY = pl.BlockSpec(memory_space=pl.ANY)
VMEM_WHOLE = pl.BlockSpec(memory_space=pltpu.VMEM)
DMA = pltpu.SemaphoreType.DMA
SPARE = 128


class Place:
    def __init__(self):
        self.dp, self.y = lax.axis_index("dp"), lax.axis_index("blk")
        self.depth = lax.axis_size("dp") // 4
        self.z = self.dp // 4
        self.x = lax.rem(self.dp // 2, 2)
        self.core = lax.rem(self.dp, 2)
        self.hops = sorted(range(1, self.depth), key=lambda hop: min(hop, self.depth - hop))

    def unit(self, z, x, core):
        return (z * 2 + x) * 2 + core

    def z_after(self, hop):
        return lax.rem(self.z + hop, self.depth)

    def z_before(self, hop):
        return lax.rem(self.z + self.depth - hop, self.depth)

    def along_z(self, hop):
        return (self.unit(self.z_after(hop), self.x, self.core), self.y)

    def over_x(self):
        return (self.unit(self.z, 1 - self.x, self.core), self.y)

    def over_core(self):
        return (self.unit(self.z, self.x, 1 - self.core), self.y)

    def over_y(self):
        return (self.dp, 1 - self.y)

    def greet(self):
        barrier = pltpu.get_barrier_semaphore()
        peers = [self.over_x(), self.over_core(), self.over_y()]
        peers += [self.along_z(hop) for hop in self.hops]
        for peer in peers:
            pl.semaphore_signal(barrier, device_id=peer, device_id_type=MESH_ID)
        pl.semaphore_wait(barrier, len(peers))


def remote(source, target, send, recv, device):
    return pltpu.make_async_remote_copy(
        src_ref=source,
        dst_ref=target,
        send_sem=send,
        recv_sem=recv,
        device_id=device,
        device_id_type=MESH_ID,
    )


class Meet:
    def __init__(self, place, shard, other, sem):
        self.place, self.shard, self.other, self.sem = place, shard, other, sem

    @staticmethod
    def scratch(own_rows, columns):
        block = (own_rows + -own_rows % 16, columns)
        return [pltpu.VMEM(block, low_type), pltpu.VMEM(block, low_type), DMA((2,))]

    def copy(self):
        return remote(self.shard, self.other, self.sem.at[0], self.sem.at[1], self.place.over_y())

    def start(self, parts):
        at = 0
        for ref in parts:
            rows, columns = ref.shape
            self.shard[:rows, at : at + columns] = ref[...]
            at += columns
        self.copy().start()

    def finish(self, pair):
        self.copy().wait()
        half = pair.shape[0] // 2
        mine = self.shard[:half].astype(f32)
        theirs = self.other[:half].astype(f32)
        first = self.place.y == 0
        pair[...] = jnp.concatenate(
            [jnp.where(first, mine, theirs), jnp.where(first, theirs, mine)], 0
        ).astype(low_type)


def hidden_parts(in_ref, down_ref, begin, end):
    chunk = in_ref.shape[1] // CHUNKS
    parts = []
    for at in range(begin, end):
        span = slice(at * chunk, (at + 1) * chunk)
        parts += [in_ref.at[:, span], down_ref.at[:, span]]
    return parts


class Gather:
    def __init__(self, place, pair, full, sems):
        self.place, self.pair, self.full = place, pair, full
        self.send_sem, self.recv_sem, self.put_sem = sems
        self.rows = pair.shape[0]
        self.mine = place.unit(place.z, place.x, place.core)
        self.has_left, self.has_right = place.z > 0, place.z < place.depth - 1

    @staticmethod
    def scratch(units):
        return [DMA((units, 4)), DMA((units,)), DMA]

    def at(self, u):
        return self.full.at[pl.ds(pl.multiple_of(u * self.rows, 16), self.rows)]

    def send(self, u, kind, source=None):
        place = self.place
        device = {
            "left": (place.dp - 4, place.y),
            "right": (place.dp + 4, place.y),
            "x": place.over_x(),
            "core": place.over_core(),
        }[kind]
        slot = ("left", "right", "x", "core").index(kind)
        source = self.at(u) if source is None else source
        return remote(source, self.at(u), self.send_sem.at[u, slot], self.recv_sem.at[u], device)

    def put(self):
        return pltpu.make_async_copy(self.pair, self.at(self.mine), self.put_sem)

    def spread(self):
        for kind, there in (("right", self.has_right), ("left", self.has_left)):

            @pl.when(there)
            def _(kind=kind):
                self.send(self.mine, kind, self.pair).start()

        self.send(self.mine, "x", self.pair).start()
        self.send(self.mine, "core", self.pair).start()
        self.put().start()

    def from_z(self, hop):
        place = self.place
        for kind, z, onward in (
            ("right", place.z - hop, self.has_right),
            ("left", place.z + hop, self.has_left),
        ):

            @pl.when((z >= 0) & (z < place.depth))
            def _(kind=kind, z=z, onward=onward):
                u = place.unit(z, place.x, place.core)
                self.send(u, "core").wait_recv()

                @pl.when(onward)
                def _():
                    self.send(u, kind).start()

                self.send(u, "x").start()
                self.send(u, "core").start()

    def from_x(self, hop):
        place = self.place
        for z in (place.z - hop, place.z + hop)[: 1 + min(hop, 1)]:

            @pl.when((z >= 0) & (z < place.depth))
            def _(z=z):
                u = place.unit(z, 1 - place.x, place.core)
                self.send(u, "core").wait_recv()
                self.send(u, "core").start()

    def from_core(self):
        place = self.place
        for z in range(place.depth):
            for x in range(2):
                self.send(place.unit(z, x, 1 - place.core), "core").wait_recv()
        self.put().wait()

    def stages(self):
        def at_hop(hop):
            if hop < self.place.depth:
                self.from_z(hop)
            self.from_x(hop - 1)

        out = [self.spread]
        out += [lambda hop=hop: at_hop(hop) for hop in range(1, self.place.depth + 1)]
        return out + [self.from_core]

    def drain(self):
        place = self.place
        for z in range(place.depth):
            u = place.unit(z, place.x, place.core)
            self.send(u, "x").wait_send()
            self.send(u, "core").wait_send()

            @pl.when((place.z >= z) & self.has_right)
            def _(u=u):
                self.send(u, "right").wait_send()

            @pl.when((place.z <= z) & self.has_left)
            def _(u=u):
                self.send(u, "left").wait_send()

            self.send(place.unit(z, 1 - place.x, place.core), "core").wait_send()


PARTS = 2


def gather_parts(place, pair, full, sems):
    size = full.shape[1] // PARTS
    out = []
    for at in range(PARTS):
        span = slice(at * size, (at + 1) * size)
        out.append(Gather(place, pair.at[:, span], full.at[:, span], sems[3 * at : 3 * at + 3]))
    return out


class Scatter:
    def __init__(self, place, full, scratch, source=None):
        self.place, self.full = place, full
        self.source = full if source is None else source
        self.core_buf, self.x_send, self.x_buf, self.z_send, self.z_buf = scratch[:5]
        self.y_send, self.y_buf = scratch[5:7]
        self.core_sem, self.x_sem, self.z_sem, self.y_sem = scratch[7:]
        self.rows = self.x_send.shape[1]
        self.order = place.hops + [0]

    @staticmethod
    def scratch(own_rows, columns, units, lead=()):
        depth, unit = units // 4, (2 * own_rows, columns)
        edge = lead + (own_rows + -own_rows % 16, columns)
        return [
            pltpu.VMEM(lead + (2, depth) + unit, low_type),
            pltpu.VMEM(lead + (depth,) + unit, low_type),
            pltpu.VMEM(lead + (depth,) + unit, low_type),
            pltpu.VMEM(lead + (depth,) + unit, low_type),
            pltpu.VMEM(lead + (depth,) + unit, low_type),
            pltpu.VMEM(edge, low_type),
            pltpu.VMEM(edge, low_type),
            DMA(lead + (2, 2, depth)),
            DMA(lead + (2, depth)),
            DMA(lead + (2, depth)),
            DMA(lead + (2,)),
        ]

    def at(self, ref, z, x, core):
        u = self.place.unit(z, x, core)
        return ref.at[pl.ds(pl.multiple_of(u * self.rows, 16), self.rows)]

    def x_of(self, side):
        return self.place.x if side == 0 else 1 - self.place.x

    def to_core(self, side, hop):
        place = self.place
        return remote(
            self.at(self.source, place.z_after(hop), self.x_of(side), 1 - place.core),
            self.core_buf.at[side, hop],
            self.core_sem.at[0, side, hop],
            self.core_sem.at[1, side, hop],
            place.over_core(),
        )

    def to_x(self, hop):
        return remote(
            self.x_send.at[hop],
            self.x_buf.at[hop],
            self.x_sem.at[0, hop],
            self.x_sem.at[1, hop],
            self.place.over_x(),
        )

    def to_z(self, hop):
        return remote(
            self.z_send.at[hop],
            self.z_buf.at[hop],
            self.z_sem.at[0, hop],
            self.z_sem.at[1, hop],
            self.place.along_z(hop),
        )

    def to_y(self):
        return remote(
            self.y_send, self.y_buf, self.y_sem.at[0], self.y_sem.at[1], self.place.over_y()
        )

    def start(self):
        for side in (1, 0):
            for hop in self.order:
                self.to_core(side, hop).start()

    def mine(self, side, hop):
        place = self.place
        self.to_core(side, hop).wait_recv()
        own = self.at(self.full, place.z_after(hop), self.x_of(side), place.core)
        return own[...].astype(f32) + self.core_buf[side, hop].astype(f32)

    def stage_x(self, hop):
        self.x_send[hop] = self.mine(1, hop).astype(low_type)
        self.to_x(hop).start()

    def stage_z(self, hop):
        part = self.mine(0, hop)
        self.to_x(hop).wait_recv()
        part = part + self.x_buf[hop].astype(f32)
        self.z_send[hop] = part.astype(low_type)
        if hop:
            self.to_z(hop).start()

    def stage_y(self):
        total = self.z_send[0].astype(f32)
        for hop in self.place.hops:
            self.to_z(hop).wait_recv()
            total = total + self.z_buf[hop].astype(f32)
        half = self.rows // 2
        first = self.place.y == 0
        self.y_send[:half] = jnp.where(first, total[half:], total[:half]).astype(low_type)
        self.to_y().start()
        return jnp.where(first, total[:half], total[half:])

    def finish(self, kept):
        self.to_y().wait()
        return kept + self.y_buf[: kept.shape[0]].astype(f32)

    def drain(self):
        for hop in self.order:
            for side in (1, 0):
                self.to_core(side, hop).wait_send()
            self.to_x(hop).wait_send()
            if hop:
                self.to_z(hop).wait_send()


class Exchange:
    def __init__(self, place, send, recv, sem):
        self.send, self.recv, self.sem = send, recv, sem
        self.targets = [place.over_core(), place.over_x(), place.over_y()]
        span = 1
        while span < place.depth:
            flip = place.z + span - 2 * span * lax.rem(place.z // span, 2)
            self.targets.append((place.unit(flip, place.x, place.core), place.y))
            span *= 2

    @staticmethod
    def rounds(units):
        return 3 + (units // 4 - 1).bit_length()

    @staticmethod
    def scratch(shape, units):
        rounds = Exchange.rounds(units)
        return [
            pltpu.VMEM((rounds,) + shape, f32),
            pltpu.VMEM((rounds,) + shape, f32),
            DMA((2, rounds)),
        ]

    def copy(self, at):
        return remote(
            self.send.at[at], self.recv.at[at], self.sem.at[0, at], self.sem.at[1, at], self.targets[at]
        )

    def start(self, at, value):
        self.send[at] = value
        self.copy(at).start()

    def finish(self, at):
        self.copy(at).wait()
        return self.send[at] + self.recv[at]


def comm_params(collective):
    return pltpu.CompilerParams(
        collective_id=collective, has_side_effects=True, vmem_limit_bytes=VMEM
    )


def first_kernel(
    wq_ref,
    wk_ref,
    wv_ref,
    gains_ref,
    second_refs,
    tokens_ref,
    q_ref,
    k_ref,
    v_ref,
    x_ref,
    w_ref,
    gain_ref,
    second_pair,
    w_all,
    x_in,
    low_here,
    stage,
    pair,
    *rest,
):
    swap_sem, load_sem, save_sem, stage_sem, w_sem = rest[21:]
    place = Place()
    per, seq, width = x_ref.shape
    rows = tokens_ref.shape[1]
    spans = (slice(2 * width, w_all.shape[1]), slice(width, 2 * width), slice(0, width))
    meets = [Meet(place, *rest[3 * at : 3 * at + 3]) for at in range(3)]
    second_meet = Meet(place, *rest[9:12])
    gathers = [
        Gather(place, pair.at[:, span], w_all.at[:, span], rest[12 + 3 * at : 15 + 3 * at])
        for at, span in enumerate(spans)
    ]
    place.greet()

    def swap(doc):
        return remote(
            tokens_ref.at[(1 - place.y) * per + doc],
            x_in.at[per + doc],
            swap_sem.at[0, doc],
            swap_sem.at[1, doc],
            place.over_y(),
        )

    def load(doc):
        return pltpu.make_async_copy(
            tokens_ref.at[place.y * per + doc], x_in.at[doc], load_sem.at[doc]
        )

    def start_of(block):
        y = jnp.where(block < per, place.y, 1 - place.y)
        return pl.multiple_of(y * rows, 16)

    def save(block):
        return pltpu.make_async_copy(
            x_in.at[block],
            x_ref.at[lax.rem(block, per), pl.ds(start_of(block), rows)],
            save_sem.at[block],
        )

    def store(block, index):
        target = (q_ref, k_ref, v_ref)[index]
        begin = pl.multiple_of(lax.rem(block, per) * seq + start_of(block), 16)
        slot = lax.rem(block, 2)
        return pltpu.make_async_copy(
            stage.at[slot, index], target.at[pl.ds(begin, rows)], stage_sem.at[slot, index]
        )

    for meet, parts in zip(meets, ((wv_ref, gains_ref), (wk_ref,), (wq_ref,))):
        meet.start(parts)
    for doc in range(per):
        load(doc).start()
        swap(doc).start()
    stages = [gather.stages() for gather in gathers]
    for at in range(3):
        meets[at].finish(pair.at[:, spans[at]])
        stages[at][0]()
    out_ref, in_ref, down_ref = second_refs
    second_meet.start([out_ref] + hidden_parts(in_ref, down_ref, 0, AHEAD))
    for index in range(1, place.depth):
        for at in range(3):
            stages[at][index]()

    def put_stage(block, index, part):
        if index == 0:
            part = part * (0.125 * LOG2E)
        stage[lax.rem(block, 2), index] = part.astype(low_type)
        store(block, index).start()

    def own_rows(at, index):
        for later in range(place.depth, len(stages[at])):
            stages[at][later]()
        if at == 0:
            gain_ref[...] = w_all[:, 3 * width :].astype(f32).T[: gain_ref.shape[0]]

        def project(block, _):
            if at == 0:
                load(block).wait()
                save(block).start()
                normed, _ = norm_rows(x_in[block].astype(f32))
                low_here[block] = (normed * gain_ref[0:1]).astype(low_type)

            @pl.when(block >= 2)
            def _():
                store(block - 2, index).wait()

            columns = w_all[:, index * width : (index + 1) * width]
            put_stage(block, index, dot(low_here[block], columns))
            return 0

        lax.fori_loop(0, per, project, 0)

    for at, index in ((0, 2), (1, 1), (2, 0)):
        own_rows(at, index)
    keep = pltpu.make_async_copy(w_all, w_ref, w_sem)
    keep.start()

    def project(block, _):
        swap(block - per).wait_recv()
        save(block).start()
        normed, _ = norm_rows(x_in[block].astype(f32))
        low = (normed * gain_ref[0:1]).astype(low_type)
        for index in (2, 1, 0):

            @pl.when(block >= 2)
            def _(index=index):
                store(block - 2, index).wait()

            put_stage(block, index, dot(low, w_all[:, index * width : (index + 1) * width]))
        return 0

    lax.fori_loop(per, 2 * per, project, 0)
    second_meet.finish(second_pair)
    for block in range(2 * per):
        save(block).wait()
        if block >= 2 * per - 2:
            for index in range(3):
                store(block, index).wait()
    keep.wait()
    for gather in gathers:
        gather.drain()
    for doc in range(per):
        swap(doc).wait_send()


def first_call(firsts, gains, seconds, tokens, ways):
    units = lax.axis_size("dp")
    count, rows, width = tokens.shape
    own_rows = gains.shape[0]
    columns = sum(w.shape[1] for w in firsts) + gains.shape[1]
    second_columns = width + AHEAD * 2 * (seconds[1].shape[1] // CHUNKS)
    per = count // ways
    total = per * rows * ways

    def kernel(*refs):
        begin = len(firsts) + 1
        end = begin + len(seconds)
        first_kernel(*refs[:begin], refs[begin:end], *refs[end:])

    return pl.pallas_call(
        kernel,
        in_specs=[VMEM_WHOLE] * (len(firsts) + 1 + len(seconds)) + [ANY],
        out_specs=[ANY] * 5 + [VMEM_WHOLE] * 2,
        out_shape=[struct((total, width))] * 3
        + [
            struct((per, rows * ways, width)),
            struct((units * ways * own_rows, columns)),
            struct((8, width), f32),
            struct((ways * own_rows, second_columns)),
        ],
        scratch_shapes=[
            pltpu.VMEM((units * ways * own_rows, columns), low_type),
            pltpu.VMEM((2 * per, rows, width), low_type),
            pltpu.VMEM((per, rows, width), low_type),
            pltpu.VMEM((2, 3, rows, width), low_type),
            pltpu.VMEM((ways * own_rows, columns), low_type),
        ]
        + Meet.scratch(own_rows, columns - 2 * width)
        + 2 * Meet.scratch(own_rows, width)
        + Meet.scratch(own_rows, second_columns)
        + 3 * Gather.scratch(units)
        + [DMA((2, per)), DMA((per,)), DMA((2 * per,)), DMA((2, 3)), DMA],
        compiler_params=comm_params(1),
        name="first",
    )(*firsts, gains, *seconds, tokens)


def attend_send_kernel(
    len_ref,
    table_ref,
    q_ref,
    k_ref,
    v_ref,
    pair_ref,
    in_ref,
    down_ref,
    cot_ref,
    o_ref,
    lse_ref,
    w_ref,
    late_pair,
    cot_doc,
    near_ref,
    cot_in,
    *rest,
    rows,
):
    place = Place()
    gathers = gather_parts(place, pair_ref, w_ref, rest[:-5])
    meet = Meet(place, *rest[-5:-2])
    swap_sem, load_sem = rest[-2:]
    per, part = cot_doc.shape[0], cot_ref.shape[1]
    step = pl.program_id(0) * pl.num_programs(1) + pl.program_id(1)
    last = pl.num_programs(0) * pl.num_programs(1) - 1
    stages = [gather.stages() for gather in gathers]

    def swap(doc):
        return remote(
            cot_ref.at[(1 - place.y) * per + doc],
            cot_doc.at[doc, pl.ds(pl.multiple_of(place.y * part, 16), part)],
            swap_sem.at[0, doc],
            swap_sem.at[1, doc],
            place.over_y(),
        )

    def load(doc):
        return pltpu.make_async_copy(
            cot_ref.at[place.y * per + doc], cot_in.at[doc], load_sem.at[0, doc]
        )

    def save(doc):
        return pltpu.make_async_copy(
            cot_in.at[doc],
            cot_doc.at[doc, pl.ds(pl.multiple_of(place.y * part, 16), part)],
            load_sem.at[1, doc],
        )

    @pl.when(step == 0)
    def _():
        place.greet()
        for doc in range(per):
            load(doc).start()

    for at, piece, index in SEND_PLAN:

        @pl.when(step == at)
        def _(piece=piece, index=index):
            stages[piece][index]()

    @pl.when(step == 1)
    def _():
        for doc in range(per):
            swap(doc).start()
            load(doc).wait()
            save(doc).start()
        meet.start(hidden_parts(in_ref, down_ref, AHEAD, CHUNKS))

    attend_kernel(len_ref, table_ref, q_ref, k_ref, v_ref, o_ref, lse_ref, near_ref, rows=rows)

    @pl.when(step == last)
    def _():
        done = {(piece, index) for _, piece, index in SEND_PLAN}
        for index in range(len(stages[0])):
            for piece in range(PARTS):
                if (piece, index) not in done:
                    stages[piece][index]()
        meet.finish(late_pair)
        for gather in gathers:
            gather.drain()
        for doc in range(per):
            save(doc).wait()
            swap(doc).wait()


SEND_PLAN = (
    (0, 0, 0), (1, 1, 0), (3, 0, 1), (4, 1, 1), (5, 0, 2), (6, 1, 2),
    (7, 0, 3), (8, 1, 3), (9, 0, 4), (10, 1, 4), (11, 0, 5),
)


def attend_send_call(lengths, table, q, k, v, pair, w_in, w_down, cot, rows=512):
    units = lax.axis_size("dp")
    docs, (total, width) = lengths.shape[0], q.shape
    seq, pairs = total // docs, width // 128
    late = (CHUNKS - AHEAD) * 2 * (w_in.shape[1] // CHUNKS)
    slab = pl.BlockSpec((seq, 128), lambda p, d: (d, p))
    return pl.pallas_call(
        functools.partial(attend_send_kernel, rows=rows),
        grid=(pairs, docs),
        in_specs=[SMEM, SMEM, slab, slab, slab]
        + [whole(operand.shape) for operand in (pair, w_in, w_down)]
        + [ANY],
        out_specs=[
            slab,
            pl.BlockSpec((1, 1, 2, seq), lambda p, d: (d, p, 0, 0)),
            ANY,
            whole((pair.shape[0], late)),
            ANY,
        ],
        out_shape=[
            struct((total, width)),
            struct((docs, pairs, 2, seq), f32),
            struct((units * pair.shape[0], pair.shape[1])),
            struct((pair.shape[0], late)),
            struct((docs, seq, width)),
        ],
        scratch_shapes=[
            pltpu.VMEM((2, 3, SUB, SUB), f32),
            pltpu.VMEM((docs, cot.shape[1], width), low_type),
        ]
        + PARTS * Gather.scratch(units)
        + Meet.scratch(w_in.shape[0], late)
        + [DMA((2, docs)), DMA((2, docs))],
        compiler_params=comm_params(3),
        name="attend",
    )(lengths, table, q, k, v, pair, w_in, w_down, cot)


def back_send_kernel(
    len_ref,
    table_ref,
    q_ref,
    k_ref,
    v_ref,
    grad_ref,
    o_ref,
    lse_ref,
    g_ref,
    mixed_ref,
    dq_ref,
    dk_ref,
    dv_ref,
    table_sum,
    gw_ref,
    mixed_out,
    near_ref,
    near_sum,
    far_sum,
    acc,
    grads,
    mixed_in,
    kept,
    *rest,
    keys,
    queries,
    steps,
):
    place = Place()
    size = grads.shape[1] // CHUNKS
    grads_sem, swap_sem, load_sem = rest[11:]

    def scatter(at):
        span = pl.ds(pl.multiple_of(at * size, 128), size)
        return Scatter(
            place, grads.at[:, span], [ref.at[at] for ref in rest[:11]], g_ref.at[:, span]
        )

    per, part = mixed_ref.shape[0], mixed_out.shape[1]
    step = pl.program_id(0) * pl.num_programs(1) + pl.program_id(1)
    last = pl.num_programs(0) * pl.num_programs(1) - 1

    def swap(doc):
        return remote(
            mixed_ref.at[doc, pl.ds(pl.multiple_of((1 - place.y) * part, 16), part)],
            mixed_out.at[place.y * per + doc],
            swap_sem.at[0, doc],
            swap_sem.at[1, doc],
            place.over_y(),
        )

    def load(doc):
        return pltpu.make_async_copy(
            mixed_ref.at[doc, pl.ds(pl.multiple_of(place.y * part, 16), part)],
            mixed_in.at[doc],
            load_sem.at[0, doc],
        )

    def save(doc):
        return pltpu.make_async_copy(
            mixed_in.at[doc], mixed_out.at[place.y * per + doc], load_sem.at[1, doc]
        )

    take = pltpu.make_async_copy(g_ref, grads, grads_sem)

    @pl.when(step == 0)
    def _():
        place.greet()
        for at in range(CHUNKS):
            scatter(at).start()
        take.start()
        for doc in range(per):
            load(doc).start()
            swap(doc).start()

    @pl.when(step == 1)
    def _():
        take.wait()

    def every_other(first, work):
        at = (step - first) // 2

        @pl.when((step >= first) & (at < CHUNKS) & (step == first + 2 * at))
        def _():
            work(at)

    def x_stages(at):
        for hop in place.hops + [0]:
            scatter(at).stage_x(hop)

    def z_stages(at):
        for hop in place.hops + [0]:
            scatter(at).stage_z(hop)

    def y_stage(at):
        kept[at] = scatter(at).stage_y()

    def finish(at):
        gw_ref[:, pl.ds(pl.multiple_of(at * size, 128), size)] = scatter(at).finish(kept[at])

    every_other(1, x_stages)
    every_other(3, z_stages)
    every_other(5, y_stage)
    every_other(6, finish)

    @pl.when(step == 3)
    def _():
        for doc in range(per):
            load(doc).wait()
            save(doc).start()

    attend_back_kernel(
        len_ref,
        table_ref,
        q_ref,
        k_ref,
        v_ref,
        grad_ref,
        o_ref,
        lse_ref,
        dq_ref,
        dk_ref,
        dv_ref,
        table_sum,
        near_ref,
        near_sum,
        far_sum,
        acc,
        keys=keys,
        queries=queries,
    )

    @pl.when(step == last)
    def _():
        for at in range(CHUNKS):
            for first, work in ((1, x_stages), (3, z_stages), (5, y_stage), (6, finish)):
                if first + 2 * at >= steps:
                    work(at)
        for at in range(CHUNKS):
            scatter(at).drain()
        for doc in range(per):
            save(doc).wait()
            swap(doc).wait()


def back_send_call(lengths, table, q, k, v, grad, o, lse, g, mixed, keys=512, queries=1024):
    units = lax.axis_size("dp")
    docs, (total, width) = lengths.shape[0], q.shape
    seq, pairs = total // docs, width // 128
    columns = g.shape[1]
    own = g.shape[0] // (2 * units)
    slab = pl.BlockSpec((seq, 128), lambda p, d: (d, p))
    return pl.pallas_call(
        functools.partial(
            back_send_kernel, keys=keys, queries=min(queries, seq), steps=pairs * docs
        ),
        grid=(pairs, docs),
        in_specs=[
            SMEM,
            SMEM,
            slab,
            slab,
            slab,
            slab,
            slab,
            pl.BlockSpec((1, 1, 2, seq), lambda p, d: (d, p, 0, 0)),
            ANY,
            ANY,
        ],
        out_specs=[
            slab,
            slab,
            slab,
            pl.BlockSpec((1, 2, BAND), lambda p, d: (p, 0, 0)),
            whole((own, columns)),
            ANY,
        ],
        out_shape=[struct((total, width))] * 3
        + [
            struct((pairs, 2, BAND), f32),
            struct((own, columns), f32),
            struct((2 * docs, seq // 2, width)),
        ],
        scratch_shapes=back_scratch(seq)
        + [
            pltpu.VMEM(g.shape, low_type),
            pltpu.VMEM((docs, seq // 2, width), low_type),
            pltpu.VMEM((CHUNKS, own, columns // CHUNKS), f32),
        ]
        + Scatter.scratch(own, columns // CHUNKS, units, (CHUNKS,))
        + [DMA, DMA((2, docs)), DMA((2, docs))],
        compiler_params=comm_params(4),
        name="attend_back",
    )(lengths, table, q, k, v, grad, o, lse, g, mixed.reshape(docs, seq, width))


def end_kernel(
    x_ref,
    dq_ref,
    dk_ref,
    dv_ref,
    mid_ref,
    w_ref,
    gain_ref,
    table_ref,
    wq_ref,
    wk_ref,
    wv_ref,
    w_in_ref,
    g_hidden_ref,
    g_out,
    gw_ref,
    gt_ref,
    small_ref,
    gains_ref,
    rows_in,
    low_all,
    grads,
    gt,
    *rest,
):
    place = Place()
    count, rows, width = gt_ref.shape
    per = count // 2
    seq = 2 * rows
    scatter_refs, kept = rest[:11], rest[11]
    small_send, small_recv, small_sem, load_sem, gt_sem = rest[12:]
    exchange = Exchange(place, small_send, small_recv, small_sem)
    sources = (x_ref, dq_ref, dk_ref, dv_ref, mid_ref)

    def scatter(at):
        return Scatter(place, grads.at[at], [ref.at[at] for ref in scatter_refs])

    def load(block, index):
        y = jnp.where(block < per, 1 - place.y, place.y)
        begin = pl.multiple_of(lax.rem(block, per) * seq + y * rows, 16)
        return pltpu.make_async_copy(
            sources[index].at[pl.ds(begin, rows)],
            rows_in.at[index, block],
            load_sem.at[block, index],
        )

    def give_away(block):
        return remote(
            gt.at[block],
            gt_ref.at[place.y * per + block],
            gt_sem.at[0, block],
            gt_sem.at[1, block],
            place.over_y(),
        )

    def give_home(block):
        return pltpu.make_async_copy(
            gt.at[block], gt_ref.at[place.y * per + block - per], gt_sem.at[0, block]
        )

    take = pltpu.make_async_copy(g_out, grads.at[0], load_sem.at[2 * per, 0])
    for index in range(5):
        load(0, index).start()
    take.start()
    for index in range(5):
        for block in range(1, 2 * per):
            load(block, index).start()
    place.greet()
    gain = gain_ref[0:1]
    take.wait()
    scatter(0).start()
    heads = table_ref.shape[0]
    small_send[0] = jnp.zeros(small_ref.shape, f32)
    small_send[0, :heads] = bucket_sums(table_ref[...], 32)
    exchange.copy(0).start()
    chunk = g_hidden_ref.shape[1] // (2 * CHUNKS)
    sum_second = jnp.zeros((gains_ref.shape[0], chunk), f32)
    for at in range(CHUNKS):
        sum_second += (
            g_hidden_ref[:, 2 * at * chunk : (2 * at + 1) * chunk]
            * w_in_ref[:, at * chunk : (at + 1) * chunk].astype(f32)
        )
    rounds = len(exchange.targets)

    def exchange_round(at):
        value = exchange.finish(at)
        if at < rounds - 1:
            exchange.start(at + 1, value)
        else:
            small_ref[...] = value

    def low_rows(block, _):
        @pl.when(block > 0)
        def _():
            load(block, 0).wait()

        normed, _ = norm_rows(rows_in[0, block].astype(f32))
        low_all[block] = (normed * gain).astype(low_type)
        return 0

    def rows_back(block):
        normed, inverse = norm_rows(rows_in[0, block].astype(f32))
        normed_grad = None
        for index in range(3):
            part = dot(
                rows_in[1 + index, block], w_ref[:, index * width : (index + 1) * width], NT
            )
            normed_grad = part if normed_grad is None else normed_grad + part
        scaled = normed_grad * gain
        inner = jnp.mean(scaled * normed, -1, keepdims=True)
        mid = rows_in[4, block].astype(f32)
        gt[block] = (mid + inverse * (scaled - normed * inner)).astype(low_type)

        @pl.when(block < per)
        def _():
            give_away(block).start()

        @pl.when(block >= per)
        def _():
            give_home(block).start()

    def weights_back(at):
        grads[at] = dot(
            low_all[...].reshape(2 * per * rows, width),
            rows_in[at].reshape(2 * per * rows, width),
            TN,
        ).astype(low_type)
        scatter(at).start()

    def during(at, first, last, work):
        @pl.when((at >= first) & (at <= last))
        def _():
            work(at)

    def x_stages(at):
        for hop in place.hops + [0]:
            scatter(at).stage_x(hop)

    def z_stages(at):
        for hop in place.hops + [0]:
            scatter(at).stage_z(hop)

    def y_stage(at):
        kept[at] = scatter(at).stage_y()

    def finish(at):
        gw_ref[at] = scatter(at).finish(kept[at])

    def project_step(at, _):
        weights_back(at)
        x_stages(at - 1)
        for index in range(2):
            during(at, index + 2, index + 2, lambda _, index=index: exchange_round(index))
        return 0

    def rows_step(block, _):
        rows_back(block)
        during(block, 1, 1, lambda _: x_stages(3))
        during(block, 1, 1, lambda _: z_stages(0))
        during(block, 1, 3, z_stages)
        during(block - 2, 0, 0, y_stage)
        during(block - 1, 1, 2, y_stage)
        during(block - 3, 0, 0, finish)
        for index in range(2, rounds):
            during(block, index - 1, index - 1, lambda _, index=index: exchange_round(index))
        return 0

    for index in range(5):
        load(0, index).wait()
    rows_back(0)
    lax.fori_loop(0, 2 * per, low_rows, 0)
    for index in range(1, 5):
        for block in range(1, 2 * per):
            load(block, index).wait()
    lax.fori_loop(1, 4, project_step, 0)
    lax.fori_loop(1, 2 * per, rows_step, 0)
    y_stage(3)
    finish(1)
    finish(2)
    finish(3)
    sum_first = jnp.zeros((gains_ref.shape[0], width), f32)
    for at, ref in enumerate((wq_ref, wk_ref, wv_ref)):
        sum_first += gw_ref[1 + at] * ref[...].astype(f32)
    lane = lax.broadcasted_iota(jnp.int32, (1, 128), 1)
    gains_ref[...] = jnp.where(
        lane == 0,
        jnp.sum(sum_first, 1, keepdims=True),
        jnp.sum(sum_second, 1, keepdims=True),
    )

    def drain(at, _):
        scatter(at).drain()
        return 0

    lax.fori_loop(0, 4, drain, 0)
    for block in range(per):
        give_away(block).wait()
        give_home(per + block).wait()


def end_call(x, dq, dk, dv, mid, w_first, gains, table, own_weights, g_hidden, g_out, docs, ways):
    units = lax.axis_size("dp")
    total, width = x.shape
    own = width // (units * ways)
    rows = total // (docs * ways)
    small = (table.shape[0] + -table.shape[0] % 8, 128)
    return pl.pallas_call(
        end_kernel,
        in_specs=[ANY] * 5 + [VMEM_WHOLE] * 8 + [ANY],
        out_specs=[VMEM_WHOLE, ANY, VMEM_WHOLE, VMEM_WHOLE],
        out_shape=[
            struct((4, own, width), f32),
            struct((docs * ways, rows, width)),
            struct(small, f32),
            struct((own, 128), f32),
        ],
        scratch_shapes=[
            pltpu.VMEM((5, docs * ways, rows, width), low_type),
            pltpu.VMEM((docs * ways, rows, width), low_type),
            pltpu.VMEM((4, width, width), low_type),
            pltpu.VMEM((docs * ways, rows, width), low_type),
        ]
        + Scatter.scratch(own, width, units, (4,))
        + [pltpu.VMEM((4, own, width), f32)]
        + Exchange.scratch(small, units)
        + [DMA((docs * ways + 1, 5)), DMA((2, docs * ways))],
        compiler_params=comm_params(2),
        name="end",
    )(x, dq, dk, dv, mid, w_first, gains, table, *own_weights, g_hidden, g_out)


def sharing(count):
    ways = lax.axis_size("blk")
    return max(1, count // ways), max(1, ways // count)


def to_documents(x):
    count, rows, width = x.shape
    ways, me = lax.axis_size("blk"), lax.axis_index("blk")
    per, share = sharing(count)
    if share > 1:
        everything = lax.all_gather(x, "blk", axis=1, tiled=True)
        return lax.dynamic_index_in_dim(everything, me // share, 0, keepdims=False)
    out = jnp.zeros((per, ways * rows, width), x.dtype)
    for hop in range(ways):
        piece = lax.dynamic_slice_in_dim(x, lax.rem(me + hop, ways) * per, per, 0)
        if hop:
            piece = lax.ppermute(piece, "blk", [(i, (i + hop) % ways) for i in range(ways)])
        source = lax.rem(me - hop + ways, ways)
        out = lax.dynamic_update_slice_in_dim(out, piece, source * rows, 1)
    return out.reshape(per * ways * rows, width)


def from_documents(y, count):
    ways, me = lax.axis_size("blk"), lax.axis_index("blk")
    per, share = sharing(count)
    width = y.shape[1]
    if share > 1:
        everything = lax.all_gather(y, "blk", axis=0, tiled=True).reshape(count, -1, width)
        rows = everything.shape[1] // ways
        return lax.dynamic_slice_in_dim(everything, me * rows, rows, 1)
    y = y.reshape(per, -1, width)
    rows = y.shape[1] // ways
    out = jnp.zeros((count, rows, width), y.dtype)
    for hop in range(ways):
        piece = lax.dynamic_slice_in_dim(y, lax.rem(me + hop, ways) * rows, rows, 1)
        if hop:
            piece = lax.ppermute(piece, "blk", [(i, (i + hop) % ways) for i in range(ways)])
        source = lax.rem(me - hop + ways, ways)
        out = lax.dynamic_update_slice_in_dim(out, piece, source * per, 0)
    return out


def among(y, share, split, concat):
    if share == 1:
        return y
    ways = lax.axis_size("blk")
    groups = [list(range(at, at + share)) for at in range(0, ways, share)]
    return lax.all_to_all(
        y, "blk", split, concat, axis_index_groups=groups, tiled=True
    )


def my_share(y, share, axis):
    if share == 1:
        return y
    size = y.shape[axis] // share
    at = lax.rem(lax.axis_index("blk"), share) * size
    return lax.dynamic_slice_in_dim(y, at, size, axis)


def body(
    tokens,
    lengths,
    norm1_gain,
    w_query,
    w_key,
    w_value,
    w_out,
    rel_table,
    norm2_gain,
    w_in,
    w_down,
    cotangent,
):
    micro, docs, rows, width = tokens.shape
    count = micro * docs
    per, share = sharing(count)
    both = ("dp", "blk")
    direct = lax.axis_size("blk") == 2 and per * 2 == count and lax.axis_size("dp") % 4 == 0
    gains = jnp.pad(jnp.stack([norm1_gain, norm2_gain], 1), ((0, 0), (0, SPARE - 2)))
    firsts, seconds = (w_query, w_key, w_value), (w_out, w_in, w_down)
    tokens_here = tokens.reshape(count, rows, width)
    cot_here = cotangent.reshape(count, rows, width)
    if direct:
        q, k, v, x, w_first, gain_rows, pair = first_call(
            firsts, gains, seconds, tokens_here, 2
        )
        x = x.reshape(-1, width)
    else:
        pair = None
        w_second = lax.all_gather(second_pieces(*seconds), both, axis=0, tiled=True)
        w_first = lax.all_gather(
            jnp.concatenate(firsts + (gains,), 1), both, axis=0, tiled=True
        )
        x = to_documents(tokens_here)
        gain_rows = w_first[:, 3 * width : 3 * width + 2].astype(f32).T
    gain_first, gain_second = gain_rows[:1], gain_rows[1:2]
    own = lax.dynamic_slice_in_dim(
        lengths.reshape(count), lax.axis_index("blk") // share * per, per, 0
    )
    x_rows = my_share(x, share, 0)
    own_rows, w_heads = own, w_first
    if share > 1:
        own_rows = own - lax.rem(lax.axis_index("blk"), share) * x_rows.shape[0]
        w_heads = jnp.concatenate(
            [my_share(w_first[:, i * width : (i + 1) * width], share, 1) for i in range(3)], 1
        )
    table = my_share((rel_table * LOG2E).T, share, 0)

    if direct:
        heads, lse, w_second, pair, cot = attend_send_call(
            own, table, q, k, v, pair, w_in, w_down, cot_here
        )
        cot = cot.reshape(-1, width)
    else:
        q, k, v = qkv_call(x, gain_first, w_heads, width // share)
        heads, lse = attend_call(own, table, q, k, v)
        cot = my_share(to_documents(cot_here), share, 0)
    mixed, heads_grad, mid, g_out, g_hidden, gn_second = middle_call(
        own_rows, x_rows, among(heads, share, 0, 1), cot, gain_second, w_second, pair
    )
    if direct:
        dq, dk, dv, table_sum, g_hidden, mixed = back_send_call(
            own, table, q, k, v, heads_grad, heads, lse, g_hidden, mixed
        )
    else:
        dq, dk, dv, table_sum = attend_back_call(
            own, table, q, k, v, among(heads_grad, share, 1, 0), heads, lse
        )
        mixed = from_documents(mixed, count)
        g_out = lax.psum_scatter(g_out, both, scatter_dimension=0, tiled=True).astype(f32)
        g_hidden = lax.psum_scatter(g_hidden, both, scatter_dimension=0, tiled=True).astype(f32)
    dq, dk, dv = (among(grad, share, 0, 1) for grad in (dq, dk, dv))
    head_count, bucket_count = rel_table.shape[1], rel_table.shape[0]
    if direct:
        g_first, grad_tokens, small, gains = end_call(
            x,
            dq,
            dk,
            dv,
            mid,
            w_first,
            gain_rows,
            table_sum.reshape(-1, BAND),
            firsts + (w_in,),
            g_hidden,
            g_out,
            per,
            2,
        )
        grad_table = small[:head_count, :bucket_count].T
        gains = (gains[:, 0] / norm1_gain.astype(f32), gains[:, 1] / norm2_gain.astype(f32))
    else:
        grad_tokens, g_first, gn_first = last_call(
            x_rows, dq, dk, dv, mid, gain_first, w_first
        )
        grad_tokens = from_documents(grad_tokens, count)
        g_first = lax.psum_scatter(g_first, both, scatter_dimension=0, tiled=True).astype(f32)
        gains = lax.psum_scatter(
            jnp.concatenate([gn_first, gn_second], 0), both, scatter_dimension=1, tiled=True
        )
        table_sum = bucket_sums(table_sum.reshape(-1, BAND), bucket_count)[:, :bucket_count]
        if share > 1:
            at = lax.rem(lax.axis_index("blk"), share) * table_sum.shape[0]
            table_sum = lax.dynamic_update_slice_in_dim(
                jnp.zeros(rel_table.T.shape, f32), table_sum, at, 0
            )
        grad_table = lax.psum(table_sum, both).T
    if direct:
        g_out, grad_query, grad_key, grad_value = g_first
    else:
        grad_query, grad_key, grad_value = (
            g_first[:, i * width : (i + 1) * width] for i in range(3)
        )
    grad_in, grad_down = split_hidden(g_hidden)
    return (
        mixed.reshape(tokens.shape),
        grad_tokens.reshape(tokens.shape),
        gains[0],
        grad_query,
        grad_key,
        grad_value,
        g_out,
        grad_table,
        gains[1],
        grad_in,
        grad_down,
    )


def solution(mesh):
    rows = P(None, "dp", "blk", None)
    weight = P(("dp", "blk"), None)
    gain = P(("dp", "blk"))
    return jax.shard_map(
        body,
        mesh=mesh,
        in_specs=(
            rows,
            P(None, "dp"),
            gain,
            weight,
            weight,
            weight,
            weight,
            P(),
            gain,
            weight,
            weight,
            rows,
        ),
        out_specs=(rows, rows, gain, weight, weight, weight, weight, P(), gain, weight, weight),
        check_vma=False,
    )
```

```python
import functools

import jax
import jax.numpy as jnp
from jax import lax
from jax.experimental import pallas as pl
from jax.experimental.pallas import tpu as pltpu
from jax.sharding import PartitionSpec as P

EPS = 1e-06
NEG = -1e30
LIMITS = (12, 16, 23, 32, 46, 64, 91)
SUB = 128
LOG2E = 1.4426950408889634
GELU_A = 0.7978845608028654
GELU_B = 0.044715
VMEM = 62 * 2**20
NN = (((1,), (0,)), ((), ()))
NT = (((1,), (1,)), ((), ()))
TN = (((0,), (0,)), ((), ()))
low_type = jnp.bfloat16
f32 = jnp.float32


def dot(left, right, dims=NN):
    return lax.dot_general(left, right, dims, preferred_element_type=f32)


def bucket_of(relative):
    distance = jnp.abs(relative)
    far_bucket = 8 + sum(((distance >= border).astype(jnp.int32) for border in LIMITS))
    bucket = jnp.where(distance < 8, distance, far_bucket)
    return bucket + 16 * (relative > 0).astype(jnp.int32)


def norm_rows(rows):
    inverse = lax.rsqrt(jnp.mean(rows * rows, -1, keepdims=True) + EPS)
    return rows * inverse, inverse


def whole(shape):
    return pl.BlockSpec(shape, lambda *_: (0,) * len(shape), pipeline_mode=pl.Buffered(1))


def params():
    return pltpu.CompilerParams(vmem_limit_bytes=VMEM)


def struct(shape, dtype=low_type):
    return jax.ShapeDtypeStruct(shape, dtype)


SMEM = pl.BlockSpec(memory_space=pltpu.SMEM)


BAND = 4 * SUB


def band_buckets(keys_are_rows):
    at = lax.broadcasted_iota(jnp.int32, (1, BAND), 1)
    apart = jnp.where(at < 3 * SUB, at, at - BAND) - SUB
    return bucket_of(-apart if keys_are_rows else apart)


def tile_columns(apart, keys_are_rows):
    at = SUB * (1 - apart if keys_are_rows else 1 + apart)
    return slice(at, at + SUB)


def fill_tiles(near, table_ref, pair, keys_are_rows):
    buckets = band_buckets(keys_are_rows)
    for h in range(2):
        line = jnp.zeros((1, BAND), f32)
        for b in range(32):
            line = jnp.where(buckets == b, table_ref[2 * pair + h, b], line)
        band = pltpu.roll(
            jnp.broadcast_to(line, (SUB, BAND)), 0, 1, stride=1, stride_axis=0
        )
        for apart in (-1, 0, 1):
            near[h, apart + 1] = band[:, tile_columns(apart, keys_are_rows)]


def band_sums(tiles):
    band = jnp.concatenate([tiles[2], tiles[1], tiles[0], jnp.zeros((SUB, SUB), f32)], 1)
    out = band[:8]
    for at in range(8, SUB, 8):
        out = out + pltpu.roll(band[at : at + 8], BAND - at, 1)
    row = lax.broadcasted_iota(jnp.int32, out.shape, 0)
    for bit in (1, 2, 4):
        out = jnp.where((row & bit) != 0, pltpu.roll(out, BAND - bit, 1), out)
    return jnp.sum(out, 0, keepdims=True)


def bucket_sums(sums, count):
    buckets = band_buckets(True)
    lane = lax.broadcasted_iota(jnp.int32, (1, SUB), 1)
    out = jnp.zeros((sums.shape[0], SUB), f32)
    for b in range(count):
        part = jnp.sum(jnp.where(buckets == b, sums, 0.0), 1, keepdims=True)
        out = jnp.where(lane == b, part, out)
    return out


def qkv_kernel(x_ref, gain_ref, w_ref, q_ref, k_ref, v_ref):
    width = q_ref.shape[1]
    normed, _ = norm_rows(x_ref[...].astype(f32))
    low = (normed * gain_ref[...]).astype(low_type)
    q_ref[...] = (dot(low, w_ref[:, :width]) * (0.125 * LOG2E)).astype(low_type)
    k_ref[...] = dot(low, w_ref[:, width : 2 * width]).astype(low_type)
    v_ref[...] = dot(low, w_ref[:, 2 * width : 3 * width]).astype(low_type)


def qkv_call(x, gain, w_first, heads_width, rows=512):
    total, width = x.shape
    row = pl.BlockSpec((rows, width), lambda i: (i, 0))
    return pl.pallas_call(
        qkv_kernel,
        grid=(total // rows,),
        in_specs=[row, whole((1, width)), whole(w_first.shape)],
        out_specs=[pl.BlockSpec((rows, heads_width), lambda i: (i, 0))] * 3,
        out_shape=[struct((total, heads_width))] * 3,
        compiler_params=params(),
        name="qkv",
    )(x, gain, w_first)


def attend_kernel(
    len_ref, table_ref, q_ref, k_ref, v_ref, o_ref, lse_ref, near_ref, *, rows
):
    pair, doc = pl.program_id(0), pl.program_id(1)

    @pl.when(doc == 0)
    def _():
        fill_tiles(near_ref, table_ref, pair, False)

    seq = q_ref.shape[0]
    subs = seq // SUB
    first = lax.broadcasted_iota(jnp.int32, (1, 128), 1) < 64
    live = lax.broadcasted_iota(jnp.int32, (1, seq), 1) < len_ref[doc]
    one = jnp.ones((), low_type)
    k, v = k_ref[...], v_ref[...]
    v_ones = (jnp.where(first, v, one), jnp.where(first, one, v))
    for block in range(seq // rows):
        span = slice(block * rows, (block + 1) * rows)
        q = q_ref[span, :]
        outs, tops = [], []
        for h in range(2):
            q_one = jnp.where(first == (h == 0), q, jnp.zeros((), low_type))
            raw = dot(q_one, k, NT)
            strips = []
            for a in range(rows // SUB):
                at = block * (rows // SUB) + a
                strip = raw[a * SUB : (a + 1) * SUB]
                low, high = max(at - 1, 0), min(at + 2, subs)
                parts = []
                if low > 0:
                    parts.append(strip[:, : low * SUB] + table_ref[2 * pair + h, 15])
                for b in range(low, high):
                    parts.append(strip[:, b * SUB : (b + 1) * SUB] + near_ref[h, b - at + 1])
                if high < subs:
                    parts.append(strip[:, high * SUB :] + table_ref[2 * pair + h, 31])
                strips.append(jnp.concatenate(parts, 1))
            scores = jnp.where(live, jnp.concatenate(strips, 0), NEG)
            top = jnp.max(scores, 1, keepdims=True)
            outs.append(dot(jnp.exp2(scores - top).astype(low_type), v_ones[h]))
            tops.append(top)
        total = jnp.where(first, pltpu.roll(outs[0], 64, 1), pltpu.roll(outs[1], 64, 1))
        o_ref[span, :] = (jnp.where(first, outs[0], outs[1]) / total).astype(low_type)
        log_total = (jnp.where(first, tops[0], tops[1]) + jnp.log2(total)).T
        lse_ref[0, 0, 0:1, span] = log_total[0:1]
        lse_ref[0, 0, 1:2, span] = log_total[64:65]


def attend_call(lengths, table, q, k, v, rows=512):
    docs, (total, width) = lengths.shape[0], q.shape
    seq, pairs = total // docs, width // 128
    slab = pl.BlockSpec((seq, 128), lambda p, d: (d, p))
    return pl.pallas_call(
        functools.partial(attend_kernel, rows=rows),
        grid=(pairs, docs),
        in_specs=[
            SMEM,
            SMEM,
            slab,
            slab,
            slab,
        ],
        out_specs=[slab, pl.BlockSpec((1, 1, 2, seq), lambda p, d: (d, p, 0, 0))],
        out_shape=[struct((total, width)), struct((docs, pairs, 2, seq), f32)],
        scratch_shapes=[pltpu.VMEM((2, 3, SUB, SUB), f32)],
        compiler_params=params(),
        name="attend",
    )(lengths, table, q, k, v)


CHUNKS = 4
AHEAD = 2


def second_pieces(w_out, w_in, w_down):
    chunk = w_in.shape[1] // CHUNKS
    parts = [w_out]
    for at in range(0, CHUNKS * chunk, chunk):
        parts += [w_in[:, at : at + chunk], w_down[:, at : at + chunk]]
    return jnp.concatenate(parts, 1)


def split_hidden(grads):
    chunk = grads.shape[1] // (2 * CHUNKS)
    parts = [grads[:, at * chunk : (at + 1) * chunk] for at in range(2 * CHUNKS)]
    return jnp.concatenate(parts[0::2], 1), jnp.concatenate(parts[1::2], 1)


def middle_kernel(
    len_ref,
    x_ref,
    heads_ref,
    cot_ref,
    gain_ref,
    w_out,
    w_hbm,
    mixed_ref,
    hgrad_ref,
    mid_ref,
    g_out,
    g_ref,
    gn_ref,
    scratch,
    *,
    seq,
    before_chunk,
):
    low_all, grad_all, normed_all, inverse_all, mixed_all, back_all = scratch[:6]
    act_all, up_all, g_buf, acc_gain, g_sem, w_all, w_sem = scratch[6:]
    step = pl.program_id(0)
    rows, width = x_ref.shape
    total = low_all.shape[0]
    chunk = w_all.shape[1] // (2 * CHUNKS)
    fine, block = total // rows, MIDDLE_BLOCK
    coarse = total // block
    begin = fine
    finish = fine + CHUNKS * coarse

    @pl.when(step < begin)
    def _():
        span = pl.ds(pl.multiple_of(step * rows, rows), rows)
        per = seq // rows
        place = lax.rem(step, per) * rows + lax.broadcasted_iota(jnp.int32, (rows, 1), 0)
        residual = x_ref[...].astype(f32) + dot(heads_ref[...], w_out[...])
        normed, inverse = norm_rows(residual)
        mixed_all[span, :] = residual
        back_all[span, :] = jnp.zeros_like(residual)
        normed_all[span, :] = normed.astype(low_type)
        inverse_all[span, :] = jnp.broadcast_to(inverse, (rows, 128))
        low_all[span, :] = (normed * gain_ref[...]).astype(low_type)
        grad_all[span, :] = jnp.where(
            place < len_ref[jnp.minimum(step // per, len_ref.shape[0] - 1)],
            cot_ref[...],
            jnp.zeros((), low_type),
        )

    def store(at):
        begins = pl.multiple_of(at * (2 * chunk), 128)
        slot = lax.rem(at, 2)
        return pltpu.make_async_copy(
            g_buf.at[slot], g_ref.at[:, pl.ds(begins, 2 * chunk)], g_sem.at[slot]
        )

    ready = w_hbm.shape[1] - width
    take = pltpu.make_async_copy(w_hbm.at[:, width:], w_all.at[:, :ready], w_sem)

    @pl.when(step == 0)
    def _():
        take.start()

    at = jnp.maximum(step - begin, 0) // coarse

    @pl.when(step == begin)
    def _():
        take.wait()

    for index in range(CHUNKS):

        @pl.when(step == begin + index * coarse)
        def _(index=index):
            before_chunk(index)

    @pl.when((step >= begin) & (step < finish))
    def _():
        span = pl.ds(pl.multiple_of((step - begin - at * coarse) * block, block), block)
        w_up = w_all[:, pl.ds(pl.multiple_of(at * (2 * chunk), 128), chunk)]
        w_down = w_all[:, pl.ds(pl.multiple_of(at * (2 * chunk) + chunk, 128), chunk)]
        u = dot(low_all[span, :], w_up)
        square = u * u
        bend = jnp.tanh(u * (GELU_A + GELU_A * GELU_B * square))
        half = 0.5 + 0.5 * bend
        act = (u * half).astype(low_type)
        slope = half + (0.5 * u) * (1 - bend * bend) * (GELU_A + 3 * GELU_A * GELU_B * square)
        up_grad = (dot(grad_all[span, :], w_down) * slope).astype(low_type)
        act_all[span, :] = act
        up_all[span, :] = up_grad
        mixed_all[span, :] += dot(act, w_down, NT)
        back_all[span, :] += dot(up_grad, w_up, NT)

    @pl.when((step >= begin) & (step < finish) & (step - begin == at * coarse + coarse - 1))
    def _():
        slot = lax.rem(at, 2)

        @pl.when(at >= 2)
        def _():
            store(at - 2).wait()

        g_buf[slot, :, :chunk] = dot(low_all[...], up_all[...], TN).astype(low_type)
        g_buf[slot, :, chunk:] = dot(grad_all[...], act_all[...], TN).astype(low_type)
        store(at).start()

    @pl.when(step >= finish)
    def _():
        span = pl.ds(pl.multiple_of((step - finish) * rows, rows), rows)
        mixed_ref[...] = mixed_all[span, :].astype(low_type)
        normed, back = normed_all[span, :].astype(f32), back_all[span, :]
        scaled = back * gain_ref[...]
        inner = jnp.mean(scaled * normed, -1, keepdims=True)
        inverse = inverse_all[span, :][:, :1]
        mid = grad_all[span, :].astype(f32) + inverse * (scaled - normed * inner)
        mid = mid.astype(low_type)
        part = jnp.sum((back * normed).reshape(rows // 8, 8, width), 0)
        acc_gain[...] = jnp.where(step == finish, part, acc_gain[...] + part)
        mid_ref[...] = mid
        act_all[span, :width] = mid
        up_all[span, :width] = heads_ref[...]
        hgrad_ref[...] = dot(mid, w_out[...], NT).astype(low_type)

    @pl.when(step == pl.num_programs(0) - 1)
    def _():
        g_out[...] = dot(up_all[:, :width], act_all[:, :width], TN).astype(low_type)
        gn_ref[...] = jnp.sum(acc_gain[...], 0, keepdims=True)
        for at in range(CHUNKS - 2, CHUNKS):
            store(at).wait()


MIDDLE_BLOCK = 512


def middle_plain_kernel(*refs, seq):
    w_ref, w_hbm, rest = refs[5], refs[6], refs[7:]
    middle_kernel(
        *refs[:5],
        w_ref,
        w_hbm,
        *rest[:6],
        rest[6:],
        seq=seq,
        before_chunk=lambda at: None,
    )


def middle_send_kernel(*refs, seq):
    w_ref, w_hbm, pair_ref, rest = refs[5], refs[6], refs[7], refs[8:]
    w_all, sems = rest[17], rest[19:]
    place = Place()
    late = w_all.at[:, w_hbm.shape[1] - refs[1].shape[1] :]
    gathers = gather_parts(place, pair_ref, late, sems)
    stages = [gather.stages() for gather in gathers]
    planned = {(part, index) for _, part, index in MIDDLE_PLAN}
    step = pl.program_id(0)

    @pl.when(step == 0)
    def _():
        place.greet()

    for when, part, index in MIDDLE_PLAN:

        @pl.when(step == when)
        def _(part=part, index=index):
            stages[part][index]()

    def before_chunk(at):
        part = (at - AHEAD) * PARTS // (CHUNKS - AHEAD)
        if at >= AHEAD and part * (CHUNKS - AHEAD) == (at - AHEAD) * PARTS:
            for index in range(len(stages[part])):
                if (part, index) not in planned:
                    stages[part][index]()

    middle_kernel(
        *refs[:5],
        w_ref,
        w_hbm,
        *rest[:6],
        rest[6:19],
        seq=seq,
        before_chunk=before_chunk,
    )

    @pl.when(step == pl.num_programs(0) - 1)
    def _():
        for gather in gathers:
            gather.drain()


MIDDLE_PLAN = (
    (0, 0, 0), (5, 0, 1), (7, 0, 2), (9, 0, 3), (10, 0, 4), (11, 0, 5),
    (6, 1, 0), (9, 1, 1), (11, 1, 2), (13, 1, 3), (14, 1, 4), (15, 1, 5),
)


def middle_call(lengths, x, heads, cot, gain, w_second, pair=None, rows=512):
    total, width = x.shape
    columns = w_second.shape[1] + (0 if pair is None else pair.shape[1])
    chunk = (columns - width) // (2 * CHUNKS)
    fine = total // rows
    steps = 2 * fine + CHUNKS * (total // MIDDLE_BLOCK)
    early = pl.BlockSpec((rows, width), lambda i: (jnp.minimum(i, fine - 1), 0))
    late = pl.BlockSpec((rows, width), lambda i: (jnp.maximum(i - (steps - fine), 0), 0))
    ends = pl.BlockSpec(
        (rows, width),
        lambda i: (jnp.where(i < steps - fine, jnp.minimum(i, fine - 1), i - (steps - fine)), 0),
    )
    square = (width, 2 * chunk)
    scratch = [
        pltpu.VMEM((total, width), low_type),
        pltpu.VMEM((total, width), low_type),
        pltpu.VMEM((total, width), low_type),
        pltpu.VMEM((total, 128), f32),
        pltpu.VMEM((total, width), f32),
        pltpu.VMEM((total, width), f32),
        pltpu.VMEM((total, max(chunk, width)), low_type),
        pltpu.VMEM((total, max(chunk, width)), low_type),
        pltpu.VMEM((2,) + square, low_type),
        pltpu.VMEM((8, width), f32),
        DMA((2,)),
        pltpu.VMEM((width, columns - width), low_type),
        DMA,
    ]
    kernel, compiler, operands = middle_plain_kernel, params(), []
    if pair is not None:
        kernel, compiler, operands = middle_send_kernel, comm_params(5), [pair]
        scratch += PARTS * Gather.scratch(lax.axis_size("dp"))
    square_out = (width, width)
    first_block = pl.BlockSpec(
        square_out, lambda i: (0, 0), pipeline_mode=pl.Buffered(1)
    )
    return pl.pallas_call(
        functools.partial(kernel, seq=total // lengths.shape[0]),
        grid=(steps,),
        in_specs=[SMEM, early, ends, early, whole((1, width)), first_block, ANY]
        + [whole(operand.shape) for operand in operands],
        out_specs=[late, late, late, whole(square_out), ANY, whole((1, width))],
        out_shape=[struct((total, width))] * 3
        + [
            struct(square_out),
            struct((width, CHUNKS * 2 * chunk)),
            struct((1, width), f32),
        ],
        scratch_shapes=scratch,
        compiler_params=compiler,
        name="middle",
    )(lengths, x, heads, cot, gain, w_second, w_second, *operands)


def attend_back_kernel(
    len_ref,
    table_ref,
    q_ref,
    k_ref,
    v_ref,
    grad_ref,
    o_ref,
    lse_ref,
    dq_ref,
    dk_ref,
    dv_ref,
    table_sum,
    near_ref,
    near_sum,
    far_sum,
    acc,
    *,
    keys,
    queries,
):
    pair, doc = pl.program_id(0), pl.program_id(1)
    seq = q_ref.shape[0]
    first = lax.broadcasted_iota(jnp.int32, (1, 128), 1) < 64
    zero = jnp.zeros((), low_type)

    def halves(x):
        return jnp.where(first, x, zero), jnp.where(first, zero, x)

    grad = grad_ref[...]
    q_one, g_one = halves(q_ref[...]), halves(grad)
    product = grad.astype(f32) * o_ref[...].astype(f32)
    upper = product.astype(low_type)
    lower = (product - upper.astype(f32)).astype(low_type)
    row = lax.broadcasted_iota(jnp.int32, (16, 128), 0)
    column = lax.broadcasted_iota(jnp.int32, (16, 128), 1)
    member = (row == column // 64).astype(f32).astype(low_type)
    delta = dot(member, upper, NT) + dot(member, lower, NT)

    @pl.when(doc == 0)
    def _():
        fill_tiles(near_ref, table_ref, pair, True)
        near_sum[...] = jnp.zeros_like(near_sum)
        far_sum[...] = jnp.zeros_like(far_sum)

    for kb in range(seq // keys):
        held = slice(kb * keys, (kb + 1) * keys)
        k, v = k_ref[held, :], v_ref[held, :]
        k_turned = k.T
        live = (kb * keys + lax.broadcasted_iota(jnp.int32, (keys, 1), 0)) < len_ref[doc]
        dk = jnp.zeros((keys, 128), f32)
        dv = jnp.zeros((keys, 128), f32)
        for qb in range(seq // queries):
            span = slice(qb * queries, (qb + 1) * queries)
            for h in range(2):
                scores = dot(k, q_one[h][span], NT)
                prob_grad = dot(v, g_one[h][span], NT)
                lse = lse_ref[0, 0, h : h + 1, span]
                lse_side = (lse - table_ref[2 * pair + h, 15], lse - table_ref[2 * pair + h, 31])
                row_delta = delta[h : h + 1, span]
                prob_rows, grad_rows = [], []
                for a in range(keys // SUB):
                    down = slice(a * SUB, (a + 1) * SUB)
                    probs, grads = [], []
                    for b in range(queries // SUB):
                        across = slice(b * SUB, (b + 1) * SUB)
                        apart = kb * (keys // SUB) + a - qb * (queries // SUB) - b
                        tile = scores[down, across]
                        if abs(apart) <= 1:
                            tile = tile + near_ref[h, apart + 1] - lse[:, across]
                        else:
                            tile = tile - lse_side[int(apart > 0)][:, across]
                        prob = jnp.where(live[down], jnp.exp2(tile), 0.0)
                        score_grad = prob * (prob_grad[down, across] - row_delta[:, across])
                        if abs(apart) <= 1:
                            near_sum[h, apart + 1] += score_grad
                        else:
                            far_sum[h, int(apart > 0)] += jnp.sum(
                                score_grad.reshape(SUB // 8, 8, SUB), 0
                            )
                        probs.append(prob.astype(low_type))
                        grads.append(score_grad.astype(low_type))
                    prob_rows.append(jnp.concatenate(probs, 1))
                    grad_rows.append(jnp.concatenate(grads, 1))
                prob_low = jnp.concatenate(prob_rows, 0)
                grad_low = jnp.concatenate(grad_rows, 0)
                dv = dv + dot(prob_low, g_one[h][span])
                dk = dk + dot(grad_low, q_one[h][span])
                side = slice(64 * h, 64 * (h + 1))
                part = dot(k_turned[side], grad_low)
                if kb:
                    part = part + acc[side, span]
                acc[side, span] = part
        dv_ref[held, :] = dv.astype(low_type)
        dk_ref[held, :] = (dk * (1 / LOG2E)).astype(low_type)
    dq_ref[...] = (acc[...] * 0.125).T.astype(low_type)

    @pl.when(doc == pl.num_programs(1) - 1)
    def _():
        lane = lax.broadcasted_iota(jnp.int32, (1, BAND), 1)
        for h in range(2):
            left = jnp.sum(far_sum[h, 0], keepdims=True)
            right = jnp.sum(far_sum[h, 1], keepdims=True)
            sums = band_sums(near_sum[h])
            table_sum[0, h : h + 1] = (
                sums + jnp.where(lane == 3 * SUB - 1, left, 0.0) + jnp.where(lane == 0, right, 0.0)
            )


def attend_back_call(lengths, table, q, k, v, grad, o, lse, keys=512, queries=1024):
    docs, (total, width) = lengths.shape[0], q.shape
    seq, pairs = total // docs, width // 128
    queries = min(queries, seq)
    slab = pl.BlockSpec((seq, 128), lambda p, d: (d, p))
    return pl.pallas_call(
        functools.partial(attend_back_kernel, keys=keys, queries=queries),
        grid=(pairs, docs),
        in_specs=[
            SMEM,
            SMEM,
            slab,
            slab,
            slab,
            slab,
            slab,
            pl.BlockSpec((1, 1, 2, seq), lambda p, d: (d, p, 0, 0)),
        ],
        out_specs=[slab, slab, slab, pl.BlockSpec((1, 2, BAND), lambda p, d: (p, 0, 0))],
        out_shape=[struct((total, width))] * 3 + [struct((pairs, 2, BAND), f32)],
        scratch_shapes=back_scratch(seq),
        compiler_params=params(),
        name="attend_back",
    )(lengths, table, q, k, v, grad, o, lse)


def back_scratch(seq):
    return [
        pltpu.VMEM((2, 3, SUB, SUB), f32),
        pltpu.VMEM((2, 3, SUB, SUB), f32),
        pltpu.VMEM((2, 2, 8, SUB), f32),
        pltpu.VMEM((128, seq), f32),
    ]


def last_kernel(
    x_ref,
    dq_ref,
    dk_ref,
    dv_ref,
    mid_ref,
    gain_ref,
    w_ref,
    gt_ref,
    gw_ref,
    gn_ref,
    acc,
    acc_gain,
):
    step = pl.program_id(0)
    rows, width = x_ref.shape

    @pl.when(step == 0)
    def _():
        acc[...] = jnp.zeros_like(acc)
        acc_gain[...] = jnp.zeros_like(acc_gain)

    gain = gain_ref[...]
    normed, inverse = norm_rows(x_ref[...].astype(f32))
    low = (normed * gain).astype(low_type)
    normed_grad = None
    for index, ref in enumerate((dq_ref, dk_ref, dv_ref)):
        part = slice(index * width, (index + 1) * width)
        grad = ref[...]
        acc[:, part] += dot(low, grad, TN)
        back = dot(grad, w_ref[:, part], NT)
        normed_grad = back if normed_grad is None else normed_grad + back
    acc_gain[...] += jnp.sum((normed_grad * normed).reshape(rows // 8, 8, width), 0)
    scaled = normed_grad * gain
    inner = jnp.mean(scaled * normed, -1, keepdims=True)
    gt_ref[...] = (mid_ref[...].astype(f32) + inverse * (scaled - normed * inner)).astype(low_type)

    @pl.when(step == pl.num_programs(0) - 1)
    def _():
        gw_ref[...] = acc[...].astype(low_type)
        gn_ref[...] = jnp.sum(acc_gain[...], 0, keepdims=True)


def last_call(x, dq, dk, dv, mid, gain, w_first, rows=512):
    total, width = x.shape
    row = pl.BlockSpec((rows, width), lambda i: (i, 0))
    grads = (width, 3 * width)
    return pl.pallas_call(
        last_kernel,
        grid=(total // rows,),
        in_specs=[row] * 5 + [whole((1, width)), whole(w_first.shape)],
        out_specs=[row, whole(grads), whole((1, width))],
        out_shape=[struct((total, width)), struct(grads), struct((1, width), f32)],
        scratch_shapes=[pltpu.VMEM(grads, f32), pltpu.VMEM((8, width), f32)],
        compiler_params=params(),
        name="last",
    )(x, dq, dk, dv, mid, gain, w_first)


MESH_ID = pl.DeviceIdType.MESH
ANY = pl.BlockSpec(memory_space=pl.ANY)
VMEM_WHOLE = pl.BlockSpec(memory_space=pltpu.VMEM)
DMA = pltpu.SemaphoreType.DMA
SPARE = 128


class Place:
    def __init__(self):
        self.dp, self.y = lax.axis_index("dp"), lax.axis_index("blk")
        self.depth = lax.axis_size("dp") // 4
        self.z = self.dp // 4
        self.x = lax.rem(self.dp // 2, 2)
        self.core = lax.rem(self.dp, 2)
        self.hops = sorted(range(1, self.depth), key=lambda hop: min(hop, self.depth - hop))

    def unit(self, z, x, core):
        return (z * 2 + x) * 2 + core

    def z_after(self, hop):
        return lax.rem(self.z + hop, self.depth)

    def z_before(self, hop):
        return lax.rem(self.z + self.depth - hop, self.depth)

    def along_z(self, hop):
        return (self.unit(self.z_after(hop), self.x, self.core), self.y)

    def over_x(self):
        return (self.unit(self.z, 1 - self.x, self.core), self.y)

    def over_core(self):
        return (self.unit(self.z, self.x, 1 - self.core), self.y)

    def over_y(self):
        return (self.dp, 1 - self.y)

    def greet(self):
        barrier = pltpu.get_barrier_semaphore()
        peers = [self.over_x(), self.over_core(), self.over_y()]
        peers += [self.along_z(hop) for hop in self.hops]
        for peer in peers:
            pl.semaphore_signal(barrier, device_id=peer, device_id_type=MESH_ID)
        pl.semaphore_wait(barrier, len(peers))


def remote(source, target, send, recv, device):
    return pltpu.make_async_remote_copy(
        src_ref=source,
        dst_ref=target,
        send_sem=send,
        recv_sem=recv,
        device_id=device,
        device_id_type=MESH_ID,
    )


class Meet:
    def __init__(self, place, shard, other, sem):
        self.place, self.shard, self.other, self.sem = place, shard, other, sem

    @staticmethod
    def scratch(own_rows, columns):
        block = (own_rows + -own_rows % 16, columns)
        return [pltpu.VMEM(block, low_type), pltpu.VMEM(block, low_type), DMA((2,))]

    def copy(self):
        return remote(self.shard, self.other, self.sem.at[0], self.sem.at[1], self.place.over_y())

    def start(self, parts):
        at = 0
        for ref in parts:
            rows, columns = ref.shape
            self.shard[:rows, at : at + columns] = ref[...]
            at += columns
        self.copy().start()

    def finish(self, pair):
        self.copy().wait()
        half = pair.shape[0] // 2
        mine = self.shard[:half].astype(f32)
        theirs = self.other[:half].astype(f32)
        first = self.place.y == 0
        pair[...] = jnp.concatenate(
            [jnp.where(first, mine, theirs), jnp.where(first, theirs, mine)], 0
        ).astype(low_type)


def hidden_parts(in_ref, down_ref, begin, end):
    chunk = in_ref.shape[1] // CHUNKS
    parts = []
    for at in range(begin, end):
        span = slice(at * chunk, (at + 1) * chunk)
        parts += [in_ref.at[:, span], down_ref.at[:, span]]
    return parts


class Gather:
    def __init__(self, place, pair, full, sems):
        self.place, self.pair, self.full = place, pair, full
        self.send_sem, self.recv_sem, self.put_sem = sems
        self.rows = pair.shape[0]
        self.mine = place.unit(place.z, place.x, place.core)
        self.has_left, self.has_right = place.z > 0, place.z < place.depth - 1

    @staticmethod
    def scratch(units):
        return [DMA((units, 4)), DMA((units,)), DMA]

    def at(self, u):
        return self.full.at[pl.ds(pl.multiple_of(u * self.rows, 16), self.rows)]

    def send(self, u, kind, source=None):
        place = self.place
        device = {
            "left": (place.dp - 4, place.y),
            "right": (place.dp + 4, place.y),
            "x": place.over_x(),
            "core": place.over_core(),
        }[kind]
        slot = ("left", "right", "x", "core").index(kind)
        source = self.at(u) if source is None else source
        return remote(source, self.at(u), self.send_sem.at[u, slot], self.recv_sem.at[u], device)

    def put(self):
        return pltpu.make_async_copy(self.pair, self.at(self.mine), self.put_sem)

    def spread(self):
        for kind, there in (("right", self.has_right), ("left", self.has_left)):

            @pl.when(there)
            def _(kind=kind):
                self.send(self.mine, kind, self.pair).start()

        self.send(self.mine, "x", self.pair).start()
        self.send(self.mine, "core", self.pair).start()
        self.put().start()

    def from_z(self, hop):
        place = self.place
        for kind, z, onward in (
            ("right", place.z - hop, self.has_right),
            ("left", place.z + hop, self.has_left),
        ):

            @pl.when((z >= 0) & (z < place.depth))
            def _(kind=kind, z=z, onward=onward):
                u = place.unit(z, place.x, place.core)
                self.send(u, "core").wait_recv()

                @pl.when(onward)
                def _():
                    self.send(u, kind).start()

                self.send(u, "x").start()
                self.send(u, "core").start()

    def from_x(self, hop):
        place = self.place
        for z in (place.z - hop, place.z + hop)[: 1 + min(hop, 1)]:

            @pl.when((z >= 0) & (z < place.depth))
            def _(z=z):
                u = place.unit(z, 1 - place.x, place.core)
                self.send(u, "core").wait_recv()
                self.send(u, "core").start()

    def from_core(self):
        place = self.place
        for z in range(place.depth):
            for x in range(2):
                self.send(place.unit(z, x, 1 - place.core), "core").wait_recv()
        self.put().wait()

    def stages(self):
        def at_hop(hop):
            if hop < self.place.depth:
                self.from_z(hop)
            self.from_x(hop - 1)

        out = [self.spread]
        out += [lambda hop=hop: at_hop(hop) for hop in range(1, self.place.depth + 1)]
        return out + [self.from_core]

    def drain(self):
        place = self.place
        for z in range(place.depth):
            u = place.unit(z, place.x, place.core)
            self.send(u, "x").wait_send()
            self.send(u, "core").wait_send()

            @pl.when((place.z >= z) & self.has_right)
            def _(u=u):
                self.send(u, "right").wait_send()

            @pl.when((place.z <= z) & self.has_left)
            def _(u=u):
                self.send(u, "left").wait_send()

            self.send(place.unit(z, 1 - place.x, place.core), "core").wait_send()


PARTS = 2


def gather_parts(place, pair, full, sems):
    size = full.shape[1] // PARTS
    out = []
    for at in range(PARTS):
        span = slice(at * size, (at + 1) * size)
        out.append(Gather(place, pair.at[:, span], full.at[:, span], sems[3 * at : 3 * at + 3]))
    return out


class Scatter:
    def __init__(self, place, full, scratch, source=None):
        self.place, self.full = place, full
        self.source = full if source is None else source
        self.core_buf, self.x_send, self.x_buf, self.z_send, self.z_buf = scratch[:5]
        self.y_send, self.y_buf = scratch[5:7]
        self.core_sem, self.x_sem, self.z_sem, self.y_sem = scratch[7:]
        self.rows = self.x_send.shape[1]
        self.order = place.hops + [0]

    @staticmethod
    def scratch(own_rows, columns, units, lead=()):
        depth, unit = units // 4, (2 * own_rows, columns)
        edge = lead + (own_rows + -own_rows % 16, columns)
        return [
            pltpu.VMEM(lead + (2, depth) + unit, low_type),
            pltpu.VMEM(lead + (depth,) + unit, low_type),
            pltpu.VMEM(lead + (depth,) + unit, low_type),
            pltpu.VMEM(lead + (depth,) + unit, low_type),
            pltpu.VMEM(lead + (depth,) + unit, low_type),
            pltpu.VMEM(edge, low_type),
            pltpu.VMEM(edge, low_type),
            DMA(lead + (2, 2, depth)),
            DMA(lead + (2, depth)),
            DMA(lead + (2, depth)),
            DMA(lead + (2,)),
        ]

    def at(self, ref, z, x, core):
        u = self.place.unit(z, x, core)
        return ref.at[pl.ds(pl.multiple_of(u * self.rows, 16), self.rows)]

    def x_of(self, side):
        return self.place.x if side == 0 else 1 - self.place.x

    def to_core(self, side, hop):
        place = self.place
        return remote(
            self.at(self.source, place.z_after(hop), self.x_of(side), 1 - place.core),
            self.core_buf.at[side, hop],
            self.core_sem.at[0, side, hop],
            self.core_sem.at[1, side, hop],
            place.over_core(),
        )

    def to_x(self, hop):
        return remote(
            self.x_send.at[hop],
            self.x_buf.at[hop],
            self.x_sem.at[0, hop],
            self.x_sem.at[1, hop],
            self.place.over_x(),
        )

    def to_z(self, hop):
        return remote(
            self.z_send.at[hop],
            self.z_buf.at[hop],
            self.z_sem.at[0, hop],
            self.z_sem.at[1, hop],
            self.place.along_z(hop),
        )

    def to_y(self):
        return remote(
            self.y_send, self.y_buf, self.y_sem.at[0], self.y_sem.at[1], self.place.over_y()
        )

    def start(self):
        for side in (1, 0):
            for hop in self.order:
                self.to_core(side, hop).start()

    def mine(self, side, hop):
        place = self.place
        self.to_core(side, hop).wait_recv()
        own = self.at(self.full, place.z_after(hop), self.x_of(side), place.core)
        return own[...].astype(f32) + self.core_buf[side, hop].astype(f32)

    def stage_x(self, hop):
        self.x_send[hop] = self.mine(1, hop).astype(low_type)
        self.to_x(hop).start()

    def stage_z(self, hop):
        part = self.mine(0, hop)
        self.to_x(hop).wait_recv()
        part = part + self.x_buf[hop].astype(f32)
        self.z_send[hop] = part.astype(low_type)
        if hop:
            self.to_z(hop).start()

    def stage_y(self):
        total = self.z_send[0].astype(f32)
        for hop in self.place.hops:
            self.to_z(hop).wait_recv()
            total = total + self.z_buf[hop].astype(f32)
        half = self.rows // 2
        first = self.place.y == 0
        self.y_send[:half] = jnp.where(first, total[half:], total[:half]).astype(low_type)
        self.to_y().start()
        return jnp.where(first, total[:half], total[half:])

    def finish(self, kept):
        self.to_y().wait()
        return kept + self.y_buf[: kept.shape[0]].astype(f32)

    def drain(self):
        for hop in self.order:
            for side in (1, 0):
                self.to_core(side, hop).wait_send()
            self.to_x(hop).wait_send()
            if hop:
                self.to_z(hop).wait_send()


class Exchange:
    def __init__(self, place, send, recv, sem):
        self.send, self.recv, self.sem = send, recv, sem
        self.targets = [place.over_core(), place.over_x(), place.over_y()]
        span = 1
        while span < place.depth:
            flip = place.z + span - 2 * span * lax.rem(place.z // span, 2)
            self.targets.append((place.unit(flip, place.x, place.core), place.y))
            span *= 2

    @staticmethod
    def rounds(units):
        return 3 + (units // 4 - 1).bit_length()

    @staticmethod
    def scratch(shape, units):
        rounds = Exchange.rounds(units)
        return [
            pltpu.VMEM((rounds,) + shape, f32),
            pltpu.VMEM((rounds,) + shape, f32),
            DMA((2, rounds)),
        ]

    def copy(self, at):
        return remote(
            self.send.at[at], self.recv.at[at], self.sem.at[0, at], self.sem.at[1, at], self.targets[at]
        )

    def start(self, at, value):
        self.send[at] = value
        self.copy(at).start()

    def finish(self, at):
        self.copy(at).wait()
        return self.send[at] + self.recv[at]


def comm_params(collective):
    return pltpu.CompilerParams(
        collective_id=collective, has_side_effects=True, vmem_limit_bytes=VMEM
    )


def first_kernel(
    wq_ref,
    wk_ref,
    wv_ref,
    gains_ref,
    second_refs,
    tokens_ref,
    q_ref,
    k_ref,
    v_ref,
    x_ref,
    w_ref,
    gain_ref,
    second_pair,
    w_all,
    x_in,
    low_here,
    stage,
    pair,
    *rest,
):
    swap_sem, load_sem, save_sem, stage_sem, w_sem = rest[21:]
    place = Place()
    per, seq, width = x_ref.shape
    rows = tokens_ref.shape[1]
    spans = (slice(2 * width, w_all.shape[1]), slice(width, 2 * width), slice(0, width))
    meets = [Meet(place, *rest[3 * at : 3 * at + 3]) for at in range(3)]
    second_meet = Meet(place, *rest[9:12])
    gathers = [
        Gather(place, pair.at[:, span], w_all.at[:, span], rest[12 + 3 * at : 15 + 3 * at])
        for at, span in enumerate(spans)
    ]
    place.greet()

    def swap(doc):
        return remote(
            tokens_ref.at[(1 - place.y) * per + doc],
            x_in.at[per + doc],
            swap_sem.at[0, doc],
            swap_sem.at[1, doc],
            place.over_y(),
        )

    def load(doc):
        return pltpu.make_async_copy(
            tokens_ref.at[place.y * per + doc], x_in.at[doc], load_sem.at[doc]
        )

    def start_of(block):
        y = jnp.where(block < per, place.y, 1 - place.y)
        return pl.multiple_of(y * rows, 16)

    def save(block):
        return pltpu.make_async_copy(
            x_in.at[block],
            x_ref.at[lax.rem(block, per), pl.ds(start_of(block), rows)],
            save_sem.at[block],
        )

    def store(block, index):
        target = (q_ref, k_ref, v_ref)[index]
        begin = pl.multiple_of(lax.rem(block, per) * seq + start_of(block), 16)
        slot = lax.rem(block, 2)
        return pltpu.make_async_copy(
            stage.at[slot, index], target.at[pl.ds(begin, rows)], stage_sem.at[slot, index]
        )

    for meet, parts in zip(meets, ((wv_ref, gains_ref), (wk_ref,), (wq_ref,))):
        meet.start(parts)
    for doc in range(per):
        load(doc).start()
        swap(doc).start()
    stages = [gather.stages() for gather in gathers]
    for at in range(3):
        meets[at].finish(pair.at[:, spans[at]])
        stages[at][0]()
    out_ref, in_ref, down_ref = second_refs
    second_meet.start([out_ref] + hidden_parts(in_ref, down_ref, 0, AHEAD))
    for index in range(1, place.depth):
        for at in range(3):
            stages[at][index]()

    def put_stage(block, index, part):
        if index == 0:
            part = part * (0.125 * LOG2E)
        stage[lax.rem(block, 2), index] = part.astype(low_type)
        store(block, index).start()

    def own_rows(at, index):
        for later in range(place.depth, len(stages[at])):
            stages[at][later]()
        if at == 0:
            gain_ref[...] = w_all[:, 3 * width :].astype(f32).T[: gain_ref.shape[0]]

        def project(block, _):
            if at == 0:
                load(block).wait()
                save(block).start()
                normed, _ = norm_rows(x_in[block].astype(f32))
                low_here[block] = (normed * gain_ref[0:1]).astype(low_type)

            @pl.when(block >= 2)
            def _():
                store(block - 2, index).wait()

            columns = w_all[:, index * width : (index + 1) * width]
            put_stage(block, index, dot(low_here[block], columns))
            return 0

        lax.fori_loop(0, per, project, 0)

    for at, index in ((0, 2), (1, 1), (2, 0)):
        own_rows(at, index)
    keep = pltpu.make_async_copy(w_all, w_ref, w_sem)
    keep.start()

    def project(block, _):
        swap(block - per).wait_recv()
        save(block).start()
        normed, _ = norm_rows(x_in[block].astype(f32))
        low = (normed * gain_ref[0:1]).astype(low_type)
        for index in (2, 1, 0):

            @pl.when(block >= 2)
            def _(index=index):
                store(block - 2, index).wait()

            put_stage(block, index, dot(low, w_all[:, index * width : (index + 1) * width]))
        return 0

    lax.fori_loop(per, 2 * per, project, 0)
    second_meet.finish(second_pair)
    for block in range(2 * per):
        save(block).wait()
        if block >= 2 * per - 2:
            for index in range(3):
                store(block, index).wait()
    keep.wait()
    for gather in gathers:
        gather.drain()
    for doc in range(per):
        swap(doc).wait_send()


def first_call(firsts, gains, seconds, tokens, ways):
    units = lax.axis_size("dp")
    count, rows, width = tokens.shape
    own_rows = gains.shape[0]
    columns = sum(w.shape[1] for w in firsts) + gains.shape[1]
    second_columns = width + AHEAD * 2 * (seconds[1].shape[1] // CHUNKS)
    per = count // ways
    total = per * rows * ways

    def kernel(*refs):
        begin = len(firsts) + 1
        end = begin + len(seconds)
        first_kernel(*refs[:begin], refs[begin:end], *refs[end:])

    return pl.pallas_call(
        kernel,
        in_specs=[VMEM_WHOLE] * (len(firsts) + 1 + len(seconds)) + [ANY],
        out_specs=[ANY] * 5 + [VMEM_WHOLE] * 2,
        out_shape=[struct((total, width))] * 3
        + [
            struct((per, rows * ways, width)),
            struct((units * ways * own_rows, columns)),
            struct((8, width), f32),
            struct((ways * own_rows, second_columns)),
        ],
        scratch_shapes=[
            pltpu.VMEM((units * ways * own_rows, columns), low_type),
            pltpu.VMEM((2 * per, rows, width), low_type),
            pltpu.VMEM((per, rows, width), low_type),
            pltpu.VMEM((2, 3, rows, width), low_type),
            pltpu.VMEM((ways * own_rows, columns), low_type),
        ]
        + Meet.scratch(own_rows, columns - 2 * width)
        + 2 * Meet.scratch(own_rows, width)
        + Meet.scratch(own_rows, second_columns)
        + 3 * Gather.scratch(units)
        + [DMA((2, per)), DMA((per,)), DMA((2 * per,)), DMA((2, 3)), DMA],
        compiler_params=comm_params(1),
        name="first",
    )(*firsts, gains, *seconds, tokens)


def attend_send_kernel(
    len_ref,
    table_ref,
    q_ref,
    k_ref,
    v_ref,
    pair_ref,
    in_ref,
    down_ref,
    cot_ref,
    o_ref,
    lse_ref,
    w_ref,
    late_pair,
    cot_doc,
    near_ref,
    cot_in,
    *rest,
    rows,
):
    place = Place()
    gathers = gather_parts(place, pair_ref, w_ref, rest[:-5])
    meet = Meet(place, *rest[-5:-2])
    swap_sem, load_sem = rest[-2:]
    per, part = cot_doc.shape[0], cot_ref.shape[1]
    step = pl.program_id(0) * pl.num_programs(1) + pl.program_id(1)
    last = pl.num_programs(0) * pl.num_programs(1) - 1
    stages = [gather.stages() for gather in gathers]

    def swap(doc):
        return remote(
            cot_ref.at[(1 - place.y) * per + doc],
            cot_doc.at[doc, pl.ds(pl.multiple_of(place.y * part, 16), part)],
            swap_sem.at[0, doc],
            swap_sem.at[1, doc],
            place.over_y(),
        )

    def load(doc):
        return pltpu.make_async_copy(
            cot_ref.at[place.y * per + doc], cot_in.at[doc], load_sem.at[0, doc]
        )

    def save(doc):
        return pltpu.make_async_copy(
            cot_in.at[doc],
            cot_doc.at[doc, pl.ds(pl.multiple_of(place.y * part, 16), part)],
            load_sem.at[1, doc],
        )

    @pl.when(step == 0)
    def _():
        place.greet()
        for doc in range(per):
            load(doc).start()

    for at, piece, index in SEND_PLAN:

        @pl.when(step == at)
        def _(piece=piece, index=index):
            stages[piece][index]()

    @pl.when(step == 1)
    def _():
        for doc in range(per):
            swap(doc).start()
            load(doc).wait()
            save(doc).start()
        meet.start(hidden_parts(in_ref, down_ref, AHEAD, CHUNKS))

    attend_kernel(len_ref, table_ref, q_ref, k_ref, v_ref, o_ref, lse_ref, near_ref, rows=rows)

    @pl.when(step == last)
    def _():
        done = {(piece, index) for _, piece, index in SEND_PLAN}
        for index in range(len(stages[0])):
            for piece in range(PARTS):
                if (piece, index) not in done:
                    stages[piece][index]()
        meet.finish(late_pair)
        for gather in gathers:
            gather.drain()
        for doc in range(per):
            save(doc).wait()
            swap(doc).wait()


SEND_PLAN = (
    (0, 0, 0), (1, 1, 0), (3, 0, 1), (5, 1, 1), (6, 0, 2), (7, 1, 2),
    (8, 0, 3), (10, 1, 3), (10, 0, 4), (11, 0, 5),
)


def attend_send_call(lengths, table, q, k, v, pair, w_in, w_down, cot, rows=512):
    units = lax.axis_size("dp")
    docs, (total, width) = lengths.shape[0], q.shape
    seq, pairs = total // docs, width // 128
    late = (CHUNKS - AHEAD) * 2 * (w_in.shape[1] // CHUNKS)
    slab = pl.BlockSpec((seq, 128), lambda p, d: (d, p))
    return pl.pallas_call(
        functools.partial(attend_send_kernel, rows=rows),
        grid=(pairs, docs),
        in_specs=[SMEM, SMEM, slab, slab, slab]
        + [whole(operand.shape) for operand in (pair, w_in, w_down)]
        + [ANY],
        out_specs=[
            slab,
            pl.BlockSpec((1, 1, 2, seq), lambda p, d: (d, p, 0, 0)),
            ANY,
            whole((pair.shape[0], late)),
            ANY,
        ],
        out_shape=[
            struct((total, width)),
            struct((docs, pairs, 2, seq), f32),
            struct((units * pair.shape[0], pair.shape[1])),
            struct((pair.shape[0], late)),
            struct((docs, seq, width)),
        ],
        scratch_shapes=[
            pltpu.VMEM((2, 3, SUB, SUB), f32),
            pltpu.VMEM((docs, cot.shape[1], width), low_type),
        ]
        + PARTS * Gather.scratch(units)
        + Meet.scratch(w_in.shape[0], late)
        + [DMA((2, docs)), DMA((2, docs))],
        compiler_params=comm_params(3),
        name="attend",
    )(lengths, table, q, k, v, pair, w_in, w_down, cot)


def back_send_kernel(
    len_ref,
    table_ref,
    q_ref,
    k_ref,
    v_ref,
    grad_ref,
    o_ref,
    lse_ref,
    g_ref,
    mixed_ref,
    dq_ref,
    dk_ref,
    dv_ref,
    table_sum,
    gw_ref,
    mixed_out,
    near_ref,
    near_sum,
    far_sum,
    acc,
    grads,
    mixed_in,
    kept,
    *rest,
    keys,
    queries,
    steps,
):
    place = Place()
    size = grads.shape[1] // CHUNKS
    grads_sem, swap_sem, load_sem = rest[11:]

    def scatter(at):
        span = pl.ds(pl.multiple_of(at * size, 128), size)
        return Scatter(
            place, grads.at[:, span], [ref.at[at] for ref in rest[:11]], g_ref.at[:, span]
        )

    per, part = mixed_ref.shape[0], mixed_out.shape[1]
    step = pl.program_id(0) * pl.num_programs(1) + pl.program_id(1)
    last = pl.num_programs(0) * pl.num_programs(1) - 1

    def swap(doc):
        return remote(
            mixed_ref.at[doc, pl.ds(pl.multiple_of((1 - place.y) * part, 16), part)],
            mixed_out.at[place.y * per + doc],
            swap_sem.at[0, doc],
            swap_sem.at[1, doc],
            place.over_y(),
        )

    def load(doc):
        return pltpu.make_async_copy(
            mixed_ref.at[doc, pl.ds(pl.multiple_of(place.y * part, 16), part)],
            mixed_in.at[doc],
            load_sem.at[0, doc],
        )

    def save(doc):
        return pltpu.make_async_copy(
            mixed_in.at[doc], mixed_out.at[place.y * per + doc], load_sem.at[1, doc]
        )

    take = pltpu.make_async_copy(g_ref, grads, grads_sem)

    @pl.when(step == 0)
    def _():
        place.greet()
        for at in range(CHUNKS):
            scatter(at).start()
        take.start()
        for doc in range(per):
            load(doc).start()
            swap(doc).start()

    @pl.when(step == 1)
    def _():
        take.wait()

    def every_other(first, work):
        at = (step - first) // 2

        @pl.when((step >= first) & (at < CHUNKS) & (step == first + 2 * at))
        def _():
            work(at)

    def x_stages(at):
        for hop in place.hops + [0]:
            scatter(at).stage_x(hop)

    def z_stages(at):
        for hop in place.hops + [0]:
            scatter(at).stage_z(hop)

    def y_stage(at):
        kept[at] = scatter(at).stage_y()

    def finish(at):
        gw_ref[:, pl.ds(pl.multiple_of(at * size, 128), size)] = scatter(at).finish(kept[at])

    every_other(1, x_stages)
    every_other(3, z_stages)
    every_other(5, y_stage)
    every_other(6, finish)

    @pl.when(step == 3)
    def _():
        for doc in range(per):
            load(doc).wait()
            save(doc).start()

    attend_back_kernel(
        len_ref,
        table_ref,
        q_ref,
        k_ref,
        v_ref,
        grad_ref,
        o_ref,
        lse_ref,
        dq_ref,
        dk_ref,
        dv_ref,
        table_sum,
        near_ref,
        near_sum,
        far_sum,
        acc,
        keys=keys,
        queries=queries,
    )

    @pl.when(step == last)
    def _():
        for at in range(CHUNKS):
            for first, work in ((1, x_stages), (3, z_stages), (5, y_stage), (6, finish)):
                if first + 2 * at >= steps:
                    work(at)
        for at in range(CHUNKS):
            scatter(at).drain()
        for doc in range(per):
            save(doc).wait()
            swap(doc).wait()


def back_send_call(lengths, table, q, k, v, grad, o, lse, g, mixed, keys=512, queries=1024):
    units = lax.axis_size("dp")
    docs, (total, width) = lengths.shape[0], q.shape
    seq, pairs = total // docs, width // 128
    columns = g.shape[1]
    own = g.shape[0] // (2 * units)
    slab = pl.BlockSpec((seq, 128), lambda p, d: (d, p))
    return pl.pallas_call(
        functools.partial(
            back_send_kernel, keys=keys, queries=min(queries, seq), steps=pairs * docs
        ),
        grid=(pairs, docs),
        in_specs=[
            SMEM,
            SMEM,
            slab,
            slab,
            slab,
            slab,
            slab,
            pl.BlockSpec((1, 1, 2, seq), lambda p, d: (d, p, 0, 0)),
            ANY,
            ANY,
        ],
        out_specs=[
            slab,
            slab,
            slab,
            pl.BlockSpec((1, 2, BAND), lambda p, d: (p, 0, 0)),
            whole((own, columns)),
            ANY,
        ],
        out_shape=[struct((total, width))] * 3
        + [
            struct((pairs, 2, BAND), f32),
            struct((own, columns), f32),
            struct((2 * docs, seq // 2, width)),
        ],
        scratch_shapes=back_scratch(seq)
        + [
            pltpu.VMEM(g.shape, low_type),
            pltpu.VMEM((docs, seq // 2, width), low_type),
            pltpu.VMEM((CHUNKS, own, columns // CHUNKS), f32),
        ]
        + Scatter.scratch(own, columns // CHUNKS, units, (CHUNKS,))
        + [DMA, DMA((2, docs)), DMA((2, docs))],
        compiler_params=comm_params(4),
        name="attend_back",
    )(lengths, table, q, k, v, grad, o, lse, g, mixed.reshape(docs, seq, width))


def end_kernel(
    x_ref,
    dq_ref,
    dk_ref,
    dv_ref,
    mid_ref,
    w_ref,
    gain_ref,
    table_ref,
    wq_ref,
    wk_ref,
    wv_ref,
    w_in_ref,
    g_hidden_ref,
    g_out,
    gw_ref,
    gt_ref,
    small_ref,
    gains_ref,
    rows_in,
    low_all,
    grads,
    gt,
    *rest,
):
    place = Place()
    count, rows, width = gt_ref.shape
    per = count // 2
    seq = 2 * rows
    scatter_refs, kept = rest[:11], rest[11]
    small_send, small_recv, small_sem, load_sem, gt_sem = rest[12:]
    exchange = Exchange(place, small_send, small_recv, small_sem)
    sources = (x_ref, dq_ref, dk_ref, dv_ref, mid_ref)

    def scatter(at):
        return Scatter(place, grads.at[at], [ref.at[at] for ref in scatter_refs])

    def load(block, index):
        y = jnp.where(block < per, 1 - place.y, place.y)
        begin = pl.multiple_of(lax.rem(block, per) * seq + y * rows, 16)
        return pltpu.make_async_copy(
            sources[index].at[pl.ds(begin, rows)],
            rows_in.at[index, block],
            load_sem.at[block, index],
        )

    def give_away(block):
        return remote(
            gt.at[block],
            gt_ref.at[place.y * per + block],
            gt_sem.at[0, block],
            gt_sem.at[1, block],
            place.over_y(),
        )

    def give_home(block):
        return pltpu.make_async_copy(
            gt.at[block], gt_ref.at[place.y * per + block - per], gt_sem.at[0, block]
        )

    take = pltpu.make_async_copy(g_out, grads.at[0], load_sem.at[2 * per, 0])
    for index in range(5):
        load(0, index).start()
    take.start()
    for index in range(5):
        for block in range(1, 2 * per):
            load(block, index).start()
    place.greet()
    gain = gain_ref[0:1]
    take.wait()
    scatter(0).start()
    heads = table_ref.shape[0]
    small_send[0] = jnp.zeros(small_ref.shape, f32)
    small_send[0, :heads] = bucket_sums(table_ref[...], 32)
    exchange.copy(0).start()
    chunk = g_hidden_ref.shape[1] // (2 * CHUNKS)
    sum_second = jnp.zeros((gains_ref.shape[0], chunk), f32)
    for at in range(CHUNKS):
        sum_second += (
            g_hidden_ref[:, 2 * at * chunk : (2 * at + 1) * chunk]
            * w_in_ref[:, at * chunk : (at + 1) * chunk].astype(f32)
        )
    rounds = len(exchange.targets)

    def exchange_round(at):
        value = exchange.finish(at)
        if at < rounds - 1:
            exchange.start(at + 1, value)
        else:
            small_ref[...] = value

    def low_rows(block, _):
        @pl.when(block > 0)
        def _():
            load(block, 0).wait()

        normed, _ = norm_rows(rows_in[0, block].astype(f32))
        low_all[block] = (normed * gain).astype(low_type)
        return 0

    def rows_back(block):
        normed, inverse = norm_rows(rows_in[0, block].astype(f32))
        normed_grad = None
        for index in range(3):
            part = dot(
                rows_in[1 + index, block], w_ref[:, index * width : (index + 1) * width], NT
            )
            normed_grad = part if normed_grad is None else normed_grad + part
        scaled = normed_grad * gain
        inner = jnp.mean(scaled * normed, -1, keepdims=True)
        mid = rows_in[4, block].astype(f32)
        gt[block] = (mid + inverse * (scaled - normed * inner)).astype(low_type)

        @pl.when(block < per)
        def _():
            give_away(block).start()

        @pl.when(block >= per)
        def _():
            give_home(block).start()

    def weights_back(at):
        grads[at] = dot(
            low_all[...].reshape(2 * per * rows, width),
            rows_in[at].reshape(2 * per * rows, width),
            TN,
        ).astype(low_type)
        scatter(at).start()

    def during(at, first, last, work):
        @pl.when((at >= first) & (at <= last))
        def _():
            work(at)

    def x_stages(at):
        for hop in place.hops + [0]:
            scatter(at).stage_x(hop)

    def z_stages(at):
        for hop in place.hops + [0]:
            scatter(at).stage_z(hop)

    def y_stage(at):
        kept[at] = scatter(at).stage_y()

    def finish(at):
        gw_ref[at] = scatter(at).finish(kept[at])

    def project_step(at, _):
        weights_back(at)
        x_stages(at - 1)
        for index in range(2):
            during(at, index + 2, index + 2, lambda _, index=index: exchange_round(index))
        return 0

    def rows_step(block, _):
        rows_back(block)
        during(block, 1, 1, lambda _: z_stages(0))
        during(block, 1, 2, z_stages)
        during(block, 2, 2, lambda _: z_stages(3))
        during(block, 3, 3, lambda _: y_stage(0))
        during(block, 3, 3, lambda _: y_stage(1))
        during(block, 3, 3, lambda _: y_stage(2))
        for index in range(2, rounds):
            during(block, index - 1, index - 1, lambda _, index=index: exchange_round(index))
        return 0

    for index in range(5):
        load(0, index).wait()
    rows_back(0)
    lax.fori_loop(0, 2 * per, low_rows, 0)
    for index in range(1, 5):
        for block in range(1, 2 * per):
            load(block, index).wait()
    lax.fori_loop(1, 4, project_step, 0)
    x_stages(3)
    lax.fori_loop(1, 2 * per, rows_step, 0)
    y_stage(3)
    finish(0)
    finish(1)
    finish(2)
    finish(3)
    sum_first = jnp.zeros((gains_ref.shape[0], width), f32)
    for at, ref in enumerate((wq_ref, wk_ref, wv_ref)):
        sum_first += gw_ref[1 + at] * ref[...].astype(f32)
    lane = lax.broadcasted_iota(jnp.int32, (1, 128), 1)
    gains_ref[...] = jnp.where(
        lane == 0,
        jnp.sum(sum_first, 1, keepdims=True),
        jnp.sum(sum_second, 1, keepdims=True),
    )

    def drain(at, _):
        scatter(at).drain()
        return 0

    lax.fori_loop(0, 4, drain, 0)
    for block in range(per):
        give_away(block).wait()
        give_home(per + block).wait()


def end_call(x, dq, dk, dv, mid, w_first, gains, table, own_weights, g_hidden, g_out, docs, ways):
    units = lax.axis_size("dp")
    total, width = x.shape
    own = width // (units * ways)
    rows = total // (docs * ways)
    small = (table.shape[0] + -table.shape[0] % 8, 128)
    return pl.pallas_call(
        end_kernel,
        in_specs=[ANY] * 5 + [VMEM_WHOLE] * 8 + [ANY],
        out_specs=[VMEM_WHOLE, ANY, VMEM_WHOLE, VMEM_WHOLE],
        out_shape=[
            struct((4, own, width), f32),
            struct((docs * ways, rows, width)),
            struct(small, f32),
            struct((own, 128), f32),
        ],
        scratch_shapes=[
            pltpu.VMEM((5, docs * ways, rows, width), low_type),
            pltpu.VMEM((docs * ways, rows, width), low_type),
            pltpu.VMEM((4, width, width), low_type),
            pltpu.VMEM((docs * ways, rows, width), low_type),
        ]
        + Scatter.scratch(own, width, units, (4,))
        + [pltpu.VMEM((4, own, width), f32)]
        + Exchange.scratch(small, units)
        + [DMA((docs * ways + 1, 5)), DMA((2, docs * ways))],
        compiler_params=comm_params(2),
        name="end",
    )(x, dq, dk, dv, mid, w_first, gains, table, *own_weights, g_hidden, g_out)


def sharing(count):
    ways = lax.axis_size("blk")
    return max(1, count // ways), max(1, ways // count)


def to_documents(x):
    count, rows, width = x.shape
    ways, me = lax.axis_size("blk"), lax.axis_index("blk")
    per, share = sharing(count)
    if share > 1:
        everything = lax.all_gather(x, "blk", axis=1, tiled=True)
        return lax.dynamic_index_in_dim(everything, me // share, 0, keepdims=False)
    out = jnp.zeros((per, ways * rows, width), x.dtype)
    for hop in range(ways):
        piece = lax.dynamic_slice_in_dim(x, lax.rem(me + hop, ways) * per, per, 0)
        if hop:
            piece = lax.ppermute(piece, "blk", [(i, (i + hop) % ways) for i in range(ways)])
        source = lax.rem(me - hop + ways, ways)
        out = lax.dynamic_update_slice_in_dim(out, piece, source * rows, 1)
    return out.reshape(per * ways * rows, width)


def from_documents(y, count):
    ways, me = lax.axis_size("blk"), lax.axis_index("blk")
    per, share = sharing(count)
    width = y.shape[1]
    if share > 1:
        everything = lax.all_gather(y, "blk", axis=0, tiled=True).reshape(count, -1, width)
        rows = everything.shape[1] // ways
        return lax.dynamic_slice_in_dim(everything, me * rows, rows, 1)
    y = y.reshape(per, -1, width)
    rows = y.shape[1] // ways
    out = jnp.zeros((count, rows, width), y.dtype)
    for hop in range(ways):
        piece = lax.dynamic_slice_in_dim(y, lax.rem(me + hop, ways) * rows, rows, 1)
        if hop:
            piece = lax.ppermute(piece, "blk", [(i, (i + hop) % ways) for i in range(ways)])
        source = lax.rem(me - hop + ways, ways)
        out = lax.dynamic_update_slice_in_dim(out, piece, source * per, 0)
    return out


def among(y, share, split, concat):
    if share == 1:
        return y
    ways = lax.axis_size("blk")
    groups = [list(range(at, at + share)) for at in range(0, ways, share)]
    return lax.all_to_all(
        y, "blk", split, concat, axis_index_groups=groups, tiled=True
    )


def my_share(y, share, axis):
    if share == 1:
        return y
    size = y.shape[axis] // share
    at = lax.rem(lax.axis_index("blk"), share) * size
    return lax.dynamic_slice_in_dim(y, at, size, axis)


def body(
    tokens,
    lengths,
    norm1_gain,
    w_query,
    w_key,
    w_value,
    w_out,
    rel_table,
    norm2_gain,
    w_in,
    w_down,
    cotangent,
):
    micro, docs, rows, width = tokens.shape
    count = micro * docs
    per, share = sharing(count)
    both = ("dp", "blk")
    direct = lax.axis_size("blk") == 2 and per * 2 == count and lax.axis_size("dp") % 4 == 0
    gains = jnp.pad(jnp.stack([norm1_gain, norm2_gain], 1), ((0, 0), (0, SPARE - 2)))
    firsts, seconds = (w_query, w_key, w_value), (w_out, w_in, w_down)
    tokens_here = tokens.reshape(count, rows, width)
    cot_here = cotangent.reshape(count, rows, width)
    if direct:
        q, k, v, x, w_first, gain_rows, pair = first_call(
            firsts, gains, seconds, tokens_here, 2
        )
        x = x.reshape(-1, width)
    else:
        pair = None
        w_second = lax.all_gather(second_pieces(*seconds), both, axis=0, tiled=True)
        w_first = lax.all_gather(
            jnp.concatenate(firsts + (gains,), 1), both, axis=0, tiled=True
        )
        x = to_documents(tokens_here)
        gain_rows = w_first[:, 3 * width : 3 * width + 2].astype(f32).T
    gain_first, gain_second = gain_rows[:1], gain_rows[1:2]
    own = lax.dynamic_slice_in_dim(
        lengths.reshape(count), lax.axis_index("blk") // share * per, per, 0
    )
    x_rows = my_share(x, share, 0)
    own_rows, w_heads = own, w_first
    if share > 1:
        own_rows = own - lax.rem(lax.axis_index("blk"), share) * x_rows.shape[0]
        w_heads = jnp.concatenate(
            [my_share(w_first[:, i * width : (i + 1) * width], share, 1) for i in range(3)], 1
        )
    table = my_share((rel_table * LOG2E).T, share, 0)

    if direct:
        heads, lse, w_second, pair, cot = attend_send_call(
            own, table, q, k, v, pair, w_in, w_down, cot_here
        )
        cot = cot.reshape(-1, width)
    else:
        q, k, v = qkv_call(x, gain_first, w_heads, width // share)
        heads, lse = attend_call(own, table, q, k, v)
        cot = my_share(to_documents(cot_here), share, 0)
    mixed, heads_grad, mid, g_out, g_hidden, gn_second = middle_call(
        own_rows, x_rows, among(heads, share, 0, 1), cot, gain_second, w_second, pair
    )
    if direct:
        dq, dk, dv, table_sum, g_hidden, mixed = back_send_call(
            own, table, q, k, v, heads_grad, heads, lse, g_hidden, mixed
        )
    else:
        dq, dk, dv, table_sum = attend_back_call(
            own, table, q, k, v, among(heads_grad, share, 1, 0), heads, lse
        )
        mixed = from_documents(mixed, count)
        g_out = lax.psum_scatter(g_out, both, scatter_dimension=0, tiled=True).astype(f32)
        g_hidden = lax.psum_scatter(g_hidden, both, scatter_dimension=0, tiled=True).astype(f32)
    dq, dk, dv = (among(grad, share, 0, 1) for grad in (dq, dk, dv))
    head_count, bucket_count = rel_table.shape[1], rel_table.shape[0]
    if direct:
        g_first, grad_tokens, small, gains = end_call(
            x,
            dq,
            dk,
            dv,
            mid,
            w_first,
            gain_rows,
            table_sum.reshape(-1, BAND),
            firsts + (w_in,),
            g_hidden,
            g_out,
            per,
            2,
        )
        grad_table = small[:head_count, :bucket_count].T
        gains = (gains[:, 0] / norm1_gain.astype(f32), gains[:, 1] / norm2_gain.astype(f32))
    else:
        grad_tokens, g_first, gn_first = last_call(
            x_rows, dq, dk, dv, mid, gain_first, w_first
        )
        grad_tokens = from_documents(grad_tokens, count)
        g_first = lax.psum_scatter(g_first, both, scatter_dimension=0, tiled=True).astype(f32)
        gains = lax.psum_scatter(
            jnp.concatenate([gn_first, gn_second], 0), both, scatter_dimension=1, tiled=True
        )
        table_sum = bucket_sums(table_sum.reshape(-1, BAND), bucket_count)[:, :bucket_count]
        if share > 1:
            at = lax.rem(lax.axis_index("blk"), share) * table_sum.shape[0]
            table_sum = lax.dynamic_update_slice_in_dim(
                jnp.zeros(rel_table.T.shape, f32), table_sum, at, 0
            )
        grad_table = lax.psum(table_sum, both).T
    if direct:
        g_out, grad_query, grad_key, grad_value = g_first
    else:
        grad_query, grad_key, grad_value = (
            g_first[:, i * width : (i + 1) * width] for i in range(3)
        )
    grad_in, grad_down = split_hidden(g_hidden)
    return (
        mixed.reshape(tokens.shape),
        grad_tokens.reshape(tokens.shape),
        gains[0],
        grad_query,
        grad_key,
        grad_value,
        g_out,
        grad_table,
        gains[1],
        grad_in,
        grad_down,
    )


def solution(mesh):
    rows = P(None, "dp", "blk", None)
    weight = P(("dp", "blk"), None)
    gain = P(("dp", "blk"))
    return jax.shard_map(
        body,
        mesh=mesh,
        in_specs=(
            rows,
            P(None, "dp"),
            gain,
            weight,
            weight,
            weight,
            weight,
            P(),
            gain,
            weight,
            weight,
            rows,
        ),
        out_specs=(rows, rows, gain, weight, weight, weight, weight, P(), gain, weight, weight),
        check_vma=False,
    )
```

```python
import functools

import jax
import jax.numpy as jnp
from jax import lax
from jax.experimental import pallas as pl
from jax.experimental.pallas import tpu as pltpu
from jax.sharding import PartitionSpec as P

EPS = 1e-06
NEG = -1e30
LIMITS = (12, 16, 23, 32, 46, 64, 91)
SUB = 128
LOG2E = 1.4426950408889634
GELU_A = 0.7978845608028654
GELU_B = 0.044715
VMEM = 62 * 2**20
NN = (((1,), (0,)), ((), ()))
NT = (((1,), (1,)), ((), ()))
TN = (((0,), (0,)), ((), ()))
low_type = jnp.bfloat16
f32 = jnp.float32


def dot(left, right, dims=NN):
    return lax.dot_general(left, right, dims, preferred_element_type=f32)


def bucket_of(relative):
    distance = jnp.abs(relative)
    far_bucket = 8 + sum(((distance >= border).astype(jnp.int32) for border in LIMITS))
    bucket = jnp.where(distance < 8, distance, far_bucket)
    return bucket + 16 * (relative > 0).astype(jnp.int32)


def norm_rows(rows):
    inverse = lax.rsqrt(jnp.mean(rows * rows, -1, keepdims=True) + EPS)
    return rows * inverse, inverse


def whole(shape):
    return pl.BlockSpec(shape, lambda *_: (0,) * len(shape), pipeline_mode=pl.Buffered(1))


def params():
    return pltpu.CompilerParams(vmem_limit_bytes=VMEM)


def struct(shape, dtype=low_type):
    return jax.ShapeDtypeStruct(shape, dtype)


SMEM = pl.BlockSpec(memory_space=pltpu.SMEM)


BAND = 4 * SUB


def band_buckets():
    at = lax.broadcasted_iota(jnp.int32, (1, BAND), 1)
    return bucket_of(jnp.where(at < 3 * SUB, at, at - BAND) - SUB)


def fill_tiles(near, table_ref, pair):
    buckets = band_buckets()
    for h in range(2):
        line = jnp.zeros((1, BAND), f32)
        for b in range(32):
            line = jnp.where(buckets == b, table_ref[2 * pair + h, b], line)
        band = pltpu.roll(
            jnp.broadcast_to(line, (SUB, BAND)), 0, 1, stride=1, stride_axis=0
        )
        for apart in (-1, 0, 1):
            near[h, apart + 1] = band[:, SUB * (1 + apart) : SUB * (2 + apart)]


def band_sums(tiles):
    band = jnp.concatenate([tiles[0], tiles[1], tiles[2], jnp.zeros((SUB, SUB), f32)], 1)
    out = band[:8]
    for at in range(8, SUB, 8):
        out = out + pltpu.roll(band[at : at + 8], BAND - at, 1)
    row = lax.broadcasted_iota(jnp.int32, out.shape, 0)
    for bit in (1, 2, 4):
        out = jnp.where((row & bit) != 0, pltpu.roll(out, BAND - bit, 1), out)
    return jnp.sum(out, 0, keepdims=True)


def bucket_sums(sums, count):
    buckets = band_buckets()
    lane = lax.broadcasted_iota(jnp.int32, (1, SUB), 1)
    out = jnp.zeros((sums.shape[0], SUB), f32)
    for b in range(count):
        part = jnp.sum(jnp.where(buckets == b, sums, 0.0), 1, keepdims=True)
        out = jnp.where(lane == b, part, out)
    return out


def qkv_kernel(x_ref, gain_ref, w_ref, q_ref, k_ref, v_ref):
    width = q_ref.shape[1]
    normed, _ = norm_rows(x_ref[...].astype(f32))
    low = (normed * gain_ref[...]).astype(low_type)
    q_ref[...] = (dot(low, w_ref[:, :width]) * (0.125 * LOG2E)).astype(low_type)
    k_ref[...] = dot(low, w_ref[:, width : 2 * width]).astype(low_type)
    v_ref[...] = dot(low, w_ref[:, 2 * width : 3 * width]).astype(low_type)


def qkv_call(x, gain, w_first, heads_width, rows=512):
    total, width = x.shape
    row = pl.BlockSpec((rows, width), lambda i: (i, 0))
    return pl.pallas_call(
        qkv_kernel,
        grid=(total // rows,),
        in_specs=[row, whole((1, width)), whole(w_first.shape)],
        out_specs=[pl.BlockSpec((rows, heads_width), lambda i: (i, 0))] * 3,
        out_shape=[struct((total, heads_width))] * 3,
        compiler_params=params(),
        name="qkv",
    )(x, gain, w_first)


def attend_kernel(
    len_ref, table_ref, q_ref, k_ref, v_ref, o_ref, lse_ref, near_ref, *, rows
):
    pair, doc = pl.program_id(0), pl.program_id(1)

    @pl.when(doc == 0)
    def _():
        fill_tiles(near_ref, table_ref, pair)

    seq = q_ref.shape[0]
    subs = seq // SUB
    first = lax.broadcasted_iota(jnp.int32, (1, 128), 1) < 64
    live = lax.broadcasted_iota(jnp.int32, (1, seq), 1) < len_ref[doc]
    one = jnp.ones((), low_type)
    k, v = k_ref[...], v_ref[...]
    v_ones = (jnp.where(first, v, one), jnp.where(first, one, v))
    for block in range(seq // rows):
        span = slice(block * rows, (block + 1) * rows)
        q = q_ref[span, :]
        outs, tops = [], []
        for h in range(2):
            q_one = jnp.where(first == (h == 0), q, jnp.zeros((), low_type))
            raw = dot(q_one, k, NT)
            strips = []
            for a in range(rows // SUB):
                at = block * (rows // SUB) + a
                strip = raw[a * SUB : (a + 1) * SUB]
                low, high = max(at - 1, 0), min(at + 2, subs)
                parts = []
                if low > 0:
                    parts.append(strip[:, : low * SUB] + table_ref[2 * pair + h, 15])
                for b in range(low, high):
                    parts.append(strip[:, b * SUB : (b + 1) * SUB] + near_ref[h, b - at + 1])
                if high < subs:
                    parts.append(strip[:, high * SUB :] + table_ref[2 * pair + h, 31])
                strips.append(jnp.concatenate(parts, 1))
            scores = jnp.where(live, jnp.concatenate(strips, 0), NEG)
            top = jnp.max(scores, 1, keepdims=True)
            outs.append(dot(jnp.exp2(scores - top).astype(low_type), v_ones[h]))
            tops.append(top)
        total = jnp.where(first, pltpu.roll(outs[0], 64, 1), pltpu.roll(outs[1], 64, 1))
        o_ref[span, :] = (jnp.where(first, outs[0], outs[1]) / total).astype(low_type)
        lse_ref[span, :] = jnp.where(first, tops[0], tops[1]) + jnp.log2(total)


def attend_call(lengths, table, q, k, v, rows=512):
    docs, (total, width) = lengths.shape[0], q.shape
    seq, pairs = total // docs, width // 128
    slab = pl.BlockSpec((seq, 128), lambda p, d: (d, p))
    return pl.pallas_call(
        functools.partial(attend_kernel, rows=rows),
        grid=(pairs, docs),
        in_specs=[
            SMEM,
            SMEM,
            slab,
            slab,
            slab,
        ],
        out_specs=[slab, slab],
        out_shape=[struct((total, width)), struct((total, width), f32)],
        scratch_shapes=[pltpu.VMEM((2, 3, SUB, SUB), f32)],
        compiler_params=params(),
        name="attend",
    )(lengths, table, q, k, v)


CHUNKS = 4
AHEAD = 2


def second_pieces(w_out, w_in, w_down):
    chunk = w_in.shape[1] // CHUNKS
    parts = [w_out]
    for at in range(0, CHUNKS * chunk, chunk):
        parts += [w_in[:, at : at + chunk], w_down[:, at : at + chunk]]
    return jnp.concatenate(parts, 1)


def split_hidden(grads):
    chunk = grads.shape[1] // (2 * CHUNKS)
    parts = [grads[:, at * chunk : (at + 1) * chunk] for at in range(2 * CHUNKS)]
    return jnp.concatenate(parts[0::2], 1), jnp.concatenate(parts[1::2], 1)


def middle_kernel(
    len_ref,
    x_ref,
    heads_ref,
    cot_ref,
    gain_ref,
    w_out,
    w_hbm,
    mixed_ref,
    hgrad_ref,
    mid_ref,
    g_out,
    g_ref,
    gn_ref,
    scratch,
    *,
    seq,
    before_chunk,
):
    low_all, grad_all, normed_all, inverse_all, mixed_all, back_all = scratch[:6]
    act_all, up_all, g_buf, acc_gain, g_sem, w_all, w_sem = scratch[6:]
    step = pl.program_id(0)
    rows, width = x_ref.shape
    total = low_all.shape[0]
    chunk = w_all.shape[1] // (2 * CHUNKS)
    fine, block = total // rows, MIDDLE_BLOCK
    coarse = total // block
    begin = fine
    finish = fine + CHUNKS * coarse

    @pl.when(step < begin)
    def _():
        span = pl.ds(pl.multiple_of(step * rows, rows), rows)
        per = seq // rows
        place = lax.rem(step, per) * rows + lax.broadcasted_iota(jnp.int32, (rows, 1), 0)
        residual = x_ref[...].astype(f32) + dot(heads_ref[...], w_out[...])
        normed, inverse = norm_rows(residual)
        mixed_all[span, :] = residual
        back_all[span, :] = jnp.zeros_like(residual)
        normed_all[span, :] = normed.astype(low_type)
        inverse_all[span, :] = jnp.broadcast_to(inverse, (rows, 128))
        low_all[span, :] = (normed * gain_ref[...]).astype(low_type)
        grad_all[span, :] = jnp.where(
            place < len_ref[jnp.minimum(step // per, len_ref.shape[0] - 1)],
            cot_ref[...],
            jnp.zeros((), low_type),
        )

    def store(at):
        begins = pl.multiple_of(at * (2 * chunk), 128)
        slot = lax.rem(at, 2)
        return pltpu.make_async_copy(
            g_buf.at[slot], g_ref.at[:, pl.ds(begins, 2 * chunk)], g_sem.at[slot]
        )

    ready = w_hbm.shape[1] - width
    take = pltpu.make_async_copy(w_hbm.at[:, width:], w_all.at[:, :ready], w_sem)

    @pl.when(step == 0)
    def _():
        take.start()

    at = jnp.maximum(step - begin, 0) // coarse

    @pl.when(step == begin)
    def _():
        take.wait()

    for index in range(CHUNKS):

        @pl.when(step == begin + index * coarse)
        def _(index=index):
            before_chunk(index)

    @pl.when((step >= begin) & (step < finish))
    def _():
        span = pl.ds(pl.multiple_of((step - begin - at * coarse) * block, block), block)
        w_up = w_all[:, pl.ds(pl.multiple_of(at * (2 * chunk), 128), chunk)]
        w_down = w_all[:, pl.ds(pl.multiple_of(at * (2 * chunk) + chunk, 128), chunk)]
        u = dot(low_all[span, :], w_up)
        square = u * u
        bend = jnp.tanh(u * (GELU_A + GELU_A * GELU_B * square))
        half = 0.5 + 0.5 * bend
        act = (u * half).astype(low_type)
        slope = half + (0.5 * u) * (1 - bend * bend) * (GELU_A + 3 * GELU_A * GELU_B * square)
        up_grad = (dot(grad_all[span, :], w_down) * slope).astype(low_type)
        act_all[span, :] = act
        up_all[span, :] = up_grad
        mixed_all[span, :] += dot(act, w_down, NT)
        back_all[span, :] += dot(up_grad, w_up, NT)

    @pl.when((step >= begin) & (step < finish) & (step - begin == at * coarse + coarse - 1))
    def _():
        slot = lax.rem(at, 2)

        @pl.when(at >= 2)
        def _():
            store(at - 2).wait()

        g_buf[slot, :, :chunk] = dot(low_all[...], up_all[...], TN).astype(low_type)
        g_buf[slot, :, chunk:] = dot(grad_all[...], act_all[...], TN).astype(low_type)
        store(at).start()

    @pl.when(step >= finish)
    def _():
        span = pl.ds(pl.multiple_of((step - finish) * rows, rows), rows)
        mixed_ref[...] = mixed_all[span, :].astype(low_type)
        normed, back = normed_all[span, :].astype(f32), back_all[span, :]
        scaled = back * gain_ref[...]
        inner = jnp.mean(scaled * normed, -1, keepdims=True)
        inverse = inverse_all[span, :][:, :1]
        mid = grad_all[span, :].astype(f32) + inverse * (scaled - normed * inner)
        mid = mid.astype(low_type)
        part = jnp.sum((back * normed).reshape(rows // 8, 8, width), 0)
        acc_gain[...] = jnp.where(step == finish, part, acc_gain[...] + part)
        mid_ref[...] = mid
        act_all[span, :width] = mid
        up_all[span, :width] = heads_ref[...]
        hgrad_ref[...] = dot(mid, w_out[...], NT).astype(low_type)

    @pl.when(step == pl.num_programs(0) - 1)
    def _():
        g_out[...] = dot(up_all[:, :width], act_all[:, :width], TN).astype(low_type)
        gn_ref[...] = jnp.sum(acc_gain[...], 0, keepdims=True)
        for at in range(CHUNKS - 2, CHUNKS):
            store(at).wait()


MIDDLE_BLOCK = 512


def middle_plain_kernel(*refs, seq):
    w_ref, w_hbm, rest = refs[5], refs[6], refs[7:]
    middle_kernel(
        *refs[:5],
        w_ref,
        w_hbm,
        *rest[:6],
        rest[6:],
        seq=seq,
        before_chunk=lambda at: None,
    )


def middle_send_kernel(*refs, seq):
    w_ref, w_hbm, pair_ref, rest = refs[5], refs[6], refs[7], refs[8:]
    w_all, sems = rest[17], rest[19:]
    place = Place()
    late = w_all.at[:, w_hbm.shape[1] - refs[1].shape[1] :]
    gathers = gather_parts(place, pair_ref, late, sems)
    stages = [gather.stages() for gather in gathers]
    planned = {(part, index) for _, part, index in MIDDLE_PLAN}
    step = pl.program_id(0)

    @pl.when(step == 0)
    def _():
        place.greet()

    for when, part, index in MIDDLE_PLAN:

        @pl.when(step == when)
        def _(part=part, index=index):
            stages[part][index]()

    def before_chunk(at):
        part = (at - AHEAD) * PARTS // (CHUNKS - AHEAD)
        if at >= AHEAD and part * (CHUNKS - AHEAD) == (at - AHEAD) * PARTS:
            for index in range(len(stages[part])):
                if (part, index) not in planned:
                    stages[part][index]()

    middle_kernel(
        *refs[:5],
        w_ref,
        w_hbm,
        *rest[:6],
        rest[6:19],
        seq=seq,
        before_chunk=before_chunk,
    )

    @pl.when(step == pl.num_programs(0) - 1)
    def _():
        for gather in gathers:
            gather.drain()


MIDDLE_PLAN = (
    (0, 0, 0), (5, 0, 1), (7, 0, 2), (9, 0, 3), (10, 0, 4), (11, 0, 5),
    (6, 1, 0), (9, 1, 1), (11, 1, 2), (13, 1, 3), (14, 1, 4), (15, 1, 5),
)


def middle_call(lengths, x, heads, cot, gain, w_second, pair=None, rows=512):
    total, width = x.shape
    columns = w_second.shape[1] + (0 if pair is None else pair.shape[1])
    chunk = (columns - width) // (2 * CHUNKS)
    fine = total // rows
    steps = 2 * fine + CHUNKS * (total // MIDDLE_BLOCK)
    early = pl.BlockSpec((rows, width), lambda i: (jnp.minimum(i, fine - 1), 0))
    late = pl.BlockSpec((rows, width), lambda i: (jnp.maximum(i - (steps - fine), 0), 0))
    ends = pl.BlockSpec(
        (rows, width),
        lambda i: (jnp.where(i < steps - fine, jnp.minimum(i, fine - 1), i - (steps - fine)), 0),
    )
    square = (width, 2 * chunk)
    scratch = [
        pltpu.VMEM((total, width), low_type),
        pltpu.VMEM((total, width), low_type),
        pltpu.VMEM((total, width), low_type),
        pltpu.VMEM((total, 128), f32),
        pltpu.VMEM((total, width), f32),
        pltpu.VMEM((total, width), f32),
        pltpu.VMEM((total, max(chunk, width)), low_type),
        pltpu.VMEM((total, max(chunk, width)), low_type),
        pltpu.VMEM((2,) + square, low_type),
        pltpu.VMEM((8, width), f32),
        DMA((2,)),
        pltpu.VMEM((width, columns - width), low_type),
        DMA,
    ]
    kernel, compiler, operands = middle_plain_kernel, params(), []
    if pair is not None:
        kernel, compiler, operands = middle_send_kernel, comm_params(5), [pair]
        scratch += PARTS * Gather.scratch(lax.axis_size("dp"))
    square_out = (width, width)
    first_block = pl.BlockSpec(
        square_out, lambda i: (0, 0), pipeline_mode=pl.Buffered(1)
    )
    return pl.pallas_call(
        functools.partial(kernel, seq=total // lengths.shape[0]),
        grid=(steps,),
        in_specs=[SMEM, early, ends, early, whole((1, width)), first_block, ANY]
        + [whole(operand.shape) for operand in operands],
        out_specs=[late, late, late, whole(square_out), ANY, whole((1, width))],
        out_shape=[struct((total, width))] * 3
        + [
            struct(square_out),
            struct((width, CHUNKS * 2 * chunk)),
            struct((1, width), f32),
        ],
        scratch_shapes=scratch,
        compiler_params=compiler,
        name="middle",
    )(lengths, x, heads, cot, gain, w_second, w_second, *operands)


def attend_back_kernel(
    len_ref,
    table_ref,
    q_ref,
    k_ref,
    v_ref,
    grad_ref,
    o_ref,
    lse_ref,
    dq_ref,
    dk_ref,
    dv_ref,
    table_sum,
    near_ref,
    near_sum,
    far_sum,
    acc,
    *,
    keys,
):
    pair, doc = pl.program_id(0), pl.program_id(1)
    seq = q_ref.shape[0]
    first = lax.broadcasted_iota(jnp.int32, (1, 128), 1) < 64
    zero = jnp.zeros((), low_type)

    def halves(x):
        return jnp.where(first, x, zero), jnp.where(first, zero, x)

    grad = grad_ref[...]
    q_one, g_one = halves(q_ref[...]), halves(grad)
    q_turned, g_turned = q_ref[...].T, grad.T
    product = grad.astype(f32) * o_ref[...].astype(f32)
    lse = lse_ref[...]
    other = pltpu.roll(lse, 64, 1)
    lse_of = (jnp.where(first, lse, other), jnp.where(first, other, lse))
    delta_of = tuple(
        jnp.broadcast_to(
            jnp.sum(jnp.where(first == (h == 0), product, 0.0), 1, keepdims=True), (seq, 128)
        )
        for h in range(2)
    )

    @pl.when(doc == 0)
    def _():
        fill_tiles(near_ref, table_ref, pair)
        near_sum[...] = jnp.zeros_like(near_sum)
        far_sum[...] = jnp.zeros_like(far_sum)

    for kb in range(seq // keys):
        held = slice(kb * keys, (kb + 1) * keys)
        k, v = k_ref[held, :], v_ref[held, :]
        live = (kb * keys + lax.broadcasted_iota(jnp.int32, (1, keys), 1)) < len_ref[doc]
        dq, dk, dv = [], [], []
        for h in range(2):
            scores = dot(q_one[h], k, NT)
            prob_grad = dot(g_one[h], v, NT)
            prob_rows, grad_rows = [], []
            for a in range(seq // SUB):
                down = slice(a * SUB, (a + 1) * SUB)
                probs, grads = [], []
                for b in range(keys // SUB):
                    across = slice(b * SUB, (b + 1) * SUB)
                    apart = kb * (keys // SUB) + b - a
                    shift = lse_of[h][down]
                    tile = scores[down, across]
                    if abs(apart) <= 1:
                        tile = tile + near_ref[h, apart + 1] - shift
                    else:
                        tile = tile - (shift - table_ref[2 * pair + h, 31 if apart > 0 else 15])
                    prob = jnp.where(live[:, across], jnp.exp2(tile), 0.0)
                    score_grad = prob * (prob_grad[down, across] - delta_of[h][down])
                    if abs(apart) <= 1:
                        near_sum[h, apart + 1] += score_grad
                    else:
                        far_sum[h, int(apart > 0)] += jnp.sum(
                            score_grad.reshape(SUB // 8, 8, SUB), 0
                        )
                    probs.append(prob.astype(low_type))
                    grads.append(score_grad.astype(low_type))
                prob_rows.append(jnp.concatenate(probs, 1))
                grad_rows.append(jnp.concatenate(grads, 1))
            prob_low = jnp.concatenate(prob_rows, 0)
            grad_low = jnp.concatenate(grad_rows, 0)
            side = slice(64 * h, 64 * (h + 1))
            dv.append(dot(g_turned[side], prob_low))
            dk.append(dot(q_turned[side], grad_low))
            dq.append(dot(grad_low, k))
        dv_ref[held, :] = jnp.concatenate(dv, 0).T.astype(low_type)
        dk_ref[held, :] = (jnp.concatenate(dk, 0) * (1 / LOG2E)).T.astype(low_type)
        part = jnp.where(first, dq[0], dq[1])
        acc[...] = part if kb == 0 else acc[...] + part
    dq_ref[...] = (acc[...] * 0.125).astype(low_type)

    @pl.when(doc == pl.num_programs(1) - 1)
    def _():
        lane = lax.broadcasted_iota(jnp.int32, (1, BAND), 1)
        for h in range(2):
            left = jnp.sum(far_sum[h, 0], keepdims=True)
            right = jnp.sum(far_sum[h, 1], keepdims=True)
            sums = band_sums(near_sum[h])
            table_sum[0, h : h + 1] = (
                sums + jnp.where(lane == 0, left, 0.0) + jnp.where(lane == 3 * SUB - 1, right, 0.0)
            )


def attend_back_call(lengths, table, q, k, v, grad, o, lse, keys=512):
    docs, (total, width) = lengths.shape[0], q.shape
    seq, pairs = total // docs, width // 128
    keys = min(keys, seq)
    slab = pl.BlockSpec((seq, 128), lambda p, d: (d, p))
    return pl.pallas_call(
        functools.partial(attend_back_kernel, keys=keys),
        grid=(pairs, docs),
        in_specs=[
            SMEM,
            SMEM,
            slab,
            slab,
            slab,
            slab,
            slab,
            slab,
        ],
        out_specs=[slab, slab, slab, pl.BlockSpec((1, 2, BAND), lambda p, d: (p, 0, 0))],
        out_shape=[struct((total, width))] * 3 + [struct((pairs, 2, BAND), f32)],
        scratch_shapes=back_scratch(seq),
        compiler_params=params(),
        name="attend_back",
    )(lengths, table, q, k, v, grad, o, lse)


def back_scratch(seq):
    return [
        pltpu.VMEM((2, 3, SUB, SUB), f32),
        pltpu.VMEM((2, 3, SUB, SUB), f32),
        pltpu.VMEM((2, 2, 8, SUB), f32),
        pltpu.VMEM((seq, 128), f32),
    ]


def last_kernel(
    x_ref,
    dq_ref,
    dk_ref,
    dv_ref,
    mid_ref,
    gain_ref,
    w_ref,
    gt_ref,
    gw_ref,
    gn_ref,
    acc,
    acc_gain,
):
    step = pl.program_id(0)
    rows, width = x_ref.shape

    @pl.when(step == 0)
    def _():
        acc[...] = jnp.zeros_like(acc)
        acc_gain[...] = jnp.zeros_like(acc_gain)

    gain = gain_ref[...]
    normed, inverse = norm_rows(x_ref[...].astype(f32))
    low = (normed * gain).astype(low_type)
    normed_grad = None
    for index, ref in enumerate((dq_ref, dk_ref, dv_ref)):
        part = slice(index * width, (index + 1) * width)
        grad = ref[...]
        acc[:, part] += dot(low, grad, TN)
        back = dot(grad, w_ref[:, part], NT)
        normed_grad = back if normed_grad is None else normed_grad + back
    acc_gain[...] += jnp.sum((normed_grad * normed).reshape(rows // 8, 8, width), 0)
    scaled = normed_grad * gain
    inner = jnp.mean(scaled * normed, -1, keepdims=True)
    gt_ref[...] = (mid_ref[...].astype(f32) + inverse * (scaled - normed * inner)).astype(low_type)

    @pl.when(step == pl.num_programs(0) - 1)
    def _():
        gw_ref[...] = acc[...].astype(low_type)
        gn_ref[...] = jnp.sum(acc_gain[...], 0, keepdims=True)


def last_call(x, dq, dk, dv, mid, gain, w_first, rows=512):
    total, width = x.shape
    row = pl.BlockSpec((rows, width), lambda i: (i, 0))
    grads = (width, 3 * width)
    return pl.pallas_call(
        last_kernel,
        grid=(total // rows,),
        in_specs=[row] * 5 + [whole((1, width)), whole(w_first.shape)],
        out_specs=[row, whole(grads), whole((1, width))],
        out_shape=[struct((total, width)), struct(grads), struct((1, width), f32)],
        scratch_shapes=[pltpu.VMEM(grads, f32), pltpu.VMEM((8, width), f32)],
        compiler_params=params(),
        name="last",
    )(x, dq, dk, dv, mid, gain, w_first)


MESH_ID = pl.DeviceIdType.MESH
ANY = pl.BlockSpec(memory_space=pl.ANY)
VMEM_WHOLE = pl.BlockSpec(memory_space=pltpu.VMEM)
DMA = pltpu.SemaphoreType.DMA
SPARE = 128


class Place:
    def __init__(self):
        self.dp, self.y = lax.axis_index("dp"), lax.axis_index("blk")
        self.depth = lax.axis_size("dp") // 4
        self.z = self.dp // 4
        self.x = lax.rem(self.dp // 2, 2)
        self.core = lax.rem(self.dp, 2)
        self.hops = sorted(range(1, self.depth), key=lambda hop: min(hop, self.depth - hop))

    def unit(self, z, x, core):
        return (z * 2 + x) * 2 + core

    def z_after(self, hop):
        return lax.rem(self.z + hop, self.depth)

    def z_before(self, hop):
        return lax.rem(self.z + self.depth - hop, self.depth)

    def along_z(self, hop):
        return (self.unit(self.z_after(hop), self.x, self.core), self.y)

    def over_x(self):
        return (self.unit(self.z, 1 - self.x, self.core), self.y)

    def over_core(self):
        return (self.unit(self.z, self.x, 1 - self.core), self.y)

    def over_y(self):
        return (self.dp, 1 - self.y)

    def greet(self):
        barrier = pltpu.get_barrier_semaphore()
        peers = [self.over_x(), self.over_core(), self.over_y()]
        peers += [self.along_z(hop) for hop in self.hops]
        for peer in peers:
            pl.semaphore_signal(barrier, device_id=peer, device_id_type=MESH_ID)
        pl.semaphore_wait(barrier, len(peers))


def remote(source, target, send, recv, device):
    return pltpu.make_async_remote_copy(
        src_ref=source,
        dst_ref=target,
        send_sem=send,
        recv_sem=recv,
        device_id=device,
        device_id_type=MESH_ID,
    )


class Meet:
    def __init__(self, place, shard, other, sem):
        self.place, self.shard, self.other, self.sem = place, shard, other, sem

    @staticmethod
    def scratch(own_rows, columns):
        block = (own_rows + -own_rows % 16, columns)
        return [pltpu.VMEM(block, low_type), pltpu.VMEM(block, low_type), DMA((2,))]

    def copy(self):
        return remote(self.shard, self.other, self.sem.at[0], self.sem.at[1], self.place.over_y())

    def start(self, parts):
        at = 0
        for ref in parts:
            rows, columns = ref.shape
            self.shard[:rows, at : at + columns] = ref[...]
            at += columns
        self.copy().start()

    def finish(self, pair):
        self.copy().wait()
        half = pair.shape[0] // 2
        mine = self.shard[:half].astype(f32)
        theirs = self.other[:half].astype(f32)
        first = self.place.y == 0
        pair[...] = jnp.concatenate(
            [jnp.where(first, mine, theirs), jnp.where(first, theirs, mine)], 0
        ).astype(low_type)


def hidden_parts(in_ref, down_ref, begin, end):
    chunk = in_ref.shape[1] // CHUNKS
    parts = []
    for at in range(begin, end):
        span = slice(at * chunk, (at + 1) * chunk)
        parts += [in_ref.at[:, span], down_ref.at[:, span]]
    return parts


class Gather:
    def __init__(self, place, pair, full, sems):
        self.place, self.pair, self.full = place, pair, full
        self.send_sem, self.recv_sem, self.put_sem = sems
        self.rows = pair.shape[0]
        self.mine = place.unit(place.z, place.x, place.core)
        self.has_left, self.has_right = place.z > 0, place.z < place.depth - 1

    @staticmethod
    def scratch(units):
        return [DMA((units, 4)), DMA((units,)), DMA]

    def at(self, u):
        return self.full.at[pl.ds(pl.multiple_of(u * self.rows, 16), self.rows)]

    def send(self, u, kind, source=None):
        place = self.place
        device = {
            "left": (place.dp - 4, place.y),
            "right": (place.dp + 4, place.y),
            "x": place.over_x(),
            "core": place.over_core(),
        }[kind]
        slot = ("left", "right", "x", "core").index(kind)
        source = self.at(u) if source is None else source
        return remote(source, self.at(u), self.send_sem.at[u, slot], self.recv_sem.at[u], device)

    def put(self):
        return pltpu.make_async_copy(self.pair, self.at(self.mine), self.put_sem)

    def spread(self):
        for kind, there in (("right", self.has_right), ("left", self.has_left)):

            @pl.when(there)
            def _(kind=kind):
                self.send(self.mine, kind, self.pair).start()

        self.send(self.mine, "x", self.pair).start()
        self.send(self.mine, "core", self.pair).start()
        self.put().start()

    def from_z(self, hop):
        place = self.place
        for kind, z, onward in (
            ("right", place.z - hop, self.has_right),
            ("left", place.z + hop, self.has_left),
        ):

            @pl.when((z >= 0) & (z < place.depth))
            def _(kind=kind, z=z, onward=onward):
                u = place.unit(z, place.x, place.core)
                self.send(u, "core").wait_recv()

                @pl.when(onward)
                def _():
                    self.send(u, kind).start()

                self.send(u, "x").start()
                self.send(u, "core").start()

    def from_x(self, hop):
        place = self.place
        for z in (place.z - hop, place.z + hop)[: 1 + min(hop, 1)]:

            @pl.when((z >= 0) & (z < place.depth))
            def _(z=z):
                u = place.unit(z, 1 - place.x, place.core)
                self.send(u, "core").wait_recv()
                self.send(u, "core").start()

    def from_core(self):
        place = self.place
        for z in range(place.depth):
            for x in range(2):
                self.send(place.unit(z, x, 1 - place.core), "core").wait_recv()
        self.put().wait()

    def stages(self):
        def at_hop(hop):
            if hop < self.place.depth:
                self.from_z(hop)
            self.from_x(hop - 1)

        out = [self.spread]
        out += [lambda hop=hop: at_hop(hop) for hop in range(1, self.place.depth + 1)]
        return out + [self.from_core]

    def drain(self):
        place = self.place
        for z in range(place.depth):
            u = place.unit(z, place.x, place.core)
            self.send(u, "x").wait_send()
            self.send(u, "core").wait_send()

            @pl.when((place.z >= z) & self.has_right)
            def _(u=u):
                self.send(u, "right").wait_send()

            @pl.when((place.z <= z) & self.has_left)
            def _(u=u):
                self.send(u, "left").wait_send()

            self.send(place.unit(z, 1 - place.x, place.core), "core").wait_send()


PARTS = 2


def gather_parts(place, pair, full, sems):
    size = full.shape[1] // PARTS
    out = []
    for at in range(PARTS):
        span = slice(at * size, (at + 1) * size)
        out.append(Gather(place, pair.at[:, span], full.at[:, span], sems[3 * at : 3 * at + 3]))
    return out


class Scatter:
    def __init__(self, place, full, scratch, source=None):
        self.place, self.full = place, full
        self.source = full if source is None else source
        self.core_buf, self.x_send, self.x_buf, self.z_send, self.z_buf = scratch[:5]
        self.y_send, self.y_buf = scratch[5:7]
        self.core_sem, self.x_sem, self.z_sem, self.y_sem = scratch[7:]
        self.rows = self.x_send.shape[1]
        self.order = place.hops + [0]

    @staticmethod
    def scratch(own_rows, columns, units, lead=()):
        depth, unit = units // 4, (2 * own_rows, columns)
        edge = lead + (own_rows + -own_rows % 16, columns)
        return [
            pltpu.VMEM(lead + (2, depth) + unit, low_type),
            pltpu.VMEM(lead + (depth,) + unit, low_type),
            pltpu.VMEM(lead + (depth,) + unit, low_type),
            pltpu.VMEM(lead + (depth,) + unit, low_type),
            pltpu.VMEM(lead + (depth,) + unit, low_type),
            pltpu.VMEM(edge, low_type),
            pltpu.VMEM(edge, low_type),
            DMA(lead + (2, 2, depth)),
            DMA(lead + (2, depth)),
            DMA(lead + (2, depth)),
            DMA(lead + (2,)),
        ]

    def at(self, ref, z, x, core):
        u = self.place.unit(z, x, core)
        return ref.at[pl.ds(pl.multiple_of(u * self.rows, 16), self.rows)]

    def x_of(self, side):
        return self.place.x if side == 0 else 1 - self.place.x

    def to_core(self, side, hop):
        place = self.place
        return remote(
            self.at(self.source, place.z_after(hop), self.x_of(side), 1 - place.core),
            self.core_buf.at[side, hop],
            self.core_sem.at[0, side, hop],
            self.core_sem.at[1, side, hop],
            place.over_core(),
        )

    def to_x(self, hop):
        return remote(
            self.x_send.at[hop],
            self.x_buf.at[hop],
            self.x_sem.at[0, hop],
            self.x_sem.at[1, hop],
            self.place.over_x(),
        )

    def to_z(self, hop):
        return remote(
            self.z_send.at[hop],
            self.z_buf.at[hop],
            self.z_sem.at[0, hop],
            self.z_sem.at[1, hop],
            self.place.along_z(hop),
        )

    def to_y(self):
        return remote(
            self.y_send, self.y_buf, self.y_sem.at[0], self.y_sem.at[1], self.place.over_y()
        )

    def start(self):
        for side in (1, 0):
            for hop in self.order:
                self.to_core(side, hop).start()

    def mine(self, side, hop):
        place = self.place
        self.to_core(side, hop).wait_recv()
        own = self.at(self.full, place.z_after(hop), self.x_of(side), place.core)
        return own[...].astype(f32) + self.core_buf[side, hop].astype(f32)

    def stage_x(self, hop):
        self.x_send[hop] = self.mine(1, hop).astype(low_type)
        self.to_x(hop).start()

    def stage_z(self, hop):
        part = self.mine(0, hop)
        self.to_x(hop).wait_recv()
        part = part + self.x_buf[hop].astype(f32)
        self.z_send[hop] = part.astype(low_type)
        if hop:
            self.to_z(hop).start()

    def stage_y(self):
        total = self.z_send[0].astype(f32)
        for hop in self.place.hops:
            self.to_z(hop).wait_recv()
            total = total + self.z_buf[hop].astype(f32)
        half = self.rows // 2
        first = self.place.y == 0
        self.y_send[:half] = jnp.where(first, total[half:], total[:half]).astype(low_type)
        self.to_y().start()
        return jnp.where(first, total[:half], total[half:])

    def finish(self, kept):
        self.to_y().wait()
        return kept + self.y_buf[: kept.shape[0]].astype(f32)

    def drain(self):
        for hop in self.order:
            for side in (1, 0):
                self.to_core(side, hop).wait_send()
            self.to_x(hop).wait_send()
            if hop:
                self.to_z(hop).wait_send()


class Exchange:
    def __init__(self, place, send, recv, sem):
        self.send, self.recv, self.sem = send, recv, sem
        self.targets = [place.over_core(), place.over_x(), place.over_y()]
        span = 1
        while span < place.depth:
            flip = place.z + span - 2 * span * lax.rem(place.z // span, 2)
            self.targets.append((place.unit(flip, place.x, place.core), place.y))
            span *= 2

    @staticmethod
    def rounds(units):
        return 3 + (units // 4 - 1).bit_length()

    @staticmethod
    def scratch(shape, units):
        rounds = Exchange.rounds(units)
        return [
            pltpu.VMEM((rounds,) + shape, f32),
            pltpu.VMEM((rounds,) + shape, f32),
            DMA((2, rounds)),
        ]

    def copy(self, at):
        return remote(
            self.send.at[at], self.recv.at[at], self.sem.at[0, at], self.sem.at[1, at], self.targets[at]
        )

    def start(self, at, value):
        self.send[at] = value
        self.copy(at).start()

    def finish(self, at):
        self.copy(at).wait()
        return self.send[at] + self.recv[at]


def comm_params(collective):
    return pltpu.CompilerParams(
        collective_id=collective, has_side_effects=True, vmem_limit_bytes=VMEM
    )


def first_kernel(
    wq_ref,
    wk_ref,
    wv_ref,
    gains_ref,
    second_refs,
    tokens_ref,
    q_ref,
    k_ref,
    v_ref,
    x_ref,
    w_ref,
    gain_ref,
    second_pair,
    w_all,
    x_in,
    low_here,
    stage,
    pair,
    *rest,
):
    swap_sem, load_sem, save_sem, stage_sem, w_sem = rest[21:]
    place = Place()
    per, seq, width = x_ref.shape
    rows = tokens_ref.shape[1]
    spans = (slice(2 * width, w_all.shape[1]), slice(width, 2 * width), slice(0, width))
    meets = [Meet(place, *rest[3 * at : 3 * at + 3]) for at in range(3)]
    second_meet = Meet(place, *rest[9:12])
    gathers = [
        Gather(place, pair.at[:, span], w_all.at[:, span], rest[12 + 3 * at : 15 + 3 * at])
        for at, span in enumerate(spans)
    ]
    place.greet()

    def swap(doc):
        return remote(
            tokens_ref.at[(1 - place.y) * per + doc],
            x_in.at[per + doc],
            swap_sem.at[0, doc],
            swap_sem.at[1, doc],
            place.over_y(),
        )

    def load(doc):
        return pltpu.make_async_copy(
            tokens_ref.at[place.y * per + doc], x_in.at[doc], load_sem.at[doc]
        )

    def start_of(block):
        y = jnp.where(block < per, place.y, 1 - place.y)
        return pl.multiple_of(y * rows, 16)

    def save(block):
        return pltpu.make_async_copy(
            x_in.at[block],
            x_ref.at[lax.rem(block, per), pl.ds(start_of(block), rows)],
            save_sem.at[block],
        )

    def store(block, index):
        target = (q_ref, k_ref, v_ref)[index]
        begin = pl.multiple_of(lax.rem(block, per) * seq + start_of(block), 16)
        slot = lax.rem(block, 2)
        return pltpu.make_async_copy(
            stage.at[slot, index], target.at[pl.ds(begin, rows)], stage_sem.at[slot, index]
        )

    for meet, parts in zip(meets, ((wv_ref, gains_ref), (wk_ref,), (wq_ref,))):
        meet.start(parts)
    for doc in range(per):
        load(doc).start()
        swap(doc).start()
    stages = [gather.stages() for gather in gathers]
    for at in range(3):
        meets[at].finish(pair.at[:, spans[at]])
        stages[at][0]()
    out_ref, in_ref, down_ref = second_refs
    second_meet.start([out_ref] + hidden_parts(in_ref, down_ref, 0, AHEAD))
    for index in range(1, place.depth):
        for at in range(3):
            stages[at][index]()

    def put_stage(block, index, part):
        if index == 0:
            part = part * (0.125 * LOG2E)
        stage[lax.rem(block, 2), index] = part.astype(low_type)
        store(block, index).start()

    def own_rows(at, index):
        for later in range(place.depth, len(stages[at])):
            stages[at][later]()
        if at == 0:
            gain_ref[...] = w_all[:, 3 * width :].astype(f32).T[: gain_ref.shape[0]]

        def project(block, _):
            if at == 0:
                load(block).wait()
                save(block).start()
                normed, _ = norm_rows(x_in[block].astype(f32))
                low_here[block] = (normed * gain_ref[0:1]).astype(low_type)

            @pl.when(block >= 2)
            def _():
                store(block - 2, index).wait()

            columns = w_all[:, index * width : (index + 1) * width]
            put_stage(block, index, dot(low_here[block], columns))
            return 0

        lax.fori_loop(0, per, project, 0)

    for at, index in ((0, 2), (1, 1), (2, 0)):
        own_rows(at, index)
    keep = pltpu.make_async_copy(w_all, w_ref, w_sem)
    keep.start()

    def project(block, _):
        swap(block - per).wait_recv()
        save(block).start()
        normed, _ = norm_rows(x_in[block].astype(f32))
        low = (normed * gain_ref[0:1]).astype(low_type)
        for index in (2, 1, 0):

            @pl.when(block >= 2)
            def _(index=index):
                store(block - 2, index).wait()

            put_stage(block, index, dot(low, w_all[:, index * width : (index + 1) * width]))
        return 0

    lax.fori_loop(per, 2 * per, project, 0)
    second_meet.finish(second_pair)
    for block in range(2 * per):
        save(block).wait()
        if block >= 2 * per - 2:
            for index in range(3):
                store(block, index).wait()
    keep.wait()
    for gather in gathers:
        gather.drain()
    for doc in range(per):
        swap(doc).wait_send()


def first_call(firsts, gains, seconds, tokens, ways):
    units = lax.axis_size("dp")
    count, rows, width = tokens.shape
    own_rows = gains.shape[0]
    columns = sum(w.shape[1] for w in firsts) + gains.shape[1]
    second_columns = width + AHEAD * 2 * (seconds[1].shape[1] // CHUNKS)
    per = count // ways
    total = per * rows * ways

    def kernel(*refs):
        begin = len(firsts) + 1
        end = begin + len(seconds)
        first_kernel(*refs[:begin], refs[begin:end], *refs[end:])

    return pl.pallas_call(
        kernel,
        in_specs=[VMEM_WHOLE] * (len(firsts) + 1 + len(seconds)) + [ANY],
        out_specs=[ANY] * 5 + [VMEM_WHOLE] * 2,
        out_shape=[struct((total, width))] * 3
        + [
            struct((per, rows * ways, width)),
            struct((units * ways * own_rows, columns)),
            struct((8, width), f32),
            struct((ways * own_rows, second_columns)),
        ],
        scratch_shapes=[
            pltpu.VMEM((units * ways * own_rows, columns), low_type),
            pltpu.VMEM((2 * per, rows, width), low_type),
            pltpu.VMEM((per, rows, width), low_type),
            pltpu.VMEM((2, 3, rows, width), low_type),
            pltpu.VMEM((ways * own_rows, columns), low_type),
        ]
        + Meet.scratch(own_rows, columns - 2 * width)
        + 2 * Meet.scratch(own_rows, width)
        + Meet.scratch(own_rows, second_columns)
        + 3 * Gather.scratch(units)
        + [DMA((2, per)), DMA((per,)), DMA((2 * per,)), DMA((2, 3)), DMA],
        compiler_params=comm_params(1),
        name="first",
    )(*firsts, gains, *seconds, tokens)


def attend_send_kernel(
    len_ref,
    table_ref,
    q_ref,
    k_ref,
    v_ref,
    pair_ref,
    in_ref,
    down_ref,
    cot_ref,
    o_ref,
    lse_ref,
    w_ref,
    late_pair,
    cot_doc,
    near_ref,
    cot_in,
    *rest,
    rows,
):
    place = Place()
    gathers = gather_parts(place, pair_ref, w_ref, rest[:-5])
    meet = Meet(place, *rest[-5:-2])
    swap_sem, load_sem = rest[-2:]
    per, part = cot_doc.shape[0], cot_ref.shape[1]
    step = pl.program_id(0) * pl.num_programs(1) + pl.program_id(1)
    last = pl.num_programs(0) * pl.num_programs(1) - 1
    stages = [gather.stages() for gather in gathers]

    def swap(doc):
        return remote(
            cot_ref.at[(1 - place.y) * per + doc],
            cot_doc.at[doc, pl.ds(pl.multiple_of(place.y * part, 16), part)],
            swap_sem.at[0, doc],
            swap_sem.at[1, doc],
            place.over_y(),
        )

    def load(doc):
        return pltpu.make_async_copy(
            cot_ref.at[place.y * per + doc], cot_in.at[doc], load_sem.at[0, doc]
        )

    def save(doc):
        return pltpu.make_async_copy(
            cot_in.at[doc],
            cot_doc.at[doc, pl.ds(pl.multiple_of(place.y * part, 16), part)],
            load_sem.at[1, doc],
        )

    @pl.when(step == 0)
    def _():
        place.greet()
        for doc in range(per):
            load(doc).start()

    for at, piece, index in SEND_PLAN:

        @pl.when(step == at)
        def _(piece=piece, index=index):
            stages[piece][index]()

    @pl.when(step == 1)
    def _():
        for doc in range(per):
            swap(doc).start()
            load(doc).wait()
            save(doc).start()
        meet.start(hidden_parts(in_ref, down_ref, AHEAD, CHUNKS))

    attend_kernel(len_ref, table_ref, q_ref, k_ref, v_ref, o_ref, lse_ref, near_ref, rows=rows)

    @pl.when(step == last)
    def _():
        done = {(piece, index) for _, piece, index in SEND_PLAN}
        for index in range(len(stages[0])):
            for piece in range(PARTS):
                if (piece, index) not in done:
                    stages[piece][index]()
        meet.finish(late_pair)
        for gather in gathers:
            gather.drain()
        for doc in range(per):
            save(doc).wait()
            swap(doc).wait()


SEND_PLAN = (
    (0, 0, 0), (1, 1, 0), (3, 0, 1), (5, 1, 1), (6, 0, 2), (7, 1, 2),
    (8, 0, 3), (10, 1, 3), (10, 0, 4), (11, 0, 5),
)


def attend_send_call(lengths, table, q, k, v, pair, w_in, w_down, cot, rows=512):
    units = lax.axis_size("dp")
    docs, (total, width) = lengths.shape[0], q.shape
    seq, pairs = total // docs, width // 128
    late = (CHUNKS - AHEAD) * 2 * (w_in.shape[1] // CHUNKS)
    slab = pl.BlockSpec((seq, 128), lambda p, d: (d, p))
    return pl.pallas_call(
        functools.partial(attend_send_kernel, rows=rows),
        grid=(pairs, docs),
        in_specs=[SMEM, SMEM, slab, slab, slab]
        + [whole(operand.shape) for operand in (pair, w_in, w_down)]
        + [ANY],
        out_specs=[
            slab,
            slab,
            ANY,
            whole((pair.shape[0], late)),
            ANY,
        ],
        out_shape=[
            struct((total, width)),
            struct((total, width), f32),
            struct((units * pair.shape[0], pair.shape[1])),
            struct((pair.shape[0], late)),
            struct((docs, seq, width)),
        ],
        scratch_shapes=[
            pltpu.VMEM((2, 3, SUB, SUB), f32),
            pltpu.VMEM((docs, cot.shape[1], width), low_type),
        ]
        + PARTS * Gather.scratch(units)
        + Meet.scratch(w_in.shape[0], late)
        + [DMA((2, docs)), DMA((2, docs))],
        compiler_params=comm_params(3),
        name="attend",
    )(lengths, table, q, k, v, pair, w_in, w_down, cot)


def back_send_kernel(
    len_ref,
    table_ref,
    q_ref,
    k_ref,
    v_ref,
    grad_ref,
    o_ref,
    lse_ref,
    g_ref,
    mixed_ref,
    dq_ref,
    dk_ref,
    dv_ref,
    table_sum,
    gw_ref,
    mixed_out,
    near_ref,
    near_sum,
    far_sum,
    acc,
    grads,
    mixed_in,
    kept,
    *rest,
    keys,
    steps,
):
    place = Place()
    size = grads.shape[1] // CHUNKS
    grads_sem, swap_sem, load_sem = rest[11:]

    def scatter(at):
        span = pl.ds(pl.multiple_of(at * size, 128), size)
        return Scatter(
            place, grads.at[:, span], [ref.at[at] for ref in rest[:11]], g_ref.at[:, span]
        )

    per, part = mixed_ref.shape[0], mixed_out.shape[1]
    step = pl.program_id(0) * pl.num_programs(1) + pl.program_id(1)
    last = pl.num_programs(0) * pl.num_programs(1) - 1

    def swap(doc):
        return remote(
            mixed_ref.at[doc, pl.ds(pl.multiple_of((1 - place.y) * part, 16), part)],
            mixed_out.at[place.y * per + doc],
            swap_sem.at[0, doc],
            swap_sem.at[1, doc],
            place.over_y(),
        )

    def load(doc):
        return pltpu.make_async_copy(
            mixed_ref.at[doc, pl.ds(pl.multiple_of(place.y * part, 16), part)],
            mixed_in.at[doc],
            load_sem.at[0, doc],
        )

    def save(doc):
        return pltpu.make_async_copy(
            mixed_in.at[doc], mixed_out.at[place.y * per + doc], load_sem.at[1, doc]
        )

    take = pltpu.make_async_copy(g_ref, grads, grads_sem)

    @pl.when(step == 0)
    def _():
        place.greet()
        for at in range(CHUNKS):
            scatter(at).start()
        take.start()
        for doc in range(per):
            load(doc).start()
            swap(doc).start()

    @pl.when(step == 1)
    def _():
        take.wait()

    def every_other(first, work):
        at = (step - first) // 2

        @pl.when((step >= first) & (at < CHUNKS) & (step == first + 2 * at))
        def _():
            work(at)

    def x_stages(at):
        for hop in place.hops + [0]:
            scatter(at).stage_x(hop)

    def z_stages(at):
        for hop in place.hops + [0]:
            scatter(at).stage_z(hop)

    def y_stage(at):
        kept[at] = scatter(at).stage_y()

    def finish(at):
        gw_ref[:, pl.ds(pl.multiple_of(at * size, 128), size)] = scatter(at).finish(kept[at])

    every_other(1, x_stages)
    every_other(3, z_stages)
    every_other(5, y_stage)
    every_other(6, finish)

    @pl.when(step == 3)
    def _():
        for doc in range(per):
            load(doc).wait()
            save(doc).start()

    attend_back_kernel(
        len_ref,
        table_ref,
        q_ref,
        k_ref,
        v_ref,
        grad_ref,
        o_ref,
        lse_ref,
        dq_ref,
        dk_ref,
        dv_ref,
        table_sum,
        near_ref,
        near_sum,
        far_sum,
        acc,
        keys=keys,
    )

    @pl.when(step == last)
    def _():
        for at in range(CHUNKS):
            for first, work in ((1, x_stages), (3, z_stages), (5, y_stage), (6, finish)):
                if first + 2 * at >= steps:
                    work(at)
        for at in range(CHUNKS):
            scatter(at).drain()
        for doc in range(per):
            save(doc).wait()
            swap(doc).wait()


def back_send_call(lengths, table, q, k, v, grad, o, lse, g, mixed, keys=512):
    units = lax.axis_size("dp")
    docs, (total, width) = lengths.shape[0], q.shape
    seq, pairs = total // docs, width // 128
    columns = g.shape[1]
    own = g.shape[0] // (2 * units)
    slab = pl.BlockSpec((seq, 128), lambda p, d: (d, p))
    return pl.pallas_call(
        functools.partial(
            back_send_kernel, keys=keys, steps=pairs * docs
        ),
        grid=(pairs, docs),
        in_specs=[
            SMEM,
            SMEM,
            slab,
            slab,
            slab,
            slab,
            slab,
            slab,
            ANY,
            ANY,
        ],
        out_specs=[
            slab,
            slab,
            slab,
            pl.BlockSpec((1, 2, BAND), lambda p, d: (p, 0, 0)),
            whole((own, columns)),
            ANY,
        ],
        out_shape=[struct((total, width))] * 3
        + [
            struct((pairs, 2, BAND), f32),
            struct((own, columns), f32),
            struct((2 * docs, seq // 2, width)),
        ],
        scratch_shapes=back_scratch(seq)
        + [
            pltpu.VMEM(g.shape, low_type),
            pltpu.VMEM((docs, seq // 2, width), low_type),
            pltpu.VMEM((CHUNKS, own, columns // CHUNKS), f32),
        ]
        + Scatter.scratch(own, columns // CHUNKS, units, (CHUNKS,))
        + [DMA, DMA((2, docs)), DMA((2, docs))],
        compiler_params=comm_params(4),
        name="attend_back",
    )(lengths, table, q, k, v, grad, o, lse, g, mixed.reshape(docs, seq, width))


def end_kernel(
    x_ref,
    dq_ref,
    dk_ref,
    dv_ref,
    mid_ref,
    w_ref,
    gain_ref,
    table_ref,
    wq_ref,
    wk_ref,
    wv_ref,
    w_in_ref,
    g_hidden_ref,
    g_out,
    gw_ref,
    gt_ref,
    small_ref,
    gains_ref,
    rows_in,
    low_all,
    grads,
    gt,
    *rest,
):
    place = Place()
    count, rows, width = gt_ref.shape
    per = count // 2
    seq = 2 * rows
    scatter_refs, kept = rest[:11], rest[11]
    small_send, small_recv, small_sem, load_sem, gt_sem = rest[12:]
    exchange = Exchange(place, small_send, small_recv, small_sem)
    sources = (x_ref, dq_ref, dk_ref, dv_ref, mid_ref)

    def scatter(at):
        return Scatter(place, grads.at[at], [ref.at[at] for ref in scatter_refs])

    def load(block, index):
        y = jnp.where(block < per, 1 - place.y, place.y)
        begin = pl.multiple_of(lax.rem(block, per) * seq + y * rows, 16)
        return pltpu.make_async_copy(
            sources[index].at[pl.ds(begin, rows)],
            rows_in.at[index, block],
            load_sem.at[block, index],
        )

    def give_away(block):
        return remote(
            gt.at[block],
            gt_ref.at[place.y * per + block],
            gt_sem.at[0, block],
            gt_sem.at[1, block],
            place.over_y(),
        )

    def give_home(block):
        return pltpu.make_async_copy(
            gt.at[block], gt_ref.at[place.y * per + block - per], gt_sem.at[0, block]
        )

    take = pltpu.make_async_copy(g_out, grads.at[0], load_sem.at[2 * per, 0])
    for index in range(5):
        load(0, index).start()
    take.start()
    for index in range(5):
        for block in range(1, 2 * per):
            load(block, index).start()
    place.greet()
    gain = gain_ref[0:1]
    take.wait()
    scatter(0).start()
    heads = table_ref.shape[0]
    small_send[0] = jnp.zeros(small_ref.shape, f32)
    small_send[0, :heads] = bucket_sums(table_ref[...], 32)
    exchange.copy(0).start()
    chunk = g_hidden_ref.shape[1] // (2 * CHUNKS)
    sum_second = jnp.zeros((gains_ref.shape[0], chunk), f32)
    for at in range(CHUNKS):
        sum_second += (
            g_hidden_ref[:, 2 * at * chunk : (2 * at + 1) * chunk]
            * w_in_ref[:, at * chunk : (at + 1) * chunk].astype(f32)
        )
    rounds = len(exchange.targets)

    def exchange_round(at):
        value = exchange.finish(at)
        if at < rounds - 1:
            exchange.start(at + 1, value)
        else:
            small_ref[...] = value

    def low_rows(block, _):
        @pl.when(block > 0)
        def _():
            load(block, 0).wait()

        normed, _ = norm_rows(rows_in[0, block].astype(f32))
        low_all[block] = (normed * gain).astype(low_type)
        return 0

    def rows_back(block):
        normed, inverse = norm_rows(rows_in[0, block].astype(f32))
        normed_grad = None
        for index in range(3):
            part = dot(
                rows_in[1 + index, block], w_ref[:, index * width : (index + 1) * width], NT
            )
            normed_grad = part if normed_grad is None else normed_grad + part
        scaled = normed_grad * gain
        inner = jnp.mean(scaled * normed, -1, keepdims=True)
        mid = rows_in[4, block].astype(f32)
        gt[block] = (mid + inverse * (scaled - normed * inner)).astype(low_type)

        @pl.when(block < per)
        def _():
            give_away(block).start()

        @pl.when(block >= per)
        def _():
            give_home(block).start()

    def weights_back(at):
        grads[at] = dot(
            low_all[...].reshape(2 * per * rows, width),
            rows_in[at].reshape(2 * per * rows, width),
            TN,
        ).astype(low_type)
        scatter(at).start()

    def during(at, first, last, work):
        @pl.when((at >= first) & (at <= last))
        def _():
            work(at)

    def x_stages(at):
        for hop in place.hops + [0]:
            scatter(at).stage_x(hop)

    def z_stages(at):
        for hop in place.hops + [0]:
            scatter(at).stage_z(hop)

    def y_stage(at):
        kept[at] = scatter(at).stage_y()

    def finish(at):
        gw_ref[at] = scatter(at).finish(kept[at])

    def project_step(at, _):
        weights_back(at)
        x_stages(at - 1)
        for index in range(2):
            during(at, index + 2, index + 2, lambda _, index=index: exchange_round(index))
        return 0

    def rows_step(block, _):
        rows_back(block)
        during(block, 1, 1, lambda _: z_stages(0))
        during(block, 1, 2, z_stages)
        during(block, 2, 2, lambda _: z_stages(3))
        during(block, 3, 3, lambda _: y_stage(0))
        during(block, 3, 3, lambda _: y_stage(1))
        during(block, 3, 3, lambda _: y_stage(2))
        for index in range(2, rounds):
            during(block, index - 1, index - 1, lambda _, index=index: exchange_round(index))
        return 0

    for index in range(5):
        load(0, index).wait()
    rows_back(0)
    lax.fori_loop(0, 2 * per, low_rows, 0)
    for index in range(1, 5):
        for block in range(1, 2 * per):
            load(block, index).wait()
    lax.fori_loop(1, 4, project_step, 0)
    x_stages(3)
    lax.fori_loop(1, 2 * per, rows_step, 0)
    y_stage(3)
    finish(0)
    finish(1)
    finish(2)
    finish(3)
    sum_first = jnp.zeros((gains_ref.shape[0], width), f32)
    for at, ref in enumerate((wq_ref, wk_ref, wv_ref)):
        sum_first += gw_ref[1 + at] * ref[...].astype(f32)
    lane = lax.broadcasted_iota(jnp.int32, (1, 128), 1)
    gains_ref[...] = jnp.where(
        lane == 0,
        jnp.sum(sum_first, 1, keepdims=True),
        jnp.sum(sum_second, 1, keepdims=True),
    )

    def drain(at, _):
        scatter(at).drain()
        return 0

    lax.fori_loop(0, 4, drain, 0)
    for block in range(per):
        give_away(block).wait()
        give_home(per + block).wait()


def end_call(x, dq, dk, dv, mid, w_first, gains, table, own_weights, g_hidden, g_out, docs, ways):
    units = lax.axis_size("dp")
    total, width = x.shape
    own = width // (units * ways)
    rows = total // (docs * ways)
    small = (table.shape[0] + -table.shape[0] % 8, 128)
    return pl.pallas_call(
        end_kernel,
        in_specs=[ANY] * 5 + [VMEM_WHOLE] * 8 + [ANY],
        out_specs=[VMEM_WHOLE, ANY, VMEM_WHOLE, VMEM_WHOLE],
        out_shape=[
            struct((4, own, width), f32),
            struct((docs * ways, rows, width)),
            struct(small, f32),
            struct((own, 128), f32),
        ],
        scratch_shapes=[
            pltpu.VMEM((5, docs * ways, rows, width), low_type),
            pltpu.VMEM((docs * ways, rows, width), low_type),
            pltpu.VMEM((4, width, width), low_type),
            pltpu.VMEM((docs * ways, rows, width), low_type),
        ]
        + Scatter.scratch(own, width, units, (4,))
        + [pltpu.VMEM((4, own, width), f32)]
        + Exchange.scratch(small, units)
        + [DMA((docs * ways + 1, 5)), DMA((2, docs * ways))],
        compiler_params=comm_params(2),
        name="end",
    )(x, dq, dk, dv, mid, w_first, gains, table, *own_weights, g_hidden, g_out)


def sharing(count):
    ways = lax.axis_size("blk")
    return max(1, count // ways), max(1, ways // count)


def to_documents(x):
    count, rows, width = x.shape
    ways, me = lax.axis_size("blk"), lax.axis_index("blk")
    per, share = sharing(count)
    if share > 1:
        everything = lax.all_gather(x, "blk", axis=1, tiled=True)
        return lax.dynamic_index_in_dim(everything, me // share, 0, keepdims=False)
    out = jnp.zeros((per, ways * rows, width), x.dtype)
    for hop in range(ways):
        piece = lax.dynamic_slice_in_dim(x, lax.rem(me + hop, ways) * per, per, 0)
        if hop:
            piece = lax.ppermute(piece, "blk", [(i, (i + hop) % ways) for i in range(ways)])
        source = lax.rem(me - hop + ways, ways)
        out = lax.dynamic_update_slice_in_dim(out, piece, source * rows, 1)
    return out.reshape(per * ways * rows, width)


def from_documents(y, count):
    ways, me = lax.axis_size("blk"), lax.axis_index("blk")
    per, share = sharing(count)
    width = y.shape[1]
    if share > 1:
        everything = lax.all_gather(y, "blk", axis=0, tiled=True).reshape(count, -1, width)
        rows = everything.shape[1] // ways
        return lax.dynamic_slice_in_dim(everything, me * rows, rows, 1)
    y = y.reshape(per, -1, width)
    rows = y.shape[1] // ways
    out = jnp.zeros((count, rows, width), y.dtype)
    for hop in range(ways):
        piece = lax.dynamic_slice_in_dim(y, lax.rem(me + hop, ways) * rows, rows, 1)
        if hop:
            piece = lax.ppermute(piece, "blk", [(i, (i + hop) % ways) for i in range(ways)])
        source = lax.rem(me - hop + ways, ways)
        out = lax.dynamic_update_slice_in_dim(out, piece, source * per, 0)
    return out


def among(y, share, split, concat):
    if share == 1:
        return y
    ways = lax.axis_size("blk")
    groups = [list(range(at, at + share)) for at in range(0, ways, share)]
    return lax.all_to_all(
        y, "blk", split, concat, axis_index_groups=groups, tiled=True
    )


def my_share(y, share, axis):
    if share == 1:
        return y
    size = y.shape[axis] // share
    at = lax.rem(lax.axis_index("blk"), share) * size
    return lax.dynamic_slice_in_dim(y, at, size, axis)


def body(
    tokens,
    lengths,
    norm1_gain,
    w_query,
    w_key,
    w_value,
    w_out,
    rel_table,
    norm2_gain,
    w_in,
    w_down,
    cotangent,
):
    micro, docs, rows, width = tokens.shape
    count = micro * docs
    per, share = sharing(count)
    both = ("dp", "blk")
    direct = lax.axis_size("blk") == 2 and per * 2 == count and lax.axis_size("dp") % 4 == 0
    gains = jnp.pad(jnp.stack([norm1_gain, norm2_gain], 1), ((0, 0), (0, SPARE - 2)))
    firsts, seconds = (w_query, w_key, w_value), (w_out, w_in, w_down)
    tokens_here = tokens.reshape(count, rows, width)
    cot_here = cotangent.reshape(count, rows, width)
    if direct:
        q, k, v, x, w_first, gain_rows, pair = first_call(
            firsts, gains, seconds, tokens_here, 2
        )
        x = x.reshape(-1, width)
    else:
        pair = None
        w_second = lax.all_gather(second_pieces(*seconds), both, axis=0, tiled=True)
        w_first = lax.all_gather(
            jnp.concatenate(firsts + (gains,), 1), both, axis=0, tiled=True
        )
        x = to_documents(tokens_here)
        gain_rows = w_first[:, 3 * width : 3 * width + 2].astype(f32).T
    gain_first, gain_second = gain_rows[:1], gain_rows[1:2]
    own = lax.dynamic_slice_in_dim(
        lengths.reshape(count), lax.axis_index("blk") // share * per, per, 0
    )
    x_rows = my_share(x, share, 0)
    own_rows, w_heads = own, w_first
    if share > 1:
        own_rows = own - lax.rem(lax.axis_index("blk"), share) * x_rows.shape[0]
        w_heads = jnp.concatenate(
            [my_share(w_first[:, i * width : (i + 1) * width], share, 1) for i in range(3)], 1
        )
    table = my_share((rel_table * LOG2E).T, share, 0)

    if direct:
        heads, lse, w_second, pair, cot = attend_send_call(
            own, table, q, k, v, pair, w_in, w_down, cot_here
        )
        cot = cot.reshape(-1, width)
    else:
        q, k, v = qkv_call(x, gain_first, w_heads, width // share)
        heads, lse = attend_call(own, table, q, k, v)
        cot = my_share(to_documents(cot_here), share, 0)
    mixed, heads_grad, mid, g_out, g_hidden, gn_second = middle_call(
        own_rows, x_rows, among(heads, share, 0, 1), cot, gain_second, w_second, pair
    )
    if direct:
        dq, dk, dv, table_sum, g_hidden, mixed = back_send_call(
            own, table, q, k, v, heads_grad, heads, lse, g_hidden, mixed
        )
    else:
        dq, dk, dv, table_sum = attend_back_call(
            own, table, q, k, v, among(heads_grad, share, 1, 0), heads, lse
        )
        mixed = from_documents(mixed, count)
        g_out = lax.psum_scatter(g_out, both, scatter_dimension=0, tiled=True).astype(f32)
        g_hidden = lax.psum_scatter(g_hidden, both, scatter_dimension=0, tiled=True).astype(f32)
    dq, dk, dv = (among(grad, share, 0, 1) for grad in (dq, dk, dv))
    head_count, bucket_count = rel_table.shape[1], rel_table.shape[0]
    if direct:
        g_first, grad_tokens, small, gains = end_call(
            x,
            dq,
            dk,
            dv,
            mid,
            w_first,
            gain_rows,
            table_sum.reshape(-1, BAND),
            firsts + (w_in,),
            g_hidden,
            g_out,
            per,
            2,
        )
        grad_table = small[:head_count, :bucket_count].T
        gains = (gains[:, 0] / norm1_gain.astype(f32), gains[:, 1] / norm2_gain.astype(f32))
    else:
        grad_tokens, g_first, gn_first = last_call(
            x_rows, dq, dk, dv, mid, gain_first, w_first
        )
        grad_tokens = from_documents(grad_tokens, count)
        g_first = lax.psum_scatter(g_first, both, scatter_dimension=0, tiled=True).astype(f32)
        gains = lax.psum_scatter(
            jnp.concatenate([gn_first, gn_second], 0), both, scatter_dimension=1, tiled=True
        )
        table_sum = bucket_sums(table_sum.reshape(-1, BAND), bucket_count)[:, :bucket_count]
        if share > 1:
            at = lax.rem(lax.axis_index("blk"), share) * table_sum.shape[0]
            table_sum = lax.dynamic_update_slice_in_dim(
                jnp.zeros(rel_table.T.shape, f32), table_sum, at, 0
            )
        grad_table = lax.psum(table_sum, both).T
    if direct:
        g_out, grad_query, grad_key, grad_value = g_first
    else:
        grad_query, grad_key, grad_value = (
            g_first[:, i * width : (i + 1) * width] for i in range(3)
        )
    grad_in, grad_down = split_hidden(g_hidden)
    return (
        mixed.reshape(tokens.shape),
        grad_tokens.reshape(tokens.shape),
        gains[0],
        grad_query,
        grad_key,
        grad_value,
        g_out,
        grad_table,
        gains[1],
        grad_in,
        grad_down,
    )


def solution(mesh):
    rows = P(None, "dp", "blk", None)
    weight = P(("dp", "blk"), None)
    gain = P(("dp", "blk"))
    return jax.shard_map(
        body,
        mesh=mesh,
        in_specs=(
            rows,
            P(None, "dp"),
            gain,
            weight,
            weight,
            weight,
            weight,
            P(),
            gain,
            weight,
            weight,
            rows,
        ),
        out_specs=(rows, rows, gain, weight, weight, weight, weight, P(), gain, weight, weight),
        check_vma=False,
    )
```
